256 devices in a mesh: slab: 128 (over x, z, y), lvl: 2 (over core).
Axes of the slice: x: 4, y: 4, z: 8, core: 2. Of those that a mesh axis runs over, the one named last changes fastest.
Arguments:
- adjoint_final: float32 [2, 256, 19, 16, 256], P('lvl', 'slab'), may hold values from -6 to 6
- populations: bfloat16 [4, 2, 256, 19, 16, 256], P(None, 'lvl', 'slab'), as said below
- relaxation: float32 [2, 256, 16, 256], P('lvl', 'slab'), may hold values from 0.8 to 1.9
- blend: float32 [2, 256, 16, 256], P('lvl', 'slab'), may hold values from 0.1 to 0.9
- solid: int32 [2, 256, 16, 256], P('lvl', 'slab'), may hold values from 0 to 1, as said below
- chain: int32 [2, 256, 2], P('lvl', 'slab'), may hold values from -1 to 255, as said below
- parent: int32 [256, 2], P('slab'), may hold values from -1 to 255, as said below
- children: int32 [256, 8], P('slab'), may hold values from -1 to 255, as said below
Outputs:
- adjoint_initial: float32 [2, 256, 19, 16, 256], P('lvl', 'slab')
The draws below stay inside these ranges and needn't reach their ends.
Inputs may be any that keep to these rules, and one draw needn't show every extreme that they name: `solid`: fluid cells fill the layers x = 0 and x = 15 of every block. chain[l, g, 1] is g + 1 or -1 and chain[l, g, 0] is g - 1 or -1; chain[l, g, 1] = g + 1 exactly when chain[l, g + 1, 0] = g; chain[l, 0, 0] = chain[l, 255, 1] = -1. parent[f, 0] is -1 (then parent[f, 1] = -1) or a coarse block p with |p // 2 - f // 2| <= 1, and parent[f, 1] its octant 0 to 7; no pair (p, octant) is named twice. For any a and b, at most one fine block f with f // 2 = a has a parent p with p // 2 = b, and for every a some b reaches 1. children[p, o] = f exactly when parent[f] = (p, o); -1 where no fine block names (p, o). Every entry is positive, and the sum over the 19 populations of a cell is positive.
All inputs are finite; a program needn't handle non-finite values.
Results may differ from the reference program's by a relative error of at most 0.0003.
Values sent between devices are 32-bit elements; how exact they have to be, the bound alone decides.
No kernel may reach another device: no remote copies, remote signals or barrier semaphores. Data moves between devices by JAX's collectives and lax.ppermute only.
A program may use at most 64 MiB of HBM per device.

```python
import jax
import jax.numpy as jnp
import numpy as np
from jax import lax

EDGE = 16
POPS = 19
STEPS = 4
BLK_DEV = 2
BLOCKS = 256


velocity_table = np.array([(0, 0, 0), (1, 0, 0), (-1, 0, 0), (0, 1, 0), (0, -1, 0), (0, 0, 1), (0, 0, -1), (1, 1, 0), (-1, -1, 0), (1, -1, 0), (-1, 1, 0), (1, 0, 1), (-1, 0, -1), (1, 0, -1), (-1, 0, 1), (0, 1, 1), (0, -1, -1), (0, 1, -1), (0, -1, 1)], np.float32)


lattice_weight_table = np.array([1.0 / 3.0] + [1.0 / 18.0] * 6 + [1.0 / 36.0] * 12, np.float32)


def draw_populations(key, part):
    key = jax.random.fold_in(key, 11)
    first_key, second_key = jax.random.split(key)
    shape = (STEPS, 2, BLOCKS, POPS, EDGE, EDGE * EDGE)
    flow_shape = (STEPS, 2, BLOCKS, 3, EDGE, EDGE * EDGE)
    factors = jax.random.uniform(first_key, shape, jnp.float32, 0.6, 1.4)
    drift_flow = jax.random.uniform(second_key, flow_shape, jnp.float32, -0.12, 0.12)
    along_x = jnp.asarray(velocity_table[:, 0])[:, None, None] * drift_flow[:, :, :, 0:1]
    along_y = jnp.asarray(velocity_table[:, 1])[:, None, None] * drift_flow[:, :, :, 1:2]
    along_z = jnp.asarray(velocity_table[:, 2])[:, None, None] * drift_flow[:, :, :, 2:3]
    shaped = factors * (1.0 + 3.0 * (along_x + along_y + along_z))
    return (shaped * jnp.asarray(lattice_weight_table)[:, None, None]).astype(jnp.bfloat16)


def draw_solid(key, part):
    key = jax.random.fold_in(key, 12)
    shape = (2, BLOCKS, EDGE, EDGE * EDGE)
    solid_pick = jax.random.randint(key, shape, 0, 6)
    layer_index = lax.broadcasted_iota(jnp.int32, shape, 2)
    inside = (layer_index >= 1) & (layer_index <= EDGE - 2)
    return jnp.where(inside & (solid_pick == 0), 1, 0).astype(jnp.int32)


def draw_chain(key, part):
    key = jax.random.fold_in(key, 13)
    cut_marks = jax.random.randint(key, (2, BLOCKS + 1), 0, 4) == 0
    boundary_index = jnp.arange(BLOCKS + 1, dtype=jnp.int32)
    cut_marks = cut_marks | (boundary_index == 0)[None] | (boundary_index == BLOCKS)[None]
    block_index = jnp.arange(BLOCKS, dtype=jnp.int32)
    before_link = jnp.where(cut_marks[:, :BLOCKS], -1, block_index[None] - 1)
    after_link = jnp.where(cut_marks[:, 1:], -1, block_index[None] + 1)
    return jnp.stack([before_link, after_link], axis=-1).astype(jnp.int32)


def interface_tables(key):
    half_count = BLK_DEV // 2
    slab_count = BLOCKS // BLK_DEV
    keys_list = jax.random.split(key, 5)
    devices = jnp.arange(slab_count, dtype=jnp.int32)
    first_offset = jax.random.randint(keys_list[0], (slab_count,), -1, 2)
    step_on = jax.random.randint(keys_list[1], (slab_count,), 1, 3)
    second_offset = (first_offset + 1 + step_on) % 3 - 1
    end_pick = jax.random.randint(keys_list[2], (slab_count,), 0, 2)
    first_offset = jnp.where(devices == 0, end_pick, jnp.where(devices == slab_count - 1, -end_pick, first_offset))
    second_offset = jnp.where(devices == 0, 1 - end_pick, jnp.where(devices == slab_count - 1, end_pick - 1, second_offset))
    fine_ids = jnp.arange(BLOCKS, dtype=jnp.int32)
    owner_slab = fine_ids // BLK_DEV
    slot_index = fine_ids % BLK_DEV
    upper_half = slot_index >= half_count
    applied_offset = jnp.where(upper_half, second_offset[owner_slab], first_offset[owner_slab])
    target_slab = owner_slab + applied_offset
    present = jnp.logical_or(jnp.logical_not(upper_half), jax.random.randint(keys_list[3], (BLOCKS,), 0, 2) == 1)
    order_index = (1 - applied_offset) * half_count + slot_index % half_count
    scores = jax.random.randint(keys_list[4], (slab_count, 8 * BLK_DEV), 0, 8 * BLK_DEV) * (8 * BLK_DEV) + jnp.arange(8 * BLK_DEV, dtype=jnp.int32)[None]
    orders = jnp.argsort(scores, axis=1, stable=True).astype(jnp.int32)
    picked = orders[target_slab, order_index]
    coarse_id = target_slab * BLK_DEV + picked // 8
    octant = picked % 8
    parent_table = jnp.stack([jnp.where(present, coarse_id, -1), jnp.where(present, octant, -1)], axis=1)
    flat_target = jnp.where(present, coarse_id * 8 + octant, BLOCKS * 8)
    children_table = jnp.full((BLOCKS * 8,), -1, jnp.int32).at[flat_target].set(fine_ids, mode='drop')
    return (parent_table.astype(jnp.int32), children_table.reshape(BLOCKS, 8).astype(jnp.int32))


def draw_parent(key, part):
    tables = interface_tables(key)
    return tables[0]


def draw_children(key, part):
    tables = interface_tables(key)
    return tables[1]


def block_scale(stream_key, shape, shards, low, largest):
    gain, own = 1.0, jax.random.fold_in(stream_key, 6)
    for dim, shards_of in shards:
        steps = jnp.exp(jax.random.uniform(jax.random.fold_in(own, dim), (shards_of,), jnp.float32, low / len(shards), largest / len(shards)))
        gain = gain * jnp.repeat(steps, shape[dim] // shards_of).reshape([-1 if axis == dim else 1 for axis in range(len(shape))])
    return gain


def gaussian(own_key, extent, scale, most, shards=(), kind=jnp.bfloat16):
    drawn = jax.random.normal(own_key, extent, jnp.float32) * scale
    if len(shards) > 0:
        drawn = block_scale(own_key, extent, shards, -0.22, 0.18) * drawn
    return jnp.clip(drawn, min=-most, max=most).astype(kind)


def setup_inputs(seed: int = 0) -> dict:
    key_list = jax.random.split(jax.random.key(seed), 9)
    return {
        "adjoint_final": gaussian(key_list[0], (2, BLOCKS, POPS, EDGE, EDGE * EDGE), 1.0, 6.0, ((0, 2), (1, 128)), jnp.float32),
        "populations": draw_populations(jax.random.fold_in(key_list[8], 71), 0),
        "relaxation": jnp.clip(0.8 + 1.09999996 * jax.random.uniform(key_list[2], (2, BLOCKS, EDGE, EDGE * EDGE), jnp.float32) ** block_scale(key_list[2], (2, BLOCKS, EDGE, EDGE * EDGE), ((0, 2), (1, 128)), -0.2, 0.2), 0.8, 1.9),
        "blend": jnp.clip(0.1 + 0.79999997 * jax.random.uniform(key_list[3], (2, BLOCKS, EDGE, EDGE * EDGE), jnp.float32) ** block_scale(key_list[3], (2, BLOCKS, EDGE, EDGE * EDGE), ((0, 2), (1, 128)), -0.2, 0.2), 0.1, 0.9),
        "solid": draw_solid(jax.random.fold_in(key_list[8], 71), 0),
        "chain": draw_chain(jax.random.fold_in(key_list[8], 71), 0),
        "parent": draw_parent(jax.random.fold_in(key_list[8], 71), 0),
        "children": draw_children(jax.random.fold_in(key_list[8], 71), 0),
    }


velocities = [(0, 0, 0), (1, 0, 0), (-1, 0, 0), (0, 1, 0), (0, -1, 0), (0, 0, 1), (0, 0, -1),
              (1, 1, 0), (-1, -1, 0), (1, -1, 0), (-1, 1, 0), (1, 0, 1), (-1, 0, -1), (1, 0, -1),
              (-1, 0, 1), (0, 1, 1), (0, -1, -1), (0, 1, -1), (0, -1, 1)]
lattice_weights = [1.0 / 3.0] + [1.0 / 18.0] * 6 + [1.0 / 36.0] * 12
east_pops = [1, 7, 9, 11, 13]
west_pops = [2, 8, 10, 12, 14]


def reverse_index(i):
    c = velocities[i]
    return velocities.index((-c[0], -c[1], -c[2]))


def pull_field(moving, c, next_layer, prev_layer, edge_cells):
    if c[0] == 1:
        moving = jnp.concatenate([moving[:, 1:], next_layer[:, None]], axis=1)
    elif c[0] == -1:
        moving = jnp.concatenate([prev_layer[:, None], moving[:, :-1]], axis=1)
    if c[1] != 0:
        moving = jnp.roll(moving, -c[1] * edge_cells, axis=-1)
    if c[2] != 0:
        z_position = lax.broadcasted_iota(jnp.int32, moving.shape, moving.ndim - 1) % edge_cells
        if c[2] == 1:
            moving = jnp.where(z_position == edge_cells - 1, jnp.roll(moving, edge_cells - 1, axis=-1),
                               jnp.roll(moving, -1, axis=-1))
        else:
            moving = jnp.where(z_position == 0, jnp.roll(moving, 1 - edge_cells, axis=-1),
                               jnp.roll(moving, 1, axis=-1))
    return moving


def stream_back(adjoint, solid_float, next_first, prev_last, edge_cells):
    zeros_layer = jnp.zeros_like(solid_float[:, 0])
    pulled_list = []
    for i in range(19):
        c = velocities[i]
        next_layer = next_first[:, east_pops.index(i)] if c[0] == 1 else None
        prev_layer = prev_last[:, west_pops.index(i)] if c[0] == -1 else None
        shifted = pull_field(adjoint[:, i], c, next_layer, prev_layer, edge_cells)
        blocked = pull_field(solid_float, c, zeros_layer, zeros_layer, edge_cells)
        pulled_list.append(jnp.where(blocked > 0.5, adjoint[:, reverse_index(i)], shifted))
    return jnp.stack(pulled_list, axis=1)


def collide_back(pulled, forward, omega_cells, solid_mask):
    density = jnp.sum(forward, axis=1)
    flows = []
    for axis_pos in range(3):
        running = jnp.zeros_like(density)
        for i in range(19):
            if velocities[i][axis_pos] != 0:
                running = running + velocities[i][axis_pos] * forward[:, i]
        flows.append(running / density)
    speed_sq = flows[0] * flows[0] + flows[1] * flows[1] + flows[2] * flows[2]
    grad_density = jnp.zeros_like(density)
    grad_flows = [jnp.zeros_like(density) for axis_pos in range(3)]
    for i in range(19):
        c = velocities[i]
        along_flow = c[0] * flows[0] + c[1] * flows[1] + c[2] * flows[2]
        weighted = lattice_weights[i] * pulled[:, i]
        grad_density = grad_density + weighted * (1.0 - 4.5 * along_flow * along_flow + 1.5 * speed_sq)
        for axis_pos in range(3):
            grad_flows[axis_pos] = grad_flows[axis_pos] + weighted * (
                3.0 * c[axis_pos] + 9.0 * along_flow * c[axis_pos] - 3.0 * flows[axis_pos])
    updated = []
    for j in range(19):
        c = velocities[j]
        projected = grad_density + c[0] * grad_flows[0] + c[1] * grad_flows[1] + c[2] * grad_flows[2]
        mixed = (1.0 - omega_cells) * pulled[:, j] + omega_cells * projected
        updated.append(jnp.where(solid_mask, 0.0, mixed))
    return jnp.stack(updated, axis=1)


def couple_back(adjoint_current_value, blend, parent, children):
    half_edge = EDGE // 2
    coarse_level = adjoint_current_value[0].reshape(BLOCKS, POPS, EDGE, EDGE, EDGE)
    fine_level = adjoint_current_value[1].reshape(BLOCKS, POPS, EDGE, EDGE, EDGE)
    coarse_weight = blend[0].reshape(BLOCKS, 1, EDGE, EDGE, EDGE)
    fine_weight = blend[1].reshape(BLOCKS, 1, EDGE, EDGE, EDGE)
    has_parent = parent[:, 0] >= 0
    parent_block = jnp.clip(parent[:, 0], 0, BLOCKS - 1)
    parent_octant = jnp.clip(parent[:, 1], 0, 7)
    octants = (coarse_weight * coarse_level).reshape(
        BLOCKS, POPS, 2, half_edge, 2, half_edge, 2, half_edge).transpose(0, 2, 4, 6, 1, 3, 5, 7).reshape(
        BLOCKS * 8, POPS, half_edge, half_edge, half_edge)
    taken_octants = octants[parent_block * 8 + parent_octant]
    spread = jnp.repeat(jnp.repeat(jnp.repeat(taken_octants, 2, axis=2), 2, axis=3), 2, axis=4) / 8.0
    mask_fine = has_parent.astype(jnp.float32).reshape(BLOCKS, 1, 1, 1, 1)
    new_fine = fine_level - mask_fine * fine_weight * fine_level + mask_fine * spread
    pooled = (fine_weight * fine_level).reshape(
        BLOCKS, POPS, half_edge, 2, half_edge, 2, half_edge, 2).sum(axis=(3, 5, 7))
    target = jnp.where(has_parent, parent_block * 8 + parent_octant, BLOCKS * 8)
    placed = jnp.zeros((BLOCKS * 8, POPS, half_edge, half_edge, half_edge), jnp.float32).at[target].add(
        pooled, mode="drop")
    placed = placed.reshape(BLOCKS, 2, 2, 2, POPS, half_edge, half_edge, half_edge).transpose(
        0, 4, 1, 5, 2, 6, 3, 7).reshape(BLOCKS, POPS, EDGE, EDGE, EDGE)
    covered = (children >= 0).astype(jnp.float32).reshape(BLOCKS, 2, 1, 2, 1, 2, 1)
    covered_cells = jnp.broadcast_to(covered, (BLOCKS, 2, half_edge, 2, half_edge, 2, half_edge)).reshape(
        BLOCKS, 1, EDGE, EDGE, EDGE)
    new_coarse = coarse_level - covered_cells * coarse_weight * coarse_level + placed
    return jnp.stack([new_coarse, new_fine]).reshape(2, BLOCKS, POPS, EDGE, EDGE * EDGE)


def reference(adjoint_final, populations, relaxation, blend, solid, chain, parent, children):
    merged = 2 * BLOCKS
    solid_mask = solid.reshape(merged, EDGE, EDGE * EDGE) > 0
    solid_float = solid_mask.astype(jnp.float32)
    omega_cells = relaxation.reshape(merged, EDGE, EDGE * EDGE)
    chain_links = chain.reshape(merged, 2)
    level_base = (jnp.arange(merged, dtype=jnp.int32) // BLOCKS) * BLOCKS
    next_index = jnp.clip(chain_links[:, 1], 0, BLOCKS - 1) + level_base
    prev_index = jnp.clip(chain_links[:, 0], 0, BLOCKS - 1) + level_base
    has_next = (chain_links[:, 1] >= 0).reshape(merged, 1, 1)
    has_prev = (chain_links[:, 0] >= 0).reshape(merged, 1, 1)
    adjoint_current_value = adjoint_final
    for step_index in range(STEPS - 1, -1, -1):
        coupled = couple_back(adjoint_current_value, blend, parent, children).reshape(merged, POPS, EDGE, EDGE * EDGE)
        first_layers = coupled[:, east_pops, 0, :]
        last_layers = coupled[:, west_pops, EDGE - 1, :]
        next_first = jnp.where(has_next, first_layers[next_index], 0.0)
        prev_last = jnp.where(has_prev, last_layers[prev_index], 0.0)
        pulled = stream_back(coupled, solid_float, next_first, prev_last, EDGE)
        forward = populations[step_index].reshape(merged, POPS, EDGE, EDGE * EDGE).astype(jnp.float32)
        adjoint_current_value = collide_back(pulled, forward, omega_cells, solid_mask).reshape(
            2, BLOCKS, POPS, EDGE, EDGE * EDGE)
    return adjoint_current_value
```

```python
import functools

import jax
import jax.numpy as jnp
from jax import lax
from jax.experimental import pallas as pl
from jax.experimental.pallas import tpu as pltpu
from jax.sharding import PartitionSpec as P

velocities = [
    (0, 0, 0),
    (1, 0, 0),
    (-1, 0, 0),
    (0, 1, 0),
    (0, -1, 0),
    (0, 0, 1),
    (0, 0, -1),
    (1, 1, 0),
    (-1, -1, 0),
    (1, -1, 0),
    (-1, 1, 0),
    (1, 0, 1),
    (-1, 0, -1),
    (1, 0, -1),
    (-1, 0, 1),
    (0, 1, 1),
    (0, -1, -1),
    (0, 1, -1),
    (0, -1, 1),
]
east_pops = [1, 7, 9, 11, 13]
west_pops = [2, 8, 10, 12, 14]
opposite = [velocities.index((-c[0], -c[1], -c[2])) for c in velocities]
axes = ("slab", "lvl")
pops, edge, plane = 19, 16, 256
f32, bf16 = jnp.float32, jnp.bfloat16

item_row = (0, 56, 112)
own_d, mate_d, own_f, far_f, mate_f, far_d = 40, 48, 96, 104, 152, 160
message_rows = 168
at_level, at_odd, at_prev, at_inner, at_next = 12, 13, 14, 15, 16


def level_swap(value, slabs):
    pairs = [(2 * s + v, 2 * s + 1 - v) for s in range(slabs) for v in (0, 1)]
    return lax.ppermute(value, axes, pairs)


def mate_swap(value, slabs):
    pairs = [(2 * s + v, 2 * (s ^ 1) + v) for s in range(slabs) for v in (0, 1)]
    return lax.ppermute(value, axes, pairs)


def far_swap(value, slabs):
    pairs = []
    for s in range(slabs):
        other = s - 1 if s % 2 == 0 else s + 1
        for v in (0, 1):
            if 0 <= other < slabs:
                pairs.append((2 * s + v, 2 * other + v))
            else:
                pairs.append((2 * s + v, 2 * s + 1 - v))
    return lax.ppermute(value, axes, pairs)


def cell_key(index, level, octant):
    y, z = index >> 4, index & 15
    fine = (y >> 1) * 8 + (z >> 1)
    inside = ((y >> 3) == ((octant >> 1) & 1)) & ((z >> 3) == (octant & 1))
    coarse = jnp.where(inside, (y & 7) * 8 + (z & 7), -1)
    return jnp.where(level == 1, fine, coarse)


def select(values, matrix):
    high = values.astype(bf16)
    low = (values - high.astype(f32)).astype(bf16)
    return jnp.dot(high, matrix, preferred_element_type=f32) + jnp.dot(
        low, matrix, preferred_element_type=f32
    )


def ones_where(mask):
    return jnp.where(mask, 1.0, 0.0).astype(bf16)


def iota(shape, dim):
    return lax.broadcasted_iota(jnp.int32, shape, dim)


def pack(d_ref, alpha_ref, w_ref, k_ref, out_ref, loc_ref, item_scr, rim_scr, half_scr):
    level = d_ref[at_level]
    odd = d_ref[at_odd]
    out_ref[...] = jnp.zeros_like(out_ref)
    item_scr[152:160, :] = jnp.zeros((8, plane), f32)
    rim_scr[...] = jnp.zeros_like(rim_scr)
    for i in range(5):
        e, w = east_pops[i], west_pops[i]
        low = alpha_ref[0, e, 0:1, :] * k_ref[0, 0:1, :]
        high = alpha_ref[1, w, edge - 1 : edge, :] * k_ref[1, edge - 1 : edge, :]
        loc_ref[i : i + 1, :] = jnp.where(odd == 1, low, high)
        loc_ref[8 + i : 9 + i, :] = jnp.where(odd == 1, high, low)
    loc_ref[5:8, :] = jnp.zeros((3, plane), f32)
    loc_ref[13:16, :] = jnp.zeros((3, plane), f32)
    for j in range(3):
        base = item_row[j]

        @pl.when(d_ref[j] == 1)
        def _(j=j, base=base):
            g, octant, other = d_ref[3 + j], d_ref[6 + j], d_ref[9 + j]
            ox = octant >> 2

            @pl.when(level == 0)
            def _():
                rows = pl.ds(pl.multiple_of(ox * 8, 8), 8)
                part = alpha_ref[g, :, rows, :] * w_ref[g, rows, :][None]
                item_scr[0:152, :] = part.reshape(152, plane)

            @pl.when(level == 1)
            def _():
                part = (alpha_ref[g] * w_ref[g][None]).reshape(304, plane)
                for n in range(2):
                    lanes = slice(128 * n, 128 * n + 128)
                    half_scr[n, 0:304, :] = part[:, lanes]
                    item_scr[0:152, lanes] = (
                        half_scr[n, pl.ds(0, 152, stride=2), :]
                        + half_scr[n, pl.ds(1, 152, stride=2), :]
                    )

            cells = cell_key(iota((plane, 128), 0), level, octant)
            picked = select(item_scr[...], ones_where(cells == (iota((plane, 128), 1) & 63)))
            left = iota((40, 128), 1) < 64
            out_ref[base : base + 40, 0:128] = jnp.where(left, picked[0:40], picked[40:80])
            out_ref[base : base + 40, 128:256] = jnp.where(left, picked[80:120], picked[120:160])

            @pl.when((level == 0) | (ox == other))
            def _():
                for i in range(5):
                    e, w = east_pops[i] * 8, west_pops[i] * 8 + 7
                    rim_scr[i : i + 1, :] = jnp.where(
                        other == 1, item_scr[w : w + 1, :], item_scr[e : e + 1, :]
                    )
                source = cell_key(iota((plane, plane), 0), level, octant)
                target = cell_key(iota((plane, plane), 1), 1 - level, octant)
                spread = select(rim_scr[...], ones_where(source == target))
                spread = spread * jnp.where(level == 0, 0.125, 1.0)
                towards_d = other != odd
                if j == 0:
                    row = jnp.where(towards_d, mate_d, mate_f)
                elif j == 1:
                    row = jnp.where(towards_d, far_d, far_f)
                else:
                    row = jnp.where(towards_d, own_d, own_f)
                out_ref[pl.ds(pl.multiple_of(row, 8), 8), :] = spread


def first_pack_kernel(d_ref, alpha_ref, w_ref, out_ref, loc_ref, k_ref, item_scr, rim_scr, half_scr):
    level = d_ref[at_level]
    x = iota((edge, plane), 0)
    cell = iota((edge, plane), 1)
    for g in range(2):
        covered = jnp.zeros((edge, plane), jnp.bool_)
        for j in range(3):
            octant = d_ref[6 + j]
            inside = (
                ((x >> 3) == (octant >> 2))
                & ((cell >> 7) == ((octant >> 1) & 1))
                & (((cell >> 3) & 1) == (octant & 1))
            ) | (level == 1)
            covered = covered | (inside & (d_ref[j] == 1) & (d_ref[3 + j] == g))
        k_ref[g] = jnp.where(covered, 1.0 - w_ref[g], 1.0)
    pack(d_ref, alpha_ref, w_ref, k_ref, out_ref, loc_ref, item_scr, rim_scr, half_scr)


def moved_cells(values, c, z):
    if c[1] == 0 and c[2] == 0:
        return values
    base = -16 * c[1]
    axis = values.ndim - 1
    if c[2] == 0:
        return pltpu.roll(values, base % plane, axis)
    inner = pltpu.roll(values, (base - c[2]) % plane, axis)
    around = pltpu.roll(values, (base + 15 * c[2]) % plane, axis)
    return jnp.where(z == (15 if c[2] == 1 else 0), around, inner)


def fields_kernel(pop_ref, relax_ref, solid_ref, u_ref, keep_ref, gain_ref, bits_ref, pad_scr):
    z = iota((edge, plane), 1) & 15
    for g in range(2):
        solid = solid_ref[g] > 0
        omega = relax_ref[g]
        keep_ref[g] = jnp.where(solid, 0.0, 1.0 - omega)
        gain_ref[g] = jnp.where(solid, 0.0, omega)
        pad_scr[0:8, :] = jnp.zeros((8, plane), f32)
        pad_scr[24:32, :] = jnp.zeros((8, plane), f32)
        pad_scr[8:24, :] = jnp.where(solid, 1.0, 0.0)
        bits = jnp.zeros((edge, plane), jnp.int32)
        for i in range(pops):
            c = velocities[i]
            blocked = moved_cells(pad_scr[8 + c[0] : 24 + c[0], :], c, z) > 0.5
            bits = bits | jnp.where(blocked, 1 << i, 0)
        bits_ref[g] = bits
    steps = pop_ref.shape[0]
    for t in range(steps):
        for g in range(2):
            total = jnp.zeros((edge, plane), f32)
            flow = [jnp.zeros((edge, plane), f32) for _ in range(3)]
            for i in range(pops):
                f = pop_ref[t, g, i].astype(f32)
                total = total + f
                for a in range(3):
                    if velocities[i][a] == 1:
                        flow[a] = flow[a] + f
                    elif velocities[i][a] == -1:
                        flow[a] = flow[a] - f
            for a in range(3):
                u_ref[t, g, a] = flow[a] / total


def collide(pulled, u, keep, gain):
    g = pulled
    plus = {i: g[i] + g[i + 1] for i in range(1, pops, 2)}
    minus = {i: g[i] - g[i + 1] for i in range(1, pops, 2)}
    xy, xz, yz = plus[7] + plus[9], plus[11] + plus[13], plus[15] + plus[17]
    px, py, pz = 2.0 * plus[1], 2.0 * plus[3], 2.0 * plus[5]
    weight = 12.0 * g[0] + (px + py + pz) + (xy + xz + yz)
    qxx, qyy, qzz = px + xy + xz, py + xy + yz, pz + xz + yz
    qxy, qxz, qyz = plus[7] - plus[9], plus[11] - plus[13], plus[15] - plus[17]
    jx = 2.0 * minus[1] + (minus[7] + minus[9]) + (minus[11] + minus[13])
    jy = 2.0 * minus[3] + (minus[7] - minus[9]) + (minus[15] + minus[17])
    jz = 2.0 * minus[5] + (minus[11] - minus[13]) + (minus[15] - minus[17])
    ux, uy, uz = u
    qux = qxx * ux + qxy * uy + qxz * uz
    quy = qxy * ux + qyy * uy + qyz * uz
    quz = qxz * ux + qyz * uy + qzz * uz
    speed = ux * ux + uy * uy + uz * uz
    along = ux * qux + uy * quy + uz * quz
    scale = gain * (1.0 / 36.0)
    rest = scale * (weight * (1.0 + 1.5 * speed) - 4.5 * along)
    scale = gain * (1.0 / 12.0)
    mx = scale * (jx + 3.0 * qux - ux * weight)
    my = scale * (jy + 3.0 * quy - uy * weight)
    mz = scale * (jz + 3.0 * quz - uz * weight)
    out = [None] * pops
    out[0] = keep * g[0] + rest
    pairs = [mx, my, mz, mx + my, mx - my, mx + mz, mx - mz, my + mz, my - mz]
    for n, i in enumerate(range(1, pops, 2)):
        out[i] = keep * g[i] + (rest + pairs[n])
        out[i + 1] = keep * g[i + 1] + (rest - pairs[n])
    return out


def step_kernel(*refs, last):
    (d_ref, alpha_ref, w_ref, k_ref, u_ref, keep_ref, gain_ref, bits_ref) = refs[:8]
    (lvl_ref, mate_ref, far_ref, late_ref) = refs[8:12]
    if last:
        out_ref, beta_scr, half_scr = refs[12:]
    else:
        out_ref, msg_ref, loc_ref, beta_scr, item_scr, rim_scr, half_scr = refs[12:]
    level = d_ref[at_level]
    odd = d_ref[at_odd]
    for g in range(2):
        beta_scr[g, :, 8:24, :] = alpha_ref[g] * k_ref[g][None]
    sources = (mate_ref, far_ref, lvl_ref)
    for j in range(3):
        first = 112 if j == 2 else 0

        @pl.when(d_ref[j] == 1)
        def _(j=j, first=first):
            g, octant = d_ref[3 + j], d_ref[6 + j]
            left = iota((40, 128), 1) < 64
            a = sources[j][first : first + 40, 0:128]
            b = sources[j][first : first + 40, 128:256]
            stacked = jnp.concatenate(
                [
                    jnp.where(left, a, 0.0),
                    jnp.where(left, 0.0, a),
                    jnp.where(left, b, 0.0),
                    jnp.where(left, 0.0, b),
                ],
                axis=0,
            )
            target = cell_key(iota((128, plane), 1), level, octant)
            spread = select(stacked, ones_where((iota((128, plane), 0) & 63) == target))

            @pl.when(level == 0)
            def _():
                rows = pl.ds(pl.multiple_of(8 + (octant >> 2) * 8, 8), 8)
                beta_scr[g, :, rows, :] += spread[0:152].reshape(pops, 8, plane)

            @pl.when(level == 1)
            def _():
                for n in range(2):
                    lanes = slice(128 * n, 128 * n + 128)
                    half = spread[:, lanes] * 0.125
                    half_scr[n, pl.ds(0, 160, stride=2), :] = half
                    half_scr[n, pl.ds(1, 160, stride=2), :] = half
                    both = half_scr[n, 0:304, :].reshape(pops, edge, 128)
                    beta_scr[g, :, 8:24, lanes] += both

    from_d = mate_ref[40:48, :] + lvl_ref[mate_f : mate_f + 8, :] + late_ref[...]
    from_f = far_ref[40:48, :] + lvl_ref[far_d : far_d + 8, :]
    above = jnp.where(odd == 1, from_f, from_d)
    below = jnp.where(odd == 1, from_d, from_f)
    above = jnp.where(d_ref[at_next] == 1, above, 0.0)
    below = jnp.where(d_ref[at_prev] == 1, below, 0.0)
    inner = d_ref[at_inner] == 1
    for i in range(5):
        e, w = east_pops[i], west_pops[i]
        beta_scr[1, e, 24:25, :] = above[i : i + 1]
        beta_scr[0, w, 7:8, :] = below[i : i + 1]
        beta_scr[0, e, 24:25, :] = jnp.where(inner, beta_scr[1, e, 8:9, :], 0.0)
        beta_scr[1, w, 7:8, :] = jnp.where(inner, beta_scr[0, w, 23:24, :], 0.0)
    z = iota((8, plane), 1) & 15
    for g in range(2):
        for h in range(2):
            rows = slice(8 * h, 8 * h + 8)
            first = 8 + 8 * h
            bits = bits_ref[g, rows, :]
            pulled = []
            for i in range(pops):
                c = velocities[i]
                v = beta_scr[g, i, first + c[0] : first + c[0] + 8, :]
                v = moved_cells(v, c, z)
                back = beta_scr[g, opposite[i], first : first + 8, :]
                pulled.append(jnp.where((bits & (1 << i)) != 0, back, v))
            u = [u_ref[g, a, rows, :] for a in range(3)]
            done = collide(pulled, u, keep_ref[g, rows, :], gain_ref[g, rows, :])
            for i in range(pops):
                out_ref[g, i, rows, :] = done[i]
    if not last:
        pack(d_ref, out_ref, w_ref, k_ref, msg_ref, loc_ref, item_scr, rim_scr, half_scr)


def smem():
    return pl.BlockSpec(memory_space=pltpu.SMEM)


def vmem():
    return pl.BlockSpec(memory_space=pltpu.VMEM)


def shape(*dims, dtype=f32):
    return jax.ShapeDtypeStruct(dims, dtype)


params = pltpu.CompilerParams(vmem_limit_bytes=24 * 1024 * 1024)
half_scratch = [pltpu.VMEM((2, 320, 128), f32)]
pack_scratch = [pltpu.VMEM((160, plane), f32), pltpu.VMEM((8, plane), f32)] + half_scratch
message = shape(message_rows, plane)
field = shape(2, edge, plane)


def describe(chain, parent, children):
    level = lax.axis_index("lvl")
    slab = lax.axis_index("slab")
    odd = slab & 1
    offsets = jnp.array([1, -1, 0], jnp.int32) * (1 - 2 * odd)
    child = children.reshape(16)
    child_code = jnp.arange(16, dtype=jnp.int32) * 2 + (child & 1)
    child_hit = (child >= 0)[None] & (((child >> 1) - slab)[None] == offsets[:, None])
    above, octant = parent[:, 0], parent[:, 1]
    fine_code = jnp.arange(2, dtype=jnp.int32) * 16 + octant * 2 + (above & 1)
    fine_hit = (above >= 0)[None] & (((above >> 1) - slab)[None] == offsets[:, None])
    coarse = level == 0
    valid = jnp.where(coarse, jnp.any(child_hit, axis=1), jnp.any(fine_hit, axis=1))
    code = jnp.where(
        coarse,
        jnp.sum(jnp.where(child_hit, child_code[None], 0), axis=1),
        jnp.sum(jnp.where(fine_hit, fine_code[None], 0), axis=1),
    )
    links = (chain[0] >= 0).astype(jnp.int32)
    rest = jnp.stack([level, odd, links[0, 0], links[0, 1], links[1, 1]])
    parts = [valid.astype(jnp.int32), code >> 4, (code >> 1) & 7, code & 1, rest]
    return jnp.concatenate([p.astype(jnp.int32) for p in parts])


def local(
    adjoint_final, populations, relaxation, blend, solid, chain, parent, children, *, slabs
):
    alpha = adjoint_final[0]
    weights = blend[0]
    steps = populations.shape[0]
    table = describe(chain, parent, children)

    with jax.named_scope("pack_first"):
        msg, loc, kept = pl.pallas_call(
            first_pack_kernel,
            out_shape=[message, shape(16, plane), field],
            in_specs=[smem(), vmem(), vmem()],
            out_specs=[vmem()] * 3,
            scratch_shapes=pack_scratch,
            compiler_params=params,
        )(table, alpha, weights)

    with jax.named_scope("flow_fields"):
        flows, keep, gain, bits = pl.pallas_call(
            fields_kernel,
            out_shape=[
                shape(steps, 2, 3, edge, plane),
                field,
                field,
                shape(2, edge, plane, dtype=jnp.int32),
            ],
            in_specs=[vmem()] * 3,
            out_specs=[vmem()] * 4,
            scratch_shapes=[pltpu.VMEM((32, plane), f32)],
            compiler_params=params,
        )(populations[:, 0], relaxation[0], solid[0])

    def padded(rows):
        return jnp.pad(rows, ((40, 8), (0, 0)))

    for t in range(steps - 1, -1, -1):
        last = t == 0
        with jax.named_scope("exchange"):
            lvl = level_swap(msg, slabs)
            mate = mate_swap(lvl[0:56] + padded(loc[0:8]), slabs)
            far = far_swap(lvl[56:112] + padded(loc[8:16] + mate[48:56]), slabs)
            late = mate_swap(far[48:56], slabs)
        outs = [shape(2, pops, edge, plane)]
        if not last:
            outs += [message, shape(16, plane)]
        with jax.named_scope("step"):
            got = pl.pallas_call(
                functools.partial(step_kernel, last=last),
                out_shape=outs,
                in_specs=[smem()] + [vmem()] * 11,
                out_specs=[vmem()] * len(outs),
                scratch_shapes=[pltpu.VMEM((2, pops, 32, plane), f32)]
                + (half_scratch if last else pack_scratch),
                compiler_params=params,
            )(table, alpha, weights, kept, flows[t], keep, gain, bits, lvl, mate, far, late)
        alpha = got[0]
        if not last:
            msg, loc = got[1:]
    return alpha[None]


def solution(mesh):
    return jax.shard_map(
        functools.partial(local, slabs=mesh.shape["slab"]),
        mesh=mesh,
        in_specs=(
            P("lvl", "slab", None, None, None),
            P(None, "lvl", "slab", None, None, None),
            P("lvl", "slab", None, None),
            P("lvl", "slab", None, None),
            P("lvl", "slab", None, None),
            P("lvl", "slab", None),
            P("slab", None),
            P("slab", None),
        ),
        out_specs=P("lvl", "slab", None, None, None),
        check_vma=False,
    )
```

```python
import functools

import jax
import jax.numpy as jnp
from jax import lax
from jax.experimental import pallas as pl
from jax.experimental.pallas import tpu as pltpu
from jax.sharding import PartitionSpec as P

velocities = [
    (0, 0, 0),
    (1, 0, 0),
    (-1, 0, 0),
    (0, 1, 0),
    (0, -1, 0),
    (0, 0, 1),
    (0, 0, -1),
    (1, 1, 0),
    (-1, -1, 0),
    (1, -1, 0),
    (-1, 1, 0),
    (1, 0, 1),
    (-1, 0, -1),
    (1, 0, -1),
    (-1, 0, 1),
    (0, 1, 1),
    (0, -1, -1),
    (0, 1, -1),
    (0, -1, 1),
]
east_pops = [1, 7, 9, 11, 13]
west_pops = [2, 8, 10, 12, 14]
opposite = [velocities.index((-c[0], -c[1], -c[2])) for c in velocities]
axes = ("slab", "lvl")
pops, edge, plane = 19, 16, 256
f32, bf16 = jnp.float32, jnp.bfloat16

item_row = (0, 0, 56)
mate_d = 40
own_f, far_f, own_d, mate_f, far_d = 40, 48, 96, 104, 112
mate_rows, level_rows = 48, 120
at_level, at_odd, at_prev, at_inner, at_next = 12, 13, 14, 15, 16
table_size = 17


def level_swap(value, slabs):
    pairs = [(2 * s + v, 2 * s + 1 - v) for s in range(slabs) for v in (0, 1)]
    return lax.ppermute(value, axes, pairs)


def mate_swap(value, slabs, cross):
    pairs = [(2 * s + v, 2 * (s ^ 1) + (v ^ cross)) for s in range(slabs) for v in (0, 1)]
    return lax.ppermute(value, axes, pairs)


def far_swap(value, slabs):
    pairs = []
    for s in range(slabs):
        other = s - 1 if s % 2 == 0 else s + 1
        for v in (0, 1):
            if 0 <= other < slabs:
                pairs.append((2 * s + v, 2 * other + v))
            else:
                pairs.append((2 * s + v, 2 * s + 1 - v))
    return lax.ppermute(value, axes, pairs)


def cell_key(index, level, octant):
    y, z = index >> 4, index & 15
    fine = (y >> 1) * 8 + (z >> 1)
    inside = ((y >> 3) == ((octant >> 1) & 1)) & ((z >> 3) == (octant & 1))
    coarse = jnp.where(inside, (y & 7) * 8 + (z & 7), -1)
    return jnp.where(level == 1, fine, coarse)


def select(values, matrix):
    high = values.astype(bf16)
    low = (values - high.astype(f32)).astype(bf16)
    return jnp.dot(high, matrix, preferred_element_type=f32) + jnp.dot(
        low, matrix, preferred_element_type=f32
    )


def ones_where(mask):
    return jnp.where(mask, 1.0, 0.0).astype(bf16)


def iota(shape, dim):
    return lax.broadcasted_iota(jnp.int32, shape, dim)


def pack(d_ref, alpha_ref, w_ref, k_ref, near_ref, lvl_ref, loc_ref, item_scr, rim_scr, half_scr):
    level = d_ref[at_level]
    odd = d_ref[at_odd]
    near_ref[...] = jnp.zeros_like(near_ref)
    lvl_ref[...] = jnp.zeros_like(lvl_ref)
    item_scr[152:160, :] = jnp.zeros((8, plane), f32)
    rim_scr[...] = jnp.zeros_like(rim_scr)
    for i in range(5):
        e, w = east_pops[i], west_pops[i]
        low = alpha_ref[0, e, 0:1, :] * k_ref[0, 0:1, :]
        high = alpha_ref[1, w, edge - 1 : edge, :] * k_ref[1, edge - 1 : edge, :]
        loc_ref[i : i + 1, :] = jnp.where(odd == 1, low, high)
        loc_ref[8 + i : 9 + i, :] = jnp.where(odd == 1, high, low)
    loc_ref[5:8, :] = jnp.zeros((3, plane), f32)
    loc_ref[13:16, :] = jnp.zeros((3, plane), f32)
    for j in range(3):
        base = item_row[j]
        out_ref = near_ref if j == 0 else lvl_ref

        @pl.when(d_ref[j] == 1)
        def _(j=j, base=base, out_ref=out_ref):
            g, octant, other = d_ref[3 + j], d_ref[6 + j], d_ref[9 + j]
            ox = octant >> 2

            @pl.when(level == 0)
            def _():
                rows = pl.ds(pl.multiple_of(ox * 8, 8), 8)
                part = alpha_ref[g, :, rows, :] * w_ref[g, rows, :][None]
                item_scr[0:152, :] = part.reshape(152, plane)

            @pl.when(level == 1)
            def _():
                part = (alpha_ref[g] * w_ref[g][None]).reshape(304, plane)
                for n in range(2):
                    lanes = slice(128 * n, 128 * n + 128)
                    half_scr[n, 0:304, :] = part[:, lanes]
                    item_scr[0:152, lanes] = (
                        half_scr[n, pl.ds(0, 152, stride=2), :]
                        + half_scr[n, pl.ds(1, 152, stride=2), :]
                    )

            cells = cell_key(iota((plane, 128), 0), level, octant)
            picked = select(item_scr[...], ones_where(cells == (iota((plane, 128), 1) & 63)))
            left = iota((40, 128), 1) < 64
            out_ref[base : base + 40, 0:128] = jnp.where(left, picked[0:40], picked[40:80])
            out_ref[base : base + 40, 128:256] = jnp.where(left, picked[80:120], picked[120:160])

            @pl.when((level == 0) | (ox == other))
            def _():
                for i in range(5):
                    e, w = east_pops[i] * 8, west_pops[i] * 8 + 7
                    rim_scr[i : i + 1, :] = jnp.where(
                        other == 1, item_scr[w : w + 1, :], item_scr[e : e + 1, :]
                    )
                source = cell_key(iota((plane, plane), 0), level, octant)
                target = cell_key(iota((plane, plane), 1), 1 - level, octant)
                spread = select(rim_scr[...], ones_where(source == target))
                spread = spread * jnp.where(level == 0, 0.125, 1.0)
                towards_d = other != odd
                if j == 0:

                    @pl.when(towards_d)
                    def _():
                        near_ref[mate_d : mate_d + 8, :] = spread

                    @pl.when(jnp.logical_not(towards_d))
                    def _():
                        lvl_ref[mate_f : mate_f + 8, :] = spread

                else:
                    if j == 1:
                        row = jnp.where(towards_d, far_d, far_f)
                    else:
                        row = jnp.where(towards_d, own_d, own_f)
                    lvl_ref[pl.ds(pl.multiple_of(row, 8), 8), :] = spread


def describe(slab, level, chain_ref, parent_ref, children_ref, d_ref):
    odd = slab & 1
    for n in range(3):
        d_ref[n] = 0

    def note(valid, offset, g, octant, other):
        slot = jnp.where(offset == 0, 2, jnp.where(offset == 1 - 2 * odd, 0, 1))

        @pl.when(valid)
        def _():
            d_ref[slot] = 1
            d_ref[3 + slot] = g
            d_ref[6 + slot] = octant
            d_ref[9 + slot] = other & 1

    @pl.when(level == 0)
    def _():
        for g in range(2):
            for octant in range(8):
                fine = children_ref[g, octant]
                note(fine >= 0, (fine >> 1) - slab, g, octant, fine)

    @pl.when(level == 1)
    def _():
        for g in range(2):
            coarse = parent_ref[g, 0]
            note(coarse >= 0, (coarse >> 1) - slab, g, parent_ref[g, 1], coarse)

    def flag(entry):
        return jnp.where(entry >= 0, 1, 0)

    d_ref[at_level] = level
    d_ref[at_odd] = odd
    d_ref[at_prev] = flag(chain_ref[0, 0])
    d_ref[at_inner] = flag(chain_ref[0, 1])
    d_ref[at_next] = flag(chain_ref[1, 1])


def first_pack_kernel(*refs):
    (chain_ref, parent_ref, children_ref, alpha_in, w_in) = refs[:5]
    d_ref, near_ref, lvl_ref, loc_ref, k_ref, alpha_ref, w_ref = refs[5:12]
    scratch, sems = refs[12:15], refs[15]
    copies = [
        pltpu.make_async_copy(alpha_in, alpha_ref, sems.at[0]),
        pltpu.make_async_copy(w_in, w_ref, sems.at[1]),
    ]
    for copy in copies:
        copy.start()
    level = lax.axis_index("lvl")
    describe(lax.axis_index("slab"), level, chain_ref, parent_ref, children_ref, d_ref)
    for n in range(3):

        @pl.when(d_ref[n] == 0)
        def _(n=n):
            for m in (3, 6, 9):
                d_ref[m + n] = 0

    x = iota((edge, plane), 0)
    cell = iota((edge, plane), 1)
    covers = []
    for g in range(2):
        covered = jnp.zeros((edge, plane), jnp.bool_)
        for j in range(3):
            octant = d_ref[6 + j]
            inside = (
                ((x >> 3) == (octant >> 2))
                & ((cell >> 7) == ((octant >> 1) & 1))
                & (((cell >> 3) & 1) == (octant & 1))
            ) | (level == 1)
            covered = covered | (inside & (d_ref[j] == 1) & (d_ref[3 + j] == g))
        covers.append(covered)
    for copy in copies:
        copy.wait()
    for g in range(2):
        k_ref[g] = jnp.where(covers[g], 1.0 - w_ref[g], 1.0)
    pack(d_ref, alpha_ref, w_ref, k_ref, near_ref, lvl_ref, loc_ref, *scratch)


def moved_cells(values, c, z):
    if c[1] == 0 and c[2] == 0:
        return values
    base = -16 * c[1]
    axis = values.ndim - 1
    if c[2] == 0:
        return pltpu.roll(values, base % plane, axis)
    inner = pltpu.roll(values, (base - c[2]) % plane, axis)
    around = pltpu.roll(values, (base + 15 * c[2]) % plane, axis)
    return jnp.where(z == (15 if c[2] == 1 else 0), around, inner)


def fields_kernel(pop_ref, relax_ref, solid_ref, u_ref, keep_ref, gain_ref, bits_ref, pad_scr):
    z = iota((edge, plane), 1) & 15
    for g in range(2):
        solid = solid_ref[g] > 0
        omega = relax_ref[g]
        keep_ref[g] = jnp.where(solid, 0.0, 1.0 - omega)
        gain_ref[g] = jnp.where(solid, 0.0, omega)
        pad_scr[0:8, :] = jnp.zeros((8, plane), f32)
        pad_scr[24:32, :] = jnp.zeros((8, plane), f32)
        pad_scr[8:24, :] = jnp.where(solid, 1.0, 0.0)
        bits = jnp.zeros((edge, plane), jnp.int32)
        for i in range(pops):
            c = velocities[i]
            blocked = moved_cells(pad_scr[8 + c[0] : 24 + c[0], :], c, z) > 0.5
            bits = bits | jnp.where(blocked, 1 << i, 0)
        bits_ref[g] = bits
    steps = pop_ref.shape[0]
    for t in range(steps):
        for g in range(2):
            total = jnp.zeros((edge, plane), f32)
            flow = [jnp.zeros((edge, plane), f32) for _ in range(3)]
            for i in range(pops):
                f = pop_ref[t, g, i].astype(f32)
                total = total + f
                for a in range(3):
                    if velocities[i][a] == 1:
                        flow[a] = flow[a] + f
                    elif velocities[i][a] == -1:
                        flow[a] = flow[a] - f
            for a in range(3):
                u_ref[t, g, a] = flow[a] / total


def collide(pulled, u, keep, gain):
    g = pulled
    plus = {i: g[i] + g[i + 1] for i in range(1, pops, 2)}
    minus = {i: g[i] - g[i + 1] for i in range(1, pops, 2)}
    xy, xz, yz = plus[7] + plus[9], plus[11] + plus[13], plus[15] + plus[17]
    px, py, pz = 2.0 * plus[1], 2.0 * plus[3], 2.0 * plus[5]
    weight = 12.0 * g[0] + (px + py + pz) + (xy + xz + yz)
    qxx, qyy, qzz = px + xy + xz, py + xy + yz, pz + xz + yz
    qxy, qxz, qyz = plus[7] - plus[9], plus[11] - plus[13], plus[15] - plus[17]
    jx = 2.0 * minus[1] + (minus[7] + minus[9]) + (minus[11] + minus[13])
    jy = 2.0 * minus[3] + (minus[7] - minus[9]) + (minus[15] + minus[17])
    jz = 2.0 * minus[5] + (minus[11] - minus[13]) + (minus[15] - minus[17])
    ux, uy, uz = u
    qux = qxx * ux + qxy * uy + qxz * uz
    quy = qxy * ux + qyy * uy + qyz * uz
    quz = qxz * ux + qyz * uy + qzz * uz
    speed = ux * ux + uy * uy + uz * uz
    along = ux * qux + uy * quy + uz * quz
    scale = gain * (1.0 / 36.0)
    rest = scale * (weight * (1.0 + 1.5 * speed) - 4.5 * along)
    scale = gain * (1.0 / 12.0)
    mx = scale * (jx + 3.0 * qux - ux * weight)
    my = scale * (jy + 3.0 * quy - uy * weight)
    mz = scale * (jz + 3.0 * quz - uz * weight)
    out = [None] * pops
    out[0] = keep * g[0] + rest
    pairs = [mx, my, mz, mx + my, mx - my, mx + mz, mx - mz, my + mz, my - mz]
    for n, i in enumerate(range(1, pops, 2)):
        out[i] = keep * g[i] + (rest + pairs[n])
        out[i + 1] = keep * g[i + 1] + (rest - pairs[n])
    return out


def step_kernel(*refs):
    (d_ref, alpha_ref, k_ref, u_ref, keep_ref, gain_ref, bits_ref) = refs[:7]
    (mate_ref, lvl_ref, far_ref, out_ref, beta_scr, half_scr) = refs[7:]
    level = d_ref[at_level]
    odd = d_ref[at_odd]
    for g in range(2):
        beta_scr[g, :, 8:24, :] = alpha_ref[g] * k_ref[g][None]
    sources = (mate_ref, far_ref, lvl_ref)
    for j in range(3):
        first = item_row[j]

        @pl.when(d_ref[j] == 1)
        def _(j=j, first=first):
            g, octant = d_ref[3 + j], d_ref[6 + j]
            left = iota((40, 128), 1) < 64
            a = sources[j][first : first + 40, 0:128]
            b = sources[j][first : first + 40, 128:256]
            stacked = jnp.concatenate(
                [
                    jnp.where(left, a, 0.0),
                    jnp.where(left, 0.0, a),
                    jnp.where(left, b, 0.0),
                    jnp.where(left, 0.0, b),
                ],
                axis=0,
            )
            target = cell_key(iota((128, plane), 1), level, octant)
            spread = select(stacked, ones_where((iota((128, plane), 0) & 63) == target))

            @pl.when(level == 0)
            def _():
                rows = pl.ds(pl.multiple_of(8 + (octant >> 2) * 8, 8), 8)
                beta_scr[g, :, rows, :] += spread[0:152].reshape(pops, 8, plane)

            @pl.when(level == 1)
            def _():
                for n in range(2):
                    lanes = slice(128 * n, 128 * n + 128)
                    half = spread[:, lanes] * 0.125
                    half_scr[n, pl.ds(0, 160, stride=2), :] = half
                    half_scr[n, pl.ds(1, 160, stride=2), :] = half
                    both = half_scr[n, 0:304, :].reshape(pops, edge, 128)
                    beta_scr[g, :, 8:24, lanes] += both

    from_d = lvl_ref[mate_f : mate_f + 8, :]
    from_f = far_ref[own_f : own_f + 8, :] + lvl_ref[far_d : far_d + 8, :]
    above = jnp.where(odd == 1, from_f, from_d)
    below = jnp.where(odd == 1, from_d, from_f)
    above = jnp.where(d_ref[at_next] == 1, above, 0.0)
    below = jnp.where(d_ref[at_prev] == 1, below, 0.0)
    inner = d_ref[at_inner] == 1
    for i in range(5):
        e, w = east_pops[i], west_pops[i]
        beta_scr[1, e, 24:25, :] = above[i : i + 1]
        beta_scr[0, w, 7:8, :] = below[i : i + 1]
        beta_scr[0, e, 24:25, :] = jnp.where(inner, beta_scr[1, e, 8:9, :], 0.0)
        beta_scr[1, w, 7:8, :] = jnp.where(inner, beta_scr[0, w, 23:24, :], 0.0)
    z = iota((8, plane), 1) & 15
    for g in range(2):
        for h in range(2):
            rows = slice(8 * h, 8 * h + 8)
            first = 8 + 8 * h
            bits = bits_ref[g, rows, :]
            pulled = []
            for i in range(pops):
                c = velocities[i]
                v = beta_scr[g, i, first + c[0] : first + c[0] + 8, :]
                v = moved_cells(v, c, z)
                back = beta_scr[g, opposite[i], first : first + 8, :]
                pulled.append(jnp.where((bits & (1 << i)) != 0, back, v))
            u = [u_ref[g, a, rows, :] for a in range(3)]
            done = collide(pulled, u, keep_ref[g, rows, :], gain_ref[g, rows, :])
            for i in range(pops):
                out_ref[g, i, rows, :] = done[i]


def add_late(d_ref, alpha_in, late_ref, u_ref, keep_ref, gain_ref, alpha_ref):
    alpha_ref[...] = alpha_in[...]
    z = iota((8, plane), 1) & 15
    late = late_ref[...]

    def side(g, x, link, moving):
        @pl.when(link == 1)
        def _():
            pulled = [0.0] * pops
            for n, i in enumerate(moving):
                pulled[i] = moved_cells(late, velocities[i], z)[n : n + 1]
            rows = slice(x, x + 1)
            u = [u_ref[g, a, rows, :] for a in range(3)]
            added = collide(pulled, u, keep_ref[g, rows, :], gain_ref[g, rows, :])
            for i in range(pops):
                alpha_ref[g, i, rows, :] += added[i]

    @pl.when(d_ref[at_odd] == 0)
    def _():
        side(1, edge - 1, d_ref[at_next], east_pops)

    @pl.when(d_ref[at_odd] == 1)
    def _():
        side(0, 0, d_ref[at_prev], west_pops)


def finish_kernel(*refs):
    (d_ref, alpha_in, late_ref, u_ref, keep_ref, gain_ref, w_ref, k_ref) = refs[:8]
    (alpha_ref, near_ref, lvl_ref, loc_ref) = refs[8:12]
    add_late(d_ref, alpha_in, late_ref, u_ref, keep_ref, gain_ref, alpha_ref)
    pack(d_ref, alpha_ref, w_ref, k_ref, near_ref, lvl_ref, loc_ref, *refs[12:])


def last_kernel(d_ref, alpha_in, late_ref, u_ref, keep_ref, gain_ref, alpha_ref):
    add_late(d_ref, alpha_in, late_ref, u_ref, keep_ref, gain_ref, alpha_ref)


def smem():
    return pl.BlockSpec(memory_space=pltpu.SMEM)


def vmem():
    return pl.BlockSpec(memory_space=pltpu.VMEM)


def shape(*dims, dtype=f32):
    return jax.ShapeDtypeStruct(dims, dtype)


params = pltpu.CompilerParams(vmem_limit_bytes=24 * 1024 * 1024)
half_scratch = [pltpu.VMEM((2, 320, 128), f32)]
pack_scratch = [pltpu.VMEM((160, plane), f32), pltpu.VMEM((8, plane), f32)] + half_scratch
near_shape = shape(mate_rows, plane)
level_shape = shape(level_rows, plane)
ends_shape = shape(16, plane)
field = shape(2, edge, plane)
state = shape(2, pops, edge, plane)


def any_space():
    return pl.BlockSpec(memory_space=pl.ANY)


def cost(flops, bytes_accessed):
    return pl.CostEstimate(flops=flops, bytes_accessed=bytes_accessed, transcendentals=0)


def local(
    adjoint_final, populations, relaxation, blend, solid, chain, parent, children, *, slabs
):
    steps = populations.shape[0]
    with jax.named_scope("pack_first"):
        table, near, lvl, ends, kept, alpha, weights = pl.pallas_call(
            first_pack_kernel,
            out_shape=[
                shape(table_size, dtype=jnp.int32),
                near_shape,
                level_shape,
                ends_shape,
                field,
                state,
                field,
            ],
            in_specs=[smem()] * 3 + [any_space()] * 2,
            out_specs=[smem()] + [vmem()] * 6,
            scratch_shapes=pack_scratch + [pltpu.SemaphoreType.DMA((2,))],
            compiler_params=params,
        )(chain[0], parent, children, adjoint_final[0], blend[0])

    with jax.named_scope("flow_fields"):
        flows, keep, gain, bits = pl.pallas_call(
            fields_kernel,
            out_shape=[
                shape(steps, 2, 3, edge, plane),
                field,
                field,
                shape(2, edge, plane, dtype=jnp.int32),
            ],
            in_specs=[vmem()] * 3,
            out_specs=[vmem()] * 4,
            scratch_shapes=[pltpu.VMEM((32, plane), f32)],
            compiler_params=params,
            cost_estimate=cost(4_000_000, 2_000_000),
        )(populations[:, 0], relaxation[0], solid[0])

    for t in range(steps - 1, -1, -1):
        u = flows[t]
        with jax.named_scope("exchange"):
            lvl = level_swap(lvl, slabs)
            mate = mate_swap(near, slabs, 1)
            extra = ends[8:16] + mate[mate_d : mate_d + 8]
            far = far_swap(lvl[0:56] + jnp.pad(extra, ((own_f, 8), (0, 0))), slabs)
            late = mate_swap(ends[0:8] + lvl[own_d : own_d + 8] + far[far_f : far_f + 8], slabs, 0)
        with jax.named_scope("step"):
            alpha = pl.pallas_call(
                step_kernel,
                out_shape=state,
                in_specs=[smem()] + [vmem()] * 9,
                out_specs=vmem(),
                scratch_shapes=[pltpu.VMEM((2, pops, 32, plane), f32)] + half_scratch,
                compiler_params=params,
                cost_estimate=cost(8_000_000, 2_000_000),
            )(table, alpha, kept, u, keep, gain, bits, mate, lvl, far)
        with jax.named_scope("finish"):
            if t == 0:
                alpha = pl.pallas_call(
                    last_kernel,
                    out_shape=state,
                    in_specs=[smem()] + [vmem()] * 5,
                    out_specs=vmem(),
                    compiler_params=params,
                )(table, alpha, late, u, keep, gain)
            else:
                alpha, near, lvl, ends = pl.pallas_call(
                    finish_kernel,
                    out_shape=[state, near_shape, level_shape, ends_shape],
                    in_specs=[smem()] + [vmem()] * 7,
                    out_specs=[vmem()] * 4,
                    scratch_shapes=pack_scratch,
                    compiler_params=params,
                )(table, alpha, late, u, keep, gain, weights, kept)
    return alpha[None]


def solution(mesh):
    return jax.shard_map(
        functools.partial(local, slabs=mesh.shape["slab"]),
        mesh=mesh,
        in_specs=(
            P("lvl", "slab", None, None, None),
            P(None, "lvl", "slab", None, None, None),
            P("lvl", "slab", None, None),
            P("lvl", "slab", None, None),
            P("lvl", "slab", None, None),
            P("lvl", "slab", None),
            P("slab", None),
            P("slab", None),
        ),
        out_specs=P("lvl", "slab", None, None, None),
        check_vma=False,
    )
```

```python
import functools

import jax
import jax.numpy as jnp
from jax import lax
from jax.experimental import pallas as pl
from jax.experimental.pallas import tpu as pltpu
from jax.sharding import PartitionSpec as P

velocities = [
    (0, 0, 0),
    (1, 0, 0),
    (-1, 0, 0),
    (0, 1, 0),
    (0, -1, 0),
    (0, 0, 1),
    (0, 0, -1),
    (1, 1, 0),
    (-1, -1, 0),
    (1, -1, 0),
    (-1, 1, 0),
    (1, 0, 1),
    (-1, 0, -1),
    (1, 0, -1),
    (-1, 0, 1),
    (0, 1, 1),
    (0, -1, -1),
    (0, 1, -1),
    (0, -1, 1),
]
east_pops = [1, 7, 9, 11, 13]
west_pops = [2, 8, 10, 12, 14]
opposite = [velocities.index((-c[0], -c[1], -c[2])) for c in velocities]
axes = ("slab", "lvl")
pops, edge, plane = 19, 16, 256
f32, bf16 = jnp.float32, jnp.bfloat16

item_row = (0, 0, 56)
mate_d = 40
own_f, far_f, own_d, mate_f, far_d = 40, 48, 96, 104, 112
mate_rows, level_rows = 48, 120
at_level, at_odd, at_prev, at_inner, at_next = 12, 13, 14, 15, 16
table_size = 17


def level_swap(value, slabs):
    pairs = [(2 * s + v, 2 * s + 1 - v) for s in range(slabs) for v in (0, 1)]
    return lax.ppermute(value, axes, pairs)


def mate_swap(value, slabs, cross):
    pairs = [(2 * s + v, 2 * (s ^ 1) + (v ^ cross)) for s in range(slabs) for v in (0, 1)]
    return lax.ppermute(value, axes, pairs)


def far_swap(value, slabs):
    pairs = []
    for s in range(slabs):
        other = s - 1 if s % 2 == 0 else s + 1
        for v in (0, 1):
            if 0 <= other < slabs:
                pairs.append((2 * s + v, 2 * other + v))
            else:
                pairs.append((2 * s + v, 2 * s + 1 - v))
    return lax.ppermute(value, axes, pairs)


def cell_key(index, level, octant):
    y, z = index >> 4, index & 15
    fine = (y >> 1) * 8 + (z >> 1)
    inside = ((y >> 3) == ((octant >> 1) & 1)) & ((z >> 3) == (octant & 1))
    coarse = jnp.where(inside, (y & 7) * 8 + (z & 7), -1)
    return jnp.where(level == 1, fine, coarse)


def select(values, matrix):
    high = values.astype(bf16)
    low = (values - high.astype(f32)).astype(bf16)
    return jnp.dot(high, matrix, preferred_element_type=f32) + jnp.dot(
        low, matrix, preferred_element_type=f32
    )


def ones_where(mask):
    return jnp.where(mask, 1.0, 0.0).astype(bf16)


def iota(shape, dim):
    return lax.broadcasted_iota(jnp.int32, shape, dim)


def pick_matrices(d_ref, j):
    level, octant = d_ref[at_level], d_ref[6 + j]
    source = cell_key(iota((plane, 128), 0), level, octant)
    pick = ones_where(source == (iota((1, 128), 1) & 63))
    target = cell_key(iota((1, plane), 1), 1 - level, octant)
    place = jnp.concatenate(
        [ones_where(source == target[:, :128]), ones_where(source == target[:, 128:])], axis=1
    )
    return pick, place


def plane_scale(d_ref):
    return jnp.where(d_ref[at_level] == 0, 0.125, 1.0)


def pack(d_ref, alpha_ref, w_ref, k_ref, near_ref, lvl_ref, loc_ref, scratch, matrices):
    item_scr, rim_scr, half_scr = scratch
    level = d_ref[at_level]
    odd = d_ref[at_odd]
    near_ref[...] = jnp.zeros_like(near_ref)
    lvl_ref[...] = jnp.zeros_like(lvl_ref)
    item_scr[152:160, :] = jnp.zeros((8, plane), f32)
    rim_scr[...] = jnp.zeros_like(rim_scr)
    loc_ref[...] = jnp.zeros_like(loc_ref)
    for i in range(5):
        e, w = east_pops[i], west_pops[i]
        low = alpha_ref[0, e, 0:1, :] * k_ref[0, 0:1, :]
        high = alpha_ref[1, w, edge - 1 : edge, :] * k_ref[1, edge - 1 : edge, :]
        loc_ref[i : i + 1, :] = jnp.where(odd == 1, low, high)
        loc_ref[8 + i : 9 + i, :] = jnp.where(odd == 1, high, low)
    for j in range(3):
        base = item_row[j]
        out_ref = near_ref if j == 0 else lvl_ref

        @pl.when(d_ref[j] == 1)
        def _(j=j, base=base, out_ref=out_ref):
            g, octant, other = d_ref[3 + j], d_ref[6 + j], d_ref[9 + j]
            ox = octant >> 2
            pick, place = matrices(j)

            @pl.when(level == 0)
            def _():
                rows = pl.ds(pl.multiple_of(ox * 8, 8), 8)
                part = alpha_ref[g, :, rows, :] * w_ref[g, rows, :][None]
                item_scr[0:152, :] = part.reshape(152, plane)

            @pl.when(level == 1)
            def _():
                part = (alpha_ref[g] * w_ref[g][None]).reshape(304, plane)
                for n in range(2):
                    lanes = slice(128 * n, 128 * n + 128)
                    half_scr[n, 0:304, :] = part[:, lanes]
                    item_scr[0:152, lanes] = (
                        half_scr[n, pl.ds(0, 152, stride=2), :]
                        + half_scr[n, pl.ds(1, 152, stride=2), :]
                    )

            picked = select(item_scr[...], pick)
            left = iota((40, 128), 1) < 64
            out_ref[base : base + 40, 0:128] = jnp.where(left, picked[0:40], picked[40:80])
            out_ref[base : base + 40, 128:256] = jnp.where(left, picked[80:120], picked[120:160])

            @pl.when((level == 0) | (ox == other))
            def _():
                for i in range(5):
                    e, w = east_pops[i] * 8, west_pops[i] * 8 + 7
                    rim_scr[i : i + 1, :] = jnp.where(
                        other == 1, item_scr[w : w + 1, :], item_scr[e : e + 1, :]
                    )
                spread = select(rim_scr[...], place) * plane_scale(d_ref)
                towards_d = other != odd
                if j == 0:

                    @pl.when(towards_d)
                    def _():
                        near_ref[mate_d : mate_d + 8, :] = spread

                    @pl.when(jnp.logical_not(towards_d))
                    def _():
                        lvl_ref[mate_f : mate_f + 8, :] = spread

                else:
                    if j == 1:
                        row = jnp.where(towards_d, far_d, far_f)
                    else:
                        row = jnp.where(towards_d, own_d, own_f)
                    lvl_ref[pl.ds(pl.multiple_of(row, 8), 8), :] = spread


def describe(slab, level, chain_ref, parent_ref, children_ref, d_ref):
    odd = slab & 1
    for n in range(at_level):
        d_ref[n] = 0

    def note(valid, offset, g, octant, other):
        slot = jnp.where(offset == 0, 2, jnp.where(offset == 1 - 2 * odd, 0, 1))

        @pl.when(valid)
        def _():
            d_ref[slot] = 1
            d_ref[3 + slot] = g
            d_ref[6 + slot] = octant
            d_ref[9 + slot] = other & 1

    @pl.when(level == 0)
    def _():
        for g in range(2):
            for octant in range(8):
                fine = children_ref[g, octant]
                note(fine >= 0, (fine >> 1) - slab, g, octant, fine)

    @pl.when(level == 1)
    def _():
        for g in range(2):
            coarse = parent_ref[g, 0]
            note(coarse >= 0, (coarse >> 1) - slab, g, parent_ref[g, 1], coarse)

    def flag(entry):
        return jnp.where(entry >= 0, 1, 0)

    d_ref[at_level] = level
    d_ref[at_odd] = odd
    d_ref[at_prev] = flag(chain_ref[0, 0])
    d_ref[at_inner] = flag(chain_ref[0, 1])
    d_ref[at_next] = flag(chain_ref[1, 1])


def first_pack_kernel(*refs):
    tables_in, (alpha_in, w_in) = refs[:3], refs[3:5]
    d_ref, near_ref, lvl_ref, loc_ref, k_ref, alpha_ref, w_ref = refs[5:12]
    scratch, tables, sems = refs[12:15], refs[15:18], refs[18]
    small = [pltpu.make_async_copy(tables_in[n], tables[n], sems.at[n]) for n in range(3)]
    large = [
        pltpu.make_async_copy(w_in, w_ref, sems.at[3]),
        pltpu.make_async_copy(alpha_in, alpha_ref, sems.at[4]),
    ]
    for copy in small + large:
        copy.start()
    for copy in small:
        copy.wait()
    level = lax.axis_index("lvl")
    describe(lax.axis_index("slab"), level, *tables, d_ref)
    x = iota((edge, plane), 0)
    cell = iota((edge, plane), 1)
    covers = []
    for g in range(2):
        covered = jnp.zeros((edge, plane), jnp.bool_)
        for j in range(3):
            octant = d_ref[6 + j]
            inside = (
                ((x >> 3) == (octant >> 2))
                & ((cell >> 7) == ((octant >> 1) & 1))
                & (((cell >> 3) & 1) == (octant & 1))
            ) | (level == 1)
            covered = covered | (inside & (d_ref[j] == 1) & (d_ref[3 + j] == g))
        covers.append(covered)
    for copy in large:
        copy.wait()
    for g in range(2):
        k_ref[g] = jnp.where(covers[g], 1.0 - w_ref[g], 1.0)
    matrices = functools.partial(pick_matrices, d_ref)
    pack(d_ref, alpha_ref, w_ref, k_ref, near_ref, lvl_ref, loc_ref, scratch, matrices)


def moved_cells(values, c, z):
    if c[1] == 0 and c[2] == 0:
        return values
    base = -16 * c[1]
    axis = values.ndim - 1
    if c[2] == 0:
        return pltpu.roll(values, base % plane, axis)
    inner = pltpu.roll(values, (base - c[2]) % plane, axis)
    around = pltpu.roll(values, (base + 15 * c[2]) % plane, axis)
    return jnp.where(z == (15 if c[2] == 1 else 0), around, inner)


def fields_kernel(*refs):
    d_ref, pop_ref, relax_ref, solid_ref = refs[:4]
    u_ref, keep_ref, gain_ref, bits_ref, pick_ref, place_ref, pad_scr = refs[4:]
    for j in range(3):
        pick_ref[j], place_ref[j] = pick_matrices(d_ref, j)
    z = iota((edge, plane), 1) & 15
    for g in range(2):
        solid = solid_ref[g] > 0
        omega = relax_ref[g]
        keep_ref[g] = jnp.where(solid, 0.0, 1.0 - omega)
        gain_ref[g] = jnp.where(solid, 0.0, omega)
        pad_scr[0:8, :] = jnp.zeros((8, plane), f32)
        pad_scr[24:32, :] = jnp.zeros((8, plane), f32)
        pad_scr[8:24, :] = jnp.where(solid, 1.0, 0.0)
        bits = jnp.zeros((edge, plane), jnp.int32)
        for i in range(pops):
            c = velocities[i]
            blocked = moved_cells(pad_scr[8 + c[0] : 24 + c[0], :], c, z) > 0.5
            bits = bits | jnp.where(blocked, 1 << i, 0)
        bits_ref[g] = bits
    steps = pop_ref.shape[0]
    for t in range(steps):
        for g in range(2):
            total = jnp.zeros((edge, plane), f32)
            flow = [jnp.zeros((edge, plane), f32) for _ in range(3)]
            for i in range(pops):
                f = pop_ref[t, g, i].astype(f32)
                total = total + f
                for a in range(3):
                    if velocities[i][a] == 1:
                        flow[a] = flow[a] + f
                    elif velocities[i][a] == -1:
                        flow[a] = flow[a] - f
            for a in range(3):
                u_ref[t, g, a] = flow[a] / total


def collide(pulled, u, keep, gain):
    g = pulled
    plus = {i: g[i] + g[i + 1] for i in range(1, pops, 2)}
    minus = {i: g[i] - g[i + 1] for i in range(1, pops, 2)}
    xy, xz, yz = plus[7] + plus[9], plus[11] + plus[13], plus[15] + plus[17]
    px, py, pz = 2.0 * plus[1], 2.0 * plus[3], 2.0 * plus[5]
    weight = 12.0 * g[0] + (px + py + pz) + (xy + xz + yz)
    qxx, qyy, qzz = px + xy + xz, py + xy + yz, pz + xz + yz
    qxy, qxz, qyz = plus[7] - plus[9], plus[11] - plus[13], plus[15] - plus[17]
    jx = 2.0 * minus[1] + (minus[7] + minus[9]) + (minus[11] + minus[13])
    jy = 2.0 * minus[3] + (minus[7] - minus[9]) + (minus[15] + minus[17])
    jz = 2.0 * minus[5] + (minus[11] - minus[13]) + (minus[15] - minus[17])
    ux, uy, uz = u
    qux = qxx * ux + qxy * uy + qxz * uz
    quy = qxy * ux + qyy * uy + qyz * uz
    quz = qxz * ux + qyz * uy + qzz * uz
    speed = ux * ux + uy * uy + uz * uz
    along = ux * qux + uy * quy + uz * quz
    scale = gain * (1.0 / 36.0)
    rest = scale * (weight * (1.0 + 1.5 * speed) - 4.5 * along)
    scale = gain * (1.0 / 12.0)
    mx = scale * (jx + 3.0 * qux - ux * weight)
    my = scale * (jy + 3.0 * quy - uy * weight)
    mz = scale * (jz + 3.0 * quz - uz * weight)
    out = [None] * pops
    out[0] = keep * g[0] + rest
    pairs = [mx, my, mz, mx + my, mx - my, mx + mz, mx - mz, my + mz, my - mz]
    for n, i in enumerate(range(1, pops, 2)):
        out[i] = keep * g[i] + (rest + pairs[n])
        out[i + 1] = keep * g[i + 1] + (rest - pairs[n])
    return out


def step_kernel(*refs, first, last):
    (d_ref, alpha_ref, k_ref, u_ref, keep_ref, gain_ref, bits_ref) = refs[:7]
    (mate_ref, lvl_ref, far_ref) = refs[7:10]
    refs = refs[10:]
    if not first:
        added_ref, refs = refs[0], refs[1:]
    if not last:
        (w_ref, pick_ref, place_ref), refs = refs[:3], refs[3:]
        out_ref, near_out, lvl_out, loc_out, beta_scr, item_scr, rim_scr, half_scr = refs
    else:
        out_ref, beta_scr, half_scr = refs
    level = d_ref[at_level]
    odd = d_ref[at_odd]
    for g in range(2):
        beta_scr[g, :, 8:24, :] = alpha_ref[g] * k_ref[g][None]
    if not first:
        for is_odd, (g, x) in enumerate(late_layer):

            @pl.when(odd == is_odd)
            def _(g=g, x=x):
                kept = k_ref[g, x : x + 1, :]
                for i in range(pops):
                    beta_scr[g, i, 8 + x : 9 + x, :] += added_ref[i : i + 1, :] * kept

    sources = (mate_ref, far_ref, lvl_ref)
    for j in range(3):
        first = item_row[j]

        @pl.when(d_ref[j] == 1)
        def _(j=j, first=first):
            g, octant = d_ref[3 + j], d_ref[6 + j]
            left = iota((40, 128), 1) < 64
            a = sources[j][first : first + 40, 0:128]
            b = sources[j][first : first + 40, 128:256]
            stacked = jnp.concatenate(
                [
                    jnp.where(left, a, 0.0),
                    jnp.where(left, 0.0, a),
                    jnp.where(left, b, 0.0),
                    jnp.where(left, 0.0, b),
                ],
                axis=0,
            )
            target = cell_key(iota((1, plane), 1), level, octant)
            spread = select(stacked, ones_where((iota((128, plane), 0) & 63) == target))

            @pl.when(level == 0)
            def _():
                rows = pl.ds(pl.multiple_of(8 + (octant >> 2) * 8, 8), 8)
                beta_scr[g, :, rows, :] += spread[0:152].reshape(pops, 8, plane)

            @pl.when(level == 1)
            def _():
                for n in range(2):
                    lanes = slice(128 * n, 128 * n + 128)
                    half = spread[:, lanes] * 0.125
                    half_scr[n, pl.ds(0, 160, stride=2), :] = half
                    half_scr[n, pl.ds(1, 160, stride=2), :] = half
                    both = half_scr[n, 0:304, :].reshape(pops, edge, 128)
                    beta_scr[g, :, 8:24, lanes] += both

    from_d = lvl_ref[mate_f : mate_f + 8, :]
    from_f = far_ref[own_f : own_f + 8, :] + lvl_ref[far_d : far_d + 8, :]
    above = jnp.where(odd == 1, from_f, from_d)
    below = jnp.where(odd == 1, from_d, from_f)
    above = jnp.where(d_ref[at_next] == 1, above, 0.0)
    below = jnp.where(d_ref[at_prev] == 1, below, 0.0)
    inner = d_ref[at_inner] == 1
    for i in range(5):
        e, w = east_pops[i], west_pops[i]
        beta_scr[1, e, 24:25, :] = above[i : i + 1]
        beta_scr[0, w, 7:8, :] = below[i : i + 1]
        beta_scr[0, e, 24:25, :] = jnp.where(inner, beta_scr[1, e, 8:9, :], 0.0)
        beta_scr[1, w, 7:8, :] = jnp.where(inner, beta_scr[0, w, 23:24, :], 0.0)
    z = iota((8, plane), 1) & 15
    for g in range(2):
        for h in range(2):
            rows = slice(8 * h, 8 * h + 8)
            first = 8 + 8 * h
            bits = bits_ref[g, rows, :]
            pulled = []
            for i in range(pops):
                c = velocities[i]
                v = beta_scr[g, i, first + c[0] : first + c[0] + 8, :]
                v = moved_cells(v, c, z)
                back = beta_scr[g, opposite[i], first : first + 8, :]
                pulled.append(jnp.where((bits & (1 << i)) != 0, back, v))
            u = [u_ref[g, a, rows, :] for a in range(3)]
            done = collide(pulled, u, keep_ref[g, rows, :], gain_ref[g, rows, :])
            for i in range(pops):
                out_ref[g, i, rows, :] = done[i]
    if not last:
        scratch = (item_scr, rim_scr, half_scr)
        matrices = lambda j: (pick_ref[j], place_ref[j])
        pack(d_ref, out_ref, w_ref, k_ref, near_out, lvl_out, loc_out, scratch, matrices)


late_layer = ((1, edge - 1), (0, 0))


def late_values(is_odd, late_ref, u_ref, keep_ref, gain_ref):
    g, x = late_layer[is_odd]
    z = iota((8, plane), 1) & 15
    late = late_ref[...]
    pulled = [0.0] * pops
    for n, i in enumerate((east_pops, west_pops)[is_odd]):
        pulled[i] = moved_cells(late, velocities[i], z)[n : n + 1]
    rows = slice(x, x + 1)
    u = [u_ref[g, a, rows, :] for a in range(3)]
    return collide(pulled, u, keep_ref[g, rows, :], gain_ref[g, rows, :])


def finish_kernel(*refs):
    (d_ref, late_ref, u_ref, keep_ref, gain_ref, w_ref, k_ref, pick_ref, place_ref) = refs[:9]
    (near_in, lvl_in, loc_in, added_ref, near_ref, lvl_ref, loc_ref, rim_scr) = refs[9:]
    level = d_ref[at_level]
    near_ref[...] = near_in[...]
    lvl_ref[...] = lvl_in[...]
    loc_ref[...] = loc_in[...]
    added_ref[...] = jnp.zeros_like(added_ref)
    rim_scr[...] = jnp.zeros_like(rim_scr)

    def side(is_odd):
        g, x = late_layer[is_odd]
        leaving = (west_pops, east_pops)[is_odd]
        values = late_values(is_odd, late_ref, u_ref, keep_ref, gain_ref)
        for i in range(pops):
            added_ref[i : i + 1, :] = values[i]
        kept, weight = k_ref[g, x : x + 1, :], w_ref[g, x : x + 1, :]
        for n, i in enumerate(leaving):
            loc_ref[n : n + 1, :] += values[i] * kept
            rim_scr[n : n + 1, :] = values[i] * weight
        weighted = added_ref[...] * weight
        left = iota((1, 128), 1) < 64
        at_row = iota((8, plane), 0) == (0 if is_odd else 7)
        for j in range(3):
            base = item_row[j]
            out_ref = near_ref if j == 0 else lvl_ref
            octant, other = d_ref[6 + j], d_ref[9 + j]
            ox = octant >> 2
            inside = (level == 1) | (ox == 1 - is_odd)

            @pl.when((d_ref[j] == 1) & (d_ref[3 + j] == g) & inside)
            def _(j=j, base=base, out_ref=out_ref, ox=ox, other=other):
                picked = select(weighted, pick_ref[j])
                for n in range(5):
                    a, b, c, d = (picked[m : m + 1] for m in (n, 5 + n, 10 + n, 15 + n))
                    row = jnp.concatenate([jnp.where(left, a, b), jnp.where(left, c, d)], axis=1)
                    tile = slice(base + 8 * n, base + 8 * n + 8)
                    out_ref[tile, :] += jnp.where(at_row, row, 0.0)

                @pl.when((other == 1 - is_odd) & ((level == 0) | (ox == other)))
                def _():
                    first = (mate_d, far_d, own_d)[j]
                    spread = select(rim_scr[...], place_ref[j]) * plane_scale(d_ref)
                    out_ref[first : first + 8, :] += spread

    @pl.when((d_ref[at_odd] == 0) & (d_ref[at_next] == 1))
    def _():
        side(0)

    @pl.when((d_ref[at_odd] == 1) & (d_ref[at_prev] == 1))
    def _():
        side(1)


def last_kernel(d_ref, alpha_in, late_ref, u_ref, keep_ref, gain_ref, alpha_ref):
    alpha_ref[...] = alpha_in[...]

    def side(is_odd):
        g, x = late_layer[is_odd]
        values = late_values(is_odd, late_ref, u_ref, keep_ref, gain_ref)
        for i in range(pops):
            alpha_ref[g, i, x : x + 1, :] += values[i]

    @pl.when((d_ref[at_odd] == 0) & (d_ref[at_next] == 1))
    def _():
        side(0)

    @pl.when((d_ref[at_odd] == 1) & (d_ref[at_prev] == 1))
    def _():
        side(1)


def smem():
    return pl.BlockSpec(memory_space=pltpu.SMEM)


def vmem():
    return pl.BlockSpec(memory_space=pltpu.VMEM)


def shape(*dims, dtype=f32):
    return jax.ShapeDtypeStruct(dims, dtype)


params = pltpu.CompilerParams(vmem_limit_bytes=24 * 1024 * 1024)
half_scratch = [pltpu.VMEM((2, 320, 128), f32)]
pack_scratch = [pltpu.VMEM((160, plane), f32), pltpu.VMEM((8, plane), f32)] + half_scratch
near_shape = shape(mate_rows, plane)
level_shape = shape(level_rows, plane)
ends_shape = shape(16, plane)
field = shape(2, edge, plane)
state = shape(2, pops, edge, plane)


def hbm():
    return pl.BlockSpec(memory_space=pltpu.HBM)


def cost(flops, bytes_accessed):
    return pl.CostEstimate(flops=flops, bytes_accessed=bytes_accessed, transcendentals=0)


def call(kernel, outs, ins, scratch, name, in_specs=None, out_specs=None, estimate=None):
    with jax.named_scope(name):
        return pl.pallas_call(
            kernel,
            out_shape=outs,
            in_specs=in_specs or [smem()] + [vmem()] * (len(ins) - 1),
            out_specs=out_specs or [vmem()] * len(outs),
            scratch_shapes=scratch,
            compiler_params=params,
            cost_estimate=estimate,
        )(*ins)


def local(
    adjoint_final, populations, relaxation, blend, solid, chain, parent, children, *, slabs
):
    steps = populations.shape[0]
    messages = [near_shape, level_shape, ends_shape]
    table, near, lvl, ends, kept, alpha, weights = call(
        first_pack_kernel,
        [shape(table_size, dtype=jnp.int32)] + messages + [field, state, field],
        (chain[0], parent, children, adjoint_final[0], blend[0]),
        pack_scratch
        + [pltpu.SMEM(v.shape, jnp.int32) for v in (chain[0], parent, children)]
        + [pltpu.SemaphoreType.DMA((5,))],
        "pack_first",
        in_specs=[hbm()] * 5,
        out_specs=[smem()] + [vmem()] * 6,
    )
    flows, keep, gain, bits, pick, place = call(
        fields_kernel,
        [
            shape(steps, 2, 3, edge, plane),
            field,
            field,
            shape(2, edge, plane, dtype=jnp.int32),
            shape(3, plane, 128, dtype=bf16),
            shape(3, plane, plane, dtype=bf16),
        ],
        (table, populations[:, 0], relaxation[0], solid[0]),
        [pltpu.VMEM((32, plane), f32)],
        "flow_fields",
        estimate=cost(4_000_000, 2_000_000),
    )
    added = None
    for t in range(steps - 1, -1, -1):
        first, last = t == steps - 1, t == 0
        u = flows[t]
        with jax.named_scope("exchange"):
            lvl = level_swap(lvl, slabs)
            mate = mate_swap(near, slabs, 1)
            extra = ends[8:16] + mate[mate_d : mate_d + 8]
            far = far_swap(lvl[0:56] + jnp.pad(extra, ((own_f, 8), (0, 0))), slabs)
            late = mate_swap(ends[0:8] + lvl[own_d : own_d + 8] + far[far_f : far_f + 8], slabs, 0)
        ins = [table, alpha, kept, u, keep, gain, bits, mate, lvl, far]
        if not first:
            ins += [added]
        if not last:
            ins += [weights, pick, place]
        got = call(
            functools.partial(step_kernel, first=first, last=last),
            [state] + ([] if last else messages),
            ins,
            [pltpu.VMEM((2, pops, 32, plane), f32)] + (half_scratch if last else pack_scratch),
            "step",
            estimate=cost(8_000_000, 2_000_000),
        )
        alpha = got[0]
        if last:
            alpha = call(
                last_kernel, [state], (table, alpha, late, u, keep, gain), (), "finish"
            )[0]
        else:
            added, near, lvl, ends = call(
                finish_kernel,
                [shape(24, plane)] + messages,
                (table, late, u, keep, gain, weights, kept, pick, place, *got[1:]),
                [pltpu.VMEM((8, plane), f32)],
                "finish",
            )
    return alpha[None]


def solution(mesh):
    return jax.shard_map(
        functools.partial(local, slabs=mesh.shape["slab"]),
        mesh=mesh,
        in_specs=(
            P("lvl", "slab", None, None, None),
            P(None, "lvl", "slab", None, None, None),
            P("lvl", "slab", None, None),
            P("lvl", "slab", None, None),
            P("lvl", "slab", None, None),
            P("lvl", "slab", None),
            P("slab", None),
            P("slab", None),
        ),
        out_specs=P("lvl", "slab", None, None, None),
        check_vma=False,
    )
```

```python
import functools

import jax
import jax.numpy as jnp
from jax import lax
from jax.experimental import pallas as pl
from jax.experimental.pallas import tpu as pltpu
from jax.sharding import PartitionSpec as P

velocities = [
    (0, 0, 0),
    (1, 0, 0),
    (-1, 0, 0),
    (0, 1, 0),
    (0, -1, 0),
    (0, 0, 1),
    (0, 0, -1),
    (1, 1, 0),
    (-1, -1, 0),
    (1, -1, 0),
    (-1, 1, 0),
    (1, 0, 1),
    (-1, 0, -1),
    (1, 0, -1),
    (-1, 0, 1),
    (0, 1, 1),
    (0, -1, -1),
    (0, 1, -1),
    (0, -1, 1),
]
east_pops = [1, 7, 9, 11, 13]
west_pops = [2, 8, 10, 12, 14]
opposite = [velocities.index((-c[0], -c[1], -c[2])) for c in velocities]
axes = ("slab", "lvl")
pops, edge, plane = 19, 16, 256
f32, bf16 = jnp.float32, jnp.bfloat16

item_row = (0, 0, 48)
own_f, mate_f, far_d, loc_d, level_rows = 40, 88, 96, 104, 112
loc_f, far_f, own_d, kept_rows = 0, 8, 16, 24
at_parent, at_octant, at_prev, at_next = 8, 9, 10, 11


def level_swap(value, slabs):
    pairs = [(2 * s + v, 2 * s + 1 - v) for s in range(slabs) for v in (0, 1)]
    return lax.ppermute(value, axes, pairs)


def mate_swap(value, slabs, cross):
    pairs = [(2 * s + v, 2 * (s ^ 1) + (v ^ cross)) for s in range(slabs) for v in (0, 1)]
    return lax.ppermute(value, axes, pairs)


def far_swap(value, slabs):
    pairs = []
    for s in range(slabs):
        other = s - 1 if s % 2 == 0 else s + 1
        for v in (0, 1):
            if 0 <= other < slabs:
                pairs.append((2 * s + v, 2 * other + v))
            else:
                pairs.append((2 * s + v, 2 * s + 1 - v))
    return lax.ppermute(value, axes, pairs)


def cell_key(index, level, octant):
    y, z = index >> 4, index & 15
    fine = (y >> 1) * 8 + (z >> 1)
    inside = ((y >> 3) == ((octant >> 1) & 1)) & ((z >> 3) == (octant & 1))
    coarse = jnp.where(inside, (y & 7) * 8 + (z & 7), -1)
    return jnp.where(level == 1, fine, coarse)


def select(values, matrix):
    rows = values.shape[0]
    high = values.astype(bf16).astype(f32)
    halves = jnp.concatenate([high, values - high], axis=0).astype(bf16)
    both = jnp.dot(halves, matrix, preferred_element_type=f32)
    return both[:rows] + both[rows:]


def ones_where(mask):
    return jnp.where(mask, 1.0, 0.0).astype(bf16)


def iota(shape, dim):
    return lax.broadcasted_iota(jnp.int32, shape, dim)


class Table:
    def __init__(self, row):
        codes = [row[0, j] for j in range(3)]
        self.valid = [code >= 0 for code in codes]
        self.block = [(code >> 4) & 1 for code in codes]
        self.octant = [(code >> 1) & 7 for code in codes]
        self.other = [code & 1 for code in codes]
        self.level, self.odd, prev, inner, next_ = (row[0, j] for j in range(3, 8))
        self.prev, self.inner, self.next = prev >= 0, inner >= 0, next_ >= 0


def make_table(tables, slab, level):
    odd = slab & 1
    row, lane = iota(tables.shape, 0), iota(tables.shape, 1)
    octant = jnp.where(level == 0, lane, pltpu.roll(tables, 127, 1))
    here = jnp.where(level == 0, jnp.where(lane < at_parent, 1, 0), jnp.where(lane == at_parent, 1, 0))
    code = row * 16 + octant * 2 + (tables & 1)
    code = jnp.where((here == 1) & (row < 2) & (tables >= 0), code, -1)
    offset = (tables >> 1) - slab
    towards = 1 - 2 * odd
    values = [jnp.max(jnp.where(offset == d, code, -1)) for d in (towards, -towards, 0)]
    values += [level, odd, tables[0, at_prev], tables[0, at_next], tables[1, at_next]]
    out = jnp.zeros(tables.shape, jnp.int32)
    for n, value in enumerate(values):
        out = jnp.where(lane == n, value, out)
    return out


def pick_matrices(t, j):
    level, octant = t.level, t.octant[j]
    source = cell_key(iota((plane, 128), 0), level, octant)
    pick = ones_where(source == (iota((1, 128), 1) & 63))
    target = cell_key(iota((1, plane), 1), 1 - level, octant)
    place = jnp.concatenate(
        [ones_where(source == target[:, :128]), ones_where(source == target[:, 128:])], axis=1
    )
    return pick, place


def plane_scale(t):
    return jnp.where(t.level == 0, 0.125, 1.0)


def pack(t, alpha_ref, w_ref, k_ref, item_ref, side_ref, lvl_ref, ends_ref, scratch, matrices):
    item_scr, rim_scr, half_scr = scratch
    level, odd = t.level, t.odd
    for ref in (item_ref, side_ref, lvl_ref, ends_ref):
        ref[...] = jnp.zeros_like(ref)
    item_scr[152:160, :] = jnp.zeros((8, plane), f32)
    rim_scr[...] = jnp.zeros_like(rim_scr)
    for i in range(5):
        e, w = east_pops[i], west_pops[i]
        low = alpha_ref[e, 0:1, :] * k_ref[0, 0:1, :]
        high = alpha_ref[pops + w, edge - 1 : edge, :] * k_ref[1, edge - 1 : edge, :]
        lvl_ref[loc_d + i : loc_d + i + 1, :] = jnp.where(odd == 1, low, high)
        ends_ref[loc_f + i : loc_f + i + 1, :] = jnp.where(odd == 1, high, low)
    for j in range(3):
        base = item_row[j]
        out_ref = item_ref if j == 0 else lvl_ref

        @pl.when(t.valid[j])
        def _(j=j, base=base, out_ref=out_ref):
            g, octant, other = t.block[j], t.octant[j], t.other[j]
            ox = octant >> 2
            pick, place = matrices(j)

            @pl.when(level == 0)
            def _():
                rows = pl.ds(pl.multiple_of(ox * 8, 8), 8)
                part = alpha_ref[pl.ds(g * pops, pops), rows, :] * w_ref[g, rows, :][None]
                item_scr[0:152, :] = part.reshape(152, plane)

            @pl.when(level == 1)
            def _():
                part = (alpha_ref[pl.ds(g * pops, pops)] * w_ref[g][None]).reshape(304, plane)
                for n in range(2):
                    lanes = slice(128 * n, 128 * n + 128)
                    half_scr[n, 0:304, :] = part[:, lanes]
                    item_scr[0:152, lanes] = (
                        half_scr[n, pl.ds(0, 152, stride=2), :]
                        + half_scr[n, pl.ds(1, 152, stride=2), :]
                    )

            picked = select(item_scr[...], pick)
            left = iota((40, 128), 1) < 64
            out_ref[base : base + 40, 0:128] = jnp.where(left, picked[0:40], picked[40:80])
            out_ref[base : base + 40, 128:256] = jnp.where(left, picked[80:120], picked[120:160])

            @pl.when((level == 0) | (ox == other))
            def _():
                for i in range(5):
                    e, w = east_pops[i] * 8, west_pops[i] * 8 + 7
                    rim_scr[i : i + 1, :] = jnp.where(
                        other == 1, item_scr[w : w + 1, :], item_scr[e : e + 1, :]
                    )
                spread = select(rim_scr[...], place) * plane_scale(t)
                towards_d = other != odd
                to_d = ((side_ref, 0), (lvl_ref, far_d), (ends_ref, own_d))[j]
                to_f = ((lvl_ref, mate_f), (ends_ref, far_f), (lvl_ref, own_f))[j]
                for wanted, (ref, row) in ((towards_d, to_d), (other == odd, to_f)):

                    @pl.when(wanted)
                    def _(ref=ref, row=row):
                        ref[row : row + 8, :] = spread


def first_pack_kernel(*refs):
    tables_ref, alpha_ref, d_ref, item_ref, side_ref, lvl_ref, ends_ref, k_ref = refs[:8]
    scratch = refs[8:]
    w_ref = alpha_ref.at[blend_at : blend_at + 2]
    row = make_table(tables_ref[...], lax.axis_index("slab"), lax.axis_index("lvl"))
    d_ref[...] = row
    t = Table(row)
    level = t.level
    x = iota((edge, plane), 0)
    cell = iota((edge, plane), 1)
    covers = []
    for g in range(2):
        covered = jnp.zeros((edge, plane), jnp.bool_)
        for j in range(3):
            octant = t.octant[j]
            inside = (
                ((x >> 3) == (octant >> 2))
                & ((cell >> 7) == ((octant >> 1) & 1))
                & (((cell >> 3) & 1) == (octant & 1))
            ) | (level == 1)
            covered = covered | (inside & t.valid[j] & (t.block[j] == g))
        covers.append(covered)
    for g in range(2):
        k_ref[g] = jnp.where(covers[g], 1.0 - w_ref[g], 1.0)
    matrices = functools.partial(pick_matrices, t)
    pack(t, alpha_ref, w_ref, k_ref, item_ref, side_ref, lvl_ref, ends_ref, scratch, matrices)


def moved_cells(values, c, z):
    if c[1] == 0 and c[2] == 0:
        return values
    base = -16 * c[1]
    axis = values.ndim - 1
    if c[2] == 0:
        return pltpu.roll(values, base % plane, axis)
    inner = pltpu.roll(values, (base - c[2]) % plane, axis)
    around = pltpu.roll(values, (base + 15 * c[2]) % plane, axis)
    return jnp.where(z == (15 if c[2] == 1 else 0), around, inner)


def fields_kernel(*refs):
    d_ref, pop_ref, relax_ref, solid_ref = refs[:4]
    u_ref, keep_ref, gain_ref, bits_ref, pick_ref, place_ref, pad_scr = refs[4:]
    t = Table(d_ref[...])
    for j in range(3):
        pick_ref[j], place_ref[j] = pick_matrices(t, j)
    z = iota((edge, plane), 1) & 15
    for g in range(2):
        solid = solid_ref[g] > 0
        omega = relax_ref[g]
        keep_ref[g] = jnp.where(solid, 0.0, 1.0 - omega)
        gain_ref[g] = jnp.where(solid, 0.0, omega)
        pad_scr[0:8, :] = jnp.zeros((8, plane), f32)
        pad_scr[24:32, :] = jnp.zeros((8, plane), f32)
        pad_scr[8:24, :] = jnp.where(solid, 1.0, 0.0)
        bits = jnp.zeros((edge, plane), jnp.int32)
        for i in range(pops):
            c = velocities[i]
            blocked = moved_cells(pad_scr[8 + c[0] : 24 + c[0], :], c, z) > 0.5
            bits = bits | jnp.where(blocked, 1 << i, 0)
        bits_ref[g] = bits
    steps = pop_ref.shape[0]
    for t in range(steps):
        for g in range(2):
            total = jnp.zeros((edge, plane), f32)
            flow = [jnp.zeros((edge, plane), f32) for _ in range(3)]
            for i in range(pops):
                f = pop_ref[t, g, i].astype(f32)
                total = total + f
                for a in range(3):
                    if velocities[i][a] == 1:
                        flow[a] = flow[a] + f
                    elif velocities[i][a] == -1:
                        flow[a] = flow[a] - f
            for a in range(3):
                u_ref[t, g, a] = flow[a] / total


def collide(pulled, u, keep, gain):
    g = pulled
    plus = {i: g[i] + g[i + 1] for i in range(1, pops, 2)}
    minus = {i: g[i] - g[i + 1] for i in range(1, pops, 2)}
    xy, xz, yz = plus[7] + plus[9], plus[11] + plus[13], plus[15] + plus[17]
    px, py, pz = 2.0 * plus[1], 2.0 * plus[3], 2.0 * plus[5]
    weight = 12.0 * g[0] + (px + py + pz) + (xy + xz + yz)
    qxx, qyy, qzz = px + xy + xz, py + xy + yz, pz + xz + yz
    qxy, qxz, qyz = plus[7] - plus[9], plus[11] - plus[13], plus[15] - plus[17]
    jx = 2.0 * minus[1] + (minus[7] + minus[9]) + (minus[11] + minus[13])
    jy = 2.0 * minus[3] + (minus[7] - minus[9]) + (minus[15] + minus[17])
    jz = 2.0 * minus[5] + (minus[11] - minus[13]) + (minus[15] - minus[17])
    ux, uy, uz = u
    qux = qxx * ux + qxy * uy + qxz * uz
    quy = qxy * ux + qyy * uy + qyz * uz
    quz = qxz * ux + qyz * uy + qzz * uz
    speed = ux * ux + uy * uy + uz * uz
    along = ux * qux + uy * quy + uz * quz
    scale = gain * (1.0 / 36.0)
    rest = scale * (weight * (1.0 + 1.5 * speed) - 4.5 * along)
    scale = gain * (1.0 / 12.0)
    mx = scale * (jx + 3.0 * qux - ux * weight)
    my = scale * (jy + 3.0 * quy - uy * weight)
    mz = scale * (jz + 3.0 * quz - uz * weight)
    out = [None] * pops
    out[0] = keep * g[0] + rest
    pairs = [mx, my, mz, mx + my, mx - my, mx + mz, mx - mz, my + mz, my - mz]
    for n, i in enumerate(range(1, pops, 2)):
        out[i] = keep * g[i] + (rest + pairs[n])
        out[i + 1] = keep * g[i + 1] + (rest - pairs[n])
    return out


def step_kernel(*refs, first, last):
    (d_ref, alpha_ref, k_ref, u_ref, keep_ref, gain_ref, bits_ref) = refs[:7]
    (mate_ref, lvl_ref, far_ref) = refs[7:10]
    refs = refs[10:]
    if not first:
        added_ref, refs = refs[0], refs[1:]
    if not last:
        (w_ref, pick_ref, place_ref), refs = refs[:3], refs[3:]
        out_ref, *sent, beta_scr, item_scr, rim_scr, half_scr = refs
    else:
        out_ref, beta_scr, half_scr = refs
    t = Table(d_ref[...])
    level, odd = t.level, t.odd
    for g in range(2):
        beta_scr[g, :, 8:24, :] = alpha_ref[g * pops : (g + 1) * pops] * k_ref[g][None]
    if not first:
        for is_odd, (g, x) in enumerate(late_layer):

            @pl.when(odd == is_odd)
            def _(g=g, x=x):
                kept = k_ref[g, x : x + 1, :]
                for i in range(pops):
                    beta_scr[g, i, 8 + x : 9 + x, :] += added_ref[i : i + 1, :] * kept

    sources = (mate_ref, far_ref, lvl_ref)
    for j in range(3):
        first = item_row[j]

        @pl.when(t.valid[j])
        def _(j=j, first=first):
            g, octant = t.block[j], t.octant[j]
            left = iota((40, 128), 1) < 64
            a = sources[j][first : first + 40, 0:128]
            b = sources[j][first : first + 40, 128:256]
            stacked = jnp.concatenate(
                [
                    jnp.where(left, a, 0.0),
                    jnp.where(left, 0.0, a),
                    jnp.where(left, b, 0.0),
                    jnp.where(left, 0.0, b),
                ],
                axis=0,
            )
            target = cell_key(iota((1, plane), 1), level, octant)
            spread = select(stacked, ones_where((iota((128, plane), 0) & 63) == target))

            @pl.when(level == 0)
            def _():
                rows = pl.ds(pl.multiple_of(8 + (octant >> 2) * 8, 8), 8)
                beta_scr[g, :, rows, :] += spread[0:152].reshape(pops, 8, plane)

            @pl.when(level == 1)
            def _():
                for n in range(2):
                    lanes = slice(128 * n, 128 * n + 128)
                    half = spread[:, lanes] * 0.125
                    half_scr[n, pl.ds(0, 160, stride=2), :] = half
                    half_scr[n, pl.ds(1, 160, stride=2), :] = half
                    both = half_scr[n, 0:304, :].reshape(pops, edge, 128)
                    beta_scr[g, :, 8:24, lanes] += both

    from_d = lvl_ref[mate_f : mate_f + 8, :]
    from_f = far_ref[40:48, :] + lvl_ref[far_d : far_d + 8, :]
    above = jnp.where(odd == 1, from_f, from_d)
    below = jnp.where(odd == 1, from_d, from_f)
    above = jnp.where(t.next, above, 0.0)
    below = jnp.where(t.prev, below, 0.0)
    inner = t.inner
    for i in range(5):
        e, w = east_pops[i], west_pops[i]
        beta_scr[1, e, 24:25, :] = above[i : i + 1]
        beta_scr[0, w, 7:8, :] = below[i : i + 1]
        beta_scr[0, e, 24:25, :] = jnp.where(inner, beta_scr[1, e, 8:9, :], 0.0)
        beta_scr[1, w, 7:8, :] = jnp.where(inner, beta_scr[0, w, 23:24, :], 0.0)
    z = iota((8, plane), 1) & 15
    for g in range(2):
        for h in range(2):
            rows = slice(8 * h, 8 * h + 8)
            first = 8 + 8 * h
            bits = bits_ref[g, rows, :]
            pulled = []
            for i in range(pops):
                c = velocities[i]
                v = beta_scr[g, i, first + c[0] : first + c[0] + 8, :]
                v = moved_cells(v, c, z)
                back = beta_scr[g, opposite[i], first : first + 8, :]
                pulled.append(jnp.where((bits & (1 << i)) != 0, back, v))
            u = [u_ref[g, a, rows, :] for a in range(3)]
            done = collide(pulled, u, keep_ref[g, rows, :], gain_ref[g, rows, :])
            for i in range(pops):
                out_ref[g * pops + i, rows, :] = done[i]
    if not last:
        scratch = (item_scr, rim_scr, half_scr)
        matrices = lambda j: (pick_ref[j], place_ref[j])
        pack(t, out_ref, w_ref, k_ref, *sent, scratch, matrices)


late_layer = ((1, edge - 1), (0, 0))


def late_values(is_odd, late_ref, u_ref, keep_ref, gain_ref):
    g, x = late_layer[is_odd]
    z = iota((8, plane), 1) & 15
    late = late_ref[...]
    pulled = [0.0] * pops
    for n, i in enumerate((east_pops, west_pops)[is_odd]):
        pulled[i] = moved_cells(late, velocities[i], z)[n : n + 1]
    rows = slice(x, x + 1)
    u = [u_ref[g, a, rows, :] for a in range(3)]
    return collide(pulled, u, keep_ref[g, rows, :], gain_ref[g, rows, :])


def finish_kernel(*refs):
    (d_ref, late_ref, u_ref, keep_ref, gain_ref, w_ref, k_ref, pick_ref, place_ref) = refs[:9]
    given, added_ref, sent, rim_scr = refs[9:13], refs[13], refs[14:18], refs[18]
    item_ref, side_ref, lvl_ref, ends_ref = sent
    t = Table(d_ref[...])
    for source, ref in zip(given, sent):
        ref[...] = source[...]
    added_ref[...] = jnp.zeros_like(added_ref)
    rim_scr[...] = jnp.zeros_like(rim_scr)

    def side(is_odd):
        g, x = late_layer[is_odd]
        leaving = (west_pops, east_pops)[is_odd]
        values = late_values(is_odd, late_ref, u_ref, keep_ref, gain_ref)
        for i in range(pops):
            added_ref[i : i + 1, :] = values[i]
        kept, weight = k_ref[g, x : x + 1, :], w_ref[g, x : x + 1, :]
        for n, i in enumerate(leaving):
            lvl_ref[loc_d + n : loc_d + n + 1, :] += values[i] * kept
            rim_scr[n : n + 1, :] = values[i] * weight
        weighted = added_ref[...] * weight
        left = iota((1, 128), 1) < 64
        at_row = iota((8, plane), 0) == (0 if is_odd else 7)
        for j in range(3):
            base = item_row[j]
            out_ref = item_ref if j == 0 else lvl_ref
            other, ox = t.other[j], t.octant[j] >> 2
            inside = (t.level == 1) | (ox == 1 - is_odd)

            @pl.when(t.valid[j] & (t.block[j] == g) & inside)
            def _(j=j, base=base, out_ref=out_ref, ox=ox, other=other):
                picked = select(weighted, pick_ref[j])
                for n in range(5):
                    a, b, c, d = (picked[m : m + 1] for m in (n, 5 + n, 10 + n, 15 + n))
                    row = jnp.concatenate([jnp.where(left, a, b), jnp.where(left, c, d)], axis=1)
                    tile = slice(base + 8 * n, base + 8 * n + 8)
                    out_ref[tile, :] += jnp.where(at_row, row, 0.0)

                @pl.when((other == 1 - is_odd) & ((t.level == 0) | (ox == other)))
                def _():
                    spread = select(rim_scr[...], place_ref[j]) * plane_scale(t)
                    ref, row = ((side_ref, 0), (lvl_ref, far_d), (ends_ref, own_d))[j]
                    ref[row : row + 8, :] += spread

    @pl.when((t.odd == 0) & t.next)
    def _():
        side(0)

    @pl.when((t.odd == 1) & t.prev)
    def _():
        side(1)


def last_kernel(d_ref, alpha_ref, late_ref, u_ref, keep_ref, gain_ref, out_ref, tile_scr, sems):
    def tile(source, g, x, sem):
        block, rows = pl.ds(g * pops, pops), pl.ds(x, 8)
        source = source.at[block, rows] if source is alpha_ref else source
        return pltpu.make_async_copy(source, out_ref.at[block, rows], sems.at[sem])

    copies = [tile(alpha_ref, 0, 8, 0), tile(alpha_ref, 1, 0, 1)]
    for copy in copies:
        copy.start()
    t = Table(d_ref[...])
    odd = t.odd
    copies.append(tile(alpha_ref, odd, pl.multiple_of(8 * odd, 8), 2))
    copies[2].start()
    reached = pl.multiple_of(8 - 8 * odd, 8)
    tile_scr[...] = alpha_ref[pl.ds((1 - odd) * pops, pops), pl.ds(reached, 8), :]

    def side(is_odd):
        values = late_values(is_odd, late_ref, u_ref, keep_ref, gain_ref)
        x = late_layer[is_odd][1] % 8
        for i in range(pops):
            tile_scr[i, x : x + 1, :] += values[i]

    @pl.when((odd == 0) & t.next)
    def _():
        side(0)

    @pl.when((odd == 1) & t.prev)
    def _():
        side(1)

    copies.append(tile(tile_scr, 1 - odd, reached, 3))
    copies[3].start()
    for copy in copies:
        copy.wait()


def vmem():
    return pl.BlockSpec(memory_space=pltpu.VMEM)


def shape(*dims, dtype=f32):
    return jax.ShapeDtypeStruct(dims, dtype)


params = pltpu.CompilerParams(vmem_limit_bytes=24 * 1024 * 1024)
half_scratch = [pltpu.VMEM((2, 320, 128), f32)]
pack_scratch = [pltpu.VMEM((160, plane), f32), pltpu.VMEM((8, plane), f32)] + half_scratch
messages = [shape(rows, plane) for rows in (40, 8, level_rows, kept_rows)]
field = shape(2, edge, plane)
state = shape(2 * pops, edge, plane)
blend_at = 2 * pops


def hbm():
    return pl.BlockSpec(memory_space=pltpu.HBM)


def cost(flops, bytes_accessed):
    return pl.CostEstimate(flops=flops, bytes_accessed=bytes_accessed, transcendentals=0)


def call(kernel, outs, ins, scratch, name, out_specs=None, estimate=None):
    with jax.named_scope(name):
        return pl.pallas_call(
            kernel,
            out_shape=outs,
            in_specs=[vmem()] * len(ins),
            out_specs=out_specs or [vmem()] * len(outs),
            scratch_shapes=scratch,
            compiler_params=params,
            cost_estimate=estimate,
        )(*ins)


def local(
    adjoint_final, populations, relaxation, blend, solid, chain, parent, children, *, slabs
):
    steps = populations.shape[0]
    alpha = jnp.concatenate([adjoint_final.reshape(2 * pops, edge, plane), blend[0]], axis=0)
    tables = jnp.concatenate([children, parent, chain[0]], axis=1)
    tables = jnp.pad(tables, ((0, 6), (0, 116)), constant_values=-1)
    table, *sent, kept = call(
        first_pack_kernel,
        [shape(8, 128, dtype=jnp.int32)] + messages + [field],
        (tables, alpha),
        pack_scratch,
        "pack_first",
    )
    weights = alpha[blend_at:]
    flows, keep, gain, bits, pick, place = call(
        fields_kernel,
        [
            shape(steps, 2, 3, edge, plane),
            field,
            field,
            shape(2, edge, plane, dtype=jnp.int32),
            shape(3, plane, 128, dtype=bf16),
            shape(3, plane, plane, dtype=bf16),
        ],
        (table, populations[:, 0], relaxation[0], solid[0]),
        [pltpu.VMEM((32, plane), f32)],
        "flow_fields",
        estimate=cost(4_000_000, 2_000_000),
    )
    added = None
    for t in range(steps - 1, -1, -1):
        first, last = t == steps - 1, t == 0
        u = flows[t]
        near, side, lvl, ends = sent
        with jax.named_scope("exchange"):
            lvl = level_swap(lvl, slabs)
            side = mate_swap(side, slabs, 1)
            end = lvl[own_f : own_f + 8] + ends[loc_f : loc_f + 8] + side
            far = jnp.concatenate([lvl[0:40], end, ends[far_f : far_f + 8]], axis=0)
            far = far_swap(far, slabs)
            mate = mate_swap(near, slabs, 1)
            end = lvl[loc_d : loc_d + 8] + ends[own_d : own_d + 8] + far[48:56]
            late = mate_swap(end, slabs, 1)
        ins = [table, alpha, kept, u, keep, gain, bits, mate, lvl, far]
        if not first:
            ins += [added]
        if not last:
            ins += [weights, pick, place]
        got = call(
            functools.partial(step_kernel, first=first, last=last),
            [state] + ([] if last else messages),
            ins,
            [pltpu.VMEM((2, pops, 32, plane), f32)] + (half_scratch if last else pack_scratch),
            "step",
            estimate=cost(8_000_000, 2_000_000),
        )
        alpha = got[0]
        if last:
            alpha = call(
                last_kernel,
                [state],
                (table, alpha, late, u, keep, gain),
                [pltpu.VMEM((pops, 8, plane), f32), pltpu.SemaphoreType.DMA((4,))],
                "finish",
                out_specs=[hbm()],
            )[0]
        else:
            added, *sent = call(
                finish_kernel,
                [shape(24, plane)] + messages,
                (table, late, u, keep, gain, weights, kept, pick, place, *got[1:]),
                [pltpu.VMEM((8, plane), f32)],
                "finish",
            )
    return alpha.reshape(1, 2, pops, edge, plane)


def solution(mesh):
    return jax.shard_map(
        functools.partial(local, slabs=mesh.shape["slab"]),
        mesh=mesh,
        in_specs=(
            P("lvl", "slab", None, None, None),
            P(None, "lvl", "slab", None, None, None),
            P("lvl", "slab", None, None),
            P("lvl", "slab", None, None),
            P("lvl", "slab", None, None),
            P("lvl", "slab", None),
            P("slab", None),
            P("slab", None),
        ),
        out_specs=P("lvl", "slab", None, None, None),
        check_vma=False,
    )
```

```python
import functools

import jax
import jax.numpy as jnp
from jax import lax
from jax.experimental import pallas as pl
from jax.experimental.pallas import tpu as pltpu
from jax.sharding import PartitionSpec as P

velocities = [
    (0, 0, 0),
    (1, 0, 0),
    (-1, 0, 0),
    (0, 1, 0),
    (0, -1, 0),
    (0, 0, 1),
    (0, 0, -1),
    (1, 1, 0),
    (-1, -1, 0),
    (1, -1, 0),
    (-1, 1, 0),
    (1, 0, 1),
    (-1, 0, -1),
    (1, 0, -1),
    (-1, 0, 1),
    (0, 1, 1),
    (0, -1, -1),
    (0, 1, -1),
    (0, -1, 1),
]
east_pops = [1, 7, 9, 11, 13]
west_pops = [2, 8, 10, 12, 14]
opposite = [velocities.index((-c[0], -c[1], -c[2])) for c in velocities]
axes = ("slab", "lvl")
pops, edge, plane = 19, 16, 256
f32, bf16 = jnp.float32, jnp.bfloat16

item_row = (0, 0, 56)
own_f, far_f, mate_f, far_d, loc_d, own_d, level_rows = 40, 48, 96, 104, 112, 120, 128
kept_loc_f, kept_far_f, kept_own_d, kept_loc_d, kept_rows = 0, 8, 16, 24, 32
rest_at, rest_rows = 56, 72
rest_mate_f, rest_far_d, rest_loc_d, rest_own_d = 40, 48, 56, 64


at_parent, at_octant, at_prev, at_next = 8, 9, 10, 11


def level_swap(value, slabs):
    pairs = [(2 * s + v, 2 * s + 1 - v) for s in range(slabs) for v in (0, 1)]
    return lax.ppermute(value, axes, pairs)


def mate_swap(value, slabs, cross):
    pairs = [(2 * s + v, 2 * (s ^ 1) + (v ^ cross)) for s in range(slabs) for v in (0, 1)]
    return lax.ppermute(value, axes, pairs)


def far_swap(value, slabs):
    pairs = []
    for s in range(slabs):
        other = s - 1 if s % 2 == 0 else s + 1
        for v in (0, 1):
            if 0 <= other < slabs:
                pairs.append((2 * s + v, 2 * other + v))
            else:
                pairs.append((2 * s + v, 2 * s + 1 - v))
    return lax.ppermute(value, axes, pairs)


def cell_key(index, level, octant):
    y, z = index >> 4, index & 15
    fine = (y >> 1) * 8 + (z >> 1)
    inside = ((y >> 3) == ((octant >> 1) & 1)) & ((z >> 3) == (octant & 1))
    coarse = jnp.where(inside, (y & 7) * 8 + (z & 7), -1)
    return jnp.where(level == 1, fine, coarse)


def select(values, matrix):
    rows = values.shape[0]
    high = values.astype(bf16).astype(f32)
    halves = jnp.concatenate([high, values - high], axis=0).astype(bf16)
    both = jnp.dot(halves, matrix, preferred_element_type=f32)
    return both[:rows] + both[rows:]


def ones_where(mask):
    return jnp.where(mask, 1.0, 0.0).astype(bf16)


def iota(shape, dim):
    return lax.broadcasted_iota(jnp.int32, shape, dim)


class Table:
    def __init__(self, row):
        codes = [row[0, j] for j in range(3)]
        self.pair_codes = [row[0, j] for j in range(8, 11)]
        self.valid = [code >= 0 for code in codes]
        self.block = [(code >> 4) & 1 for code in codes]
        self.octant = [(code >> 1) & 7 for code in codes]
        self.other = [code & 1 for code in codes]
        self.level, self.odd, prev, inner, next_ = (row[0, j] for j in range(3, 8))
        self.prev, self.inner, self.next = prev >= 0, inner >= 0, next_ >= 0


def make_table(tables, slab, level):
    odd = slab & 1
    row, lane = iota(tables.shape, 0), iota(tables.shape, 1)
    towards = 1 - 2 * odd

    def codes(of_level):
        octant = jnp.where(of_level == 0, lane, pltpu.roll(tables, 127, 1))
        coarse, fine = jnp.where(lane < at_parent, 1, 0), jnp.where(lane == at_parent, 1, 0)
        here = jnp.where(of_level == 0, coarse, fine)
        code = row * 16 + octant * 2 + (tables & 1)
        code = jnp.where((here == 1) & (row < 2) & (tables >= 0), code, -1)
        offset = (tables >> 1) - slab
        return [jnp.max(jnp.where(offset == d, code, -1)) for d in (towards, -towards, 0)]

    values = codes(level)
    values += [level, odd, tables[0, at_prev], tables[0, at_next], tables[1, at_next]]
    values += codes(1 - level)
    out = jnp.zeros(tables.shape, jnp.int32)
    for n, value in enumerate(values):
        out = jnp.where(lane == n, value, out)
    return out


def pick_matrices(t, j):
    return coupling_matrices(t.level, t.octant[j])


def coupling_matrices(level, octant):
    y0, z0 = ((octant >> 1) & 1) * 8, (octant & 1) * 8

    def own_cell(y, z):
        return jnp.where(level == 0, ((y0 + y) << 4) | (z0 + z), (y << 5) | (z << 1))

    cell = iota((plane, 128), 0) & jnp.where(level == 0, 255, 238)
    item = iota((1, 128), 1) & 63
    pick = ones_where(cell == own_cell(item >> 3, item & 7))
    there = iota((1, plane), 1)
    y, z = there >> 4, there & 15
    inside = ((y & 8) == y0) & ((z & 8) == z0)
    to_fine = own_cell(y >> 1, z >> 1)
    to_coarse = jnp.where(inside, own_cell(y & 7, z & 7), -1)
    target = jnp.where(level == 0, to_fine, to_coarse)
    place = jnp.concatenate(
        [ones_where(cell == target[:, :128]), ones_where(cell == target[:, 128:])], axis=1
    )
    return pick, place


def plane_scale(t):
    return jnp.where(t.level == 0, 0.125, 1.0)


def pack(t, alpha_ref, w_ref, k_ref, item_ref, side_ref, lvl_ref, ends_ref, scratch, matrices):
    item_scr, rim_scr, half_scr = scratch
    level, odd = t.level, t.odd
    for ref in (item_ref, side_ref, lvl_ref, ends_ref):
        ref[...] = jnp.zeros_like(ref)
    item_scr[152:160, :] = jnp.zeros((8, plane), f32)
    rim_scr[...] = jnp.zeros_like(rim_scr)
    for i in range(5):
        e, w = east_pops[i], west_pops[i]
        low = alpha_ref[e, 0:1, :] * k_ref[0, 0:1, :]
        high = alpha_ref[pops + w, edge - 1 : edge, :] * k_ref[1, edge - 1 : edge, :]
        lvl_ref[loc_d + i : loc_d + i + 1, :] = jnp.where(odd == 1, low, high)
        ends_ref[kept_loc_f + i : kept_loc_f + i + 1, :] = jnp.where(odd == 1, high, low)
    for j in range(3):
        base = item_row[j]
        out_ref = item_ref if j == 0 else lvl_ref

        @pl.when(t.valid[j])
        def _(j=j, base=base, out_ref=out_ref):
            g, octant, other = t.block[j], t.octant[j], t.other[j]
            ox = octant >> 2
            pick, place = matrices(j)

            @pl.when(level == 0)
            def _():
                rows = pl.ds(pl.multiple_of(ox * 8, 8), 8)
                part = alpha_ref[pl.ds(g * pops, pops), rows, :] * w_ref[g, rows, :][None]
                item_scr[0:152, :] = part.reshape(152, plane)

            @pl.when(level == 1)
            def _():
                part = (alpha_ref[pl.ds(g * pops, pops)] * w_ref[g][None]).reshape(304, plane)
                for n in range(2):
                    lanes = slice(128 * n, 128 * n + 128)
                    half_scr[n, 0:304, :] = part[:, lanes]
                    item_scr[0:152, lanes] = (
                        half_scr[n, pl.ds(0, 152, stride=2), :]
                        + half_scr[n, pl.ds(1, 152, stride=2), :]
                    )

            picked = select(item_scr[...], pick)
            left = iota((40, 128), 1) < 64
            out_ref[base : base + 40, 0:128] = jnp.where(left, picked[0:40], picked[40:80])
            out_ref[base : base + 40, 128:256] = jnp.where(left, picked[80:120], picked[120:160])

            @pl.when((level == 0) | (ox == other))
            def _():
                for i in range(5):
                    e, w = east_pops[i] * 8, west_pops[i] * 8 + 7
                    rim_scr[i : i + 1, :] = jnp.where(
                        other == 1, item_scr[w : w + 1, :], item_scr[e : e + 1, :]
                    )
                spread = select(rim_scr[...], place) * plane_scale(t)
                towards_d = other != odd
                to_d = ((side_ref, 0), (lvl_ref, far_d), (lvl_ref, own_d))[j]
                to_f = ((lvl_ref, mate_f), (lvl_ref, far_f), (lvl_ref, own_f))[j]
                for wanted, (ref, row) in ((towards_d, to_d), (other == odd, to_f)):

                    @pl.when(wanted)
                    def _(ref=ref, row=row):
                        ref[row : row + 8, :] = spread

    for row, kept in ((far_f, kept_far_f), (own_d, kept_own_d), (loc_d, kept_loc_d)):
        ends_ref[kept : kept + 8, :] = lvl_ref[row : row + 8, :]


def first_pack_kernel(*refs):
    alpha_ref, d_ref, item_ref, side_ref, lvl_ref, ends_ref, k_ref = refs[:7]
    scratch = refs[7:]
    w_ref = alpha_ref.at[blend_at : blend_at + 2]
    tables = alpha_ref[tables_at, 0:8, 0:128].astype(jnp.int32)
    row = make_table(tables, lax.axis_index("slab"), lax.axis_index("lvl"))
    d_ref[...] = row
    t = Table(row)
    level = t.level
    x = iota((edge, plane), 0)
    cell = iota((edge, plane), 1)
    covers = []
    for g in range(2):
        covered = jnp.zeros((edge, plane), jnp.bool_)
        for j in range(3):
            octant = t.octant[j]
            inside = (
                ((x >> 3) == (octant >> 2))
                & ((cell >> 7) == ((octant >> 1) & 1))
                & (((cell >> 3) & 1) == (octant & 1))
            ) | (level == 1)
            covered = covered | (inside & t.valid[j] & (t.block[j] == g))
        covers.append(covered)
    for g in range(2):
        k_ref[g] = jnp.where(covers[g], 1.0 - w_ref[g], 1.0)
    matrices = functools.partial(pick_matrices, t)
    pack(t, alpha_ref, w_ref, k_ref, item_ref, side_ref, lvl_ref, ends_ref, scratch, matrices)


def moved_cells(values, c, z):
    if c[1] == 0 and c[2] == 0:
        return values
    base = -16 * c[1]
    axis = values.ndim - 1
    if c[2] == 0:
        return pltpu.roll(values, base % plane, axis)
    inner = pltpu.roll(values, (base - c[2]) % plane, axis)
    around = pltpu.roll(values, (base + 15 * c[2]) % plane, axis)
    return jnp.where(z == (15 if c[2] == 1 else 0), around, inner)


def fields_kernel(*refs):
    d_ref, pop_ref, relax_ref, solid_ref, w_ref, k_ref = refs[:6]
    u_ref, keep_ref, gain_ref, bits_ref, pick_ref, place_ref = refs[6:12]
    late_ref, fix_pick_ref, fix_place_ref, pad_scr = refs[12:]
    t = Table(d_ref[...])
    for j in range(3):
        pick_ref[j], place_ref[j] = pick_matrices(t, j)

    def fixes(level, odd, valid, block, octant, other):
        pick, place = coupling_matrices(level, octant)
        ox, side = octant >> 2, 1 - odd
        item = valid & (block == side) & ((level == 1) | (ox == side))
        end = item & (other == side) & ((level == 0) | (ox == other))
        scale = jnp.where(level == 0, 0.125, 1.0)
        pick = (pick.astype(f32) * jnp.where(item, 1.0, 0.0)).astype(bf16)
        place = (place.astype(f32) * jnp.where(end, scale, 0.0)).astype(bf16)
        return pick, place

    def of_code(code, level):
        return fixes(level, t.odd, code >= 0, (code >> 4) & 1, (code >> 1) & 7, code & 1)

    pair = 1 - t.level
    fix_pick_ref[0], fix_place_ref[0] = of_code(t.pair_codes[1], pair)
    fix_pick_ref[1], fix_place_ref[1] = of_code(t.pair_codes[2], pair)
    fix_pick_ref[2], fix_place_ref[2] = fixes(
        pair, 1 - t.odd, t.valid[0], t.other[0], t.octant[0], t.block[0]
    )
    fix_place_ref[3] = fixes(t.level, t.odd, t.valid[2], t.block[2], t.octant[2], t.other[2])[1]
    z = iota((edge, plane), 1) & 15
    for g in range(2):
        solid = solid_ref[g] > 0
        omega = relax_ref[g]
        keep_ref[g] = jnp.where(solid, 0.0, 1.0 - omega)
        gain_ref[g] = jnp.where(solid, 0.0, omega)
        pad_scr[0:8, :] = jnp.zeros((8, plane), f32)
        pad_scr[24:32, :] = jnp.zeros((8, plane), f32)
        pad_scr[8:24, :] = jnp.where(solid, 1.0, 0.0)
        bits = jnp.zeros((edge, plane), jnp.int32)
        for i in range(pops):
            c = velocities[i]
            blocked = moved_cells(pad_scr[8 + c[0] : 24 + c[0], :], c, z) > 0.5
            bits = bits | jnp.where(blocked, 1 << i, 0)
        bits_ref[g] = bits
    steps = pop_ref.shape[0]
    for n in range(steps):
        for g in range(2):
            total = jnp.zeros((edge, plane), f32)
            flow = [jnp.zeros((edge, plane), f32) for _ in range(3)]
            for i in range(pops):
                f = pop_ref[n, g, i].astype(f32)
                total = total + f
                for a in range(3):
                    if velocities[i][a] == 1:
                        flow[a] = flow[a] + f
                    elif velocities[i][a] == -1:
                        flow[a] = flow[a] - f
            for a in range(3):
                u_ref[n, g, a] = flow[a] / total
    for is_odd, (g, x) in enumerate(late_layer):

        @pl.when(t.odd == is_odd)
        def _(is_odd=is_odd, g=g, x=x):
            link = jnp.where(t.prev if is_odd else t.next, 1.0, 0.0)
            rows = [u_ref[n, g, a, x : x + 1, :] for n in range(steps) for a in range(3)]
            rows += [keep_ref[g, x : x + 1, :] * link, gain_ref[g, x : x + 1, :] * link]
            rows += [w_ref[g, x : x + 1, :], k_ref[g, x : x + 1, :]]
            for n, row in enumerate(rows):
                late_ref[n : n + 1, :] = row


def collide(pulled, u, keep, gain):
    g = pulled
    plus = {i: g[i] + g[i + 1] for i in range(1, pops, 2)}
    minus = {i: g[i] - g[i + 1] for i in range(1, pops, 2)}
    xy, xz, yz = plus[7] + plus[9], plus[11] + plus[13], plus[15] + plus[17]
    px, py, pz = 2.0 * plus[1], 2.0 * plus[3], 2.0 * plus[5]
    weight = 12.0 * g[0] + (px + py + pz) + (xy + xz + yz)
    qxx, qyy, qzz = px + xy + xz, py + xy + yz, pz + xz + yz
    qxy, qxz, qyz = plus[7] - plus[9], plus[11] - plus[13], plus[15] - plus[17]
    jx = 2.0 * minus[1] + (minus[7] + minus[9]) + (minus[11] + minus[13])
    jy = 2.0 * minus[3] + (minus[7] - minus[9]) + (minus[15] + minus[17])
    jz = 2.0 * minus[5] + (minus[11] - minus[13]) + (minus[15] - minus[17])
    ux, uy, uz = u
    qux = qxx * ux + qxy * uy + qxz * uz
    quy = qxy * ux + qyy * uy + qyz * uz
    quz = qxz * ux + qyz * uy + qzz * uz
    speed = ux * ux + uy * uy + uz * uz
    along = ux * qux + uy * quy + uz * quz
    scale = gain * (1.0 / 36.0)
    rest = scale * (weight * (1.0 + 1.5 * speed) - 4.5 * along)
    scale = gain * (1.0 / 12.0)
    mx = scale * (jx + 3.0 * qux - ux * weight)
    my = scale * (jy + 3.0 * quy - uy * weight)
    mz = scale * (jz + 3.0 * quz - uz * weight)
    out = [None] * pops
    out[0] = keep * g[0] + rest
    pairs = [mx, my, mz, mx + my, mx - my, mx + mz, mx - mz, my + mz, my - mz]
    for n, i in enumerate(range(1, pops, 2)):
        out[i] = keep * g[i] + (rest + pairs[n])
        out[i + 1] = keep * g[i + 1] + (rest - pairs[n])
    return out


def add_item(t, j, item, half_scr, add):
    level, g, octant = t.level, t.block[j], t.octant[j]
    left = iota((40, 128), 1) < 64
    a, b = item[:, 0:128], item[:, 128:256]
    parts = [(a, left), (a, ~left), (b, left), (b, ~left)]
    stacked = jnp.concatenate([jnp.where(m, v, 0.0) for v, m in parts], axis=0)
    high = stacked.astype(bf16).astype(f32)
    halves = jnp.concatenate([high, stacked - high], axis=1).astype(bf16)
    target = cell_key(iota((1, plane), 1), level, octant)
    matrix = ones_where((iota((plane, plane), 0) & 63) == target)
    spread = jnp.dot(halves, matrix, preferred_element_type=f32)

    @pl.when(level == 0)
    def _():
        first = pl.multiple_of((octant >> 2) * 8, 8)
        add(g, first, 8, slice(0, plane), spread[0:152].reshape(pops, 8, plane))

    @pl.when(level == 1)
    def _():
        for n in range(2):
            lanes = slice(128 * n, 128 * n + 128)
            half = spread[:, lanes] * 0.125
            half_scr[n, pl.ds(0, 160, stride=2), :] = half
            half_scr[n, pl.ds(1, 160, stride=2), :] = half
            both = half_scr[n, 0:304, :].reshape(pops, edge, 128)
            add(g, 0, edge, lanes, both)


def before_kernel(*refs, first):
    (d_ref, alpha_ref, k_ref, mate_ref, rest_ref) = refs[:5]
    refs = refs[5:]
    if not first:
        (added_ref, fix_ref), refs = refs[:2], refs[2:]
    out_ref, half_scr = refs
    t = Table(d_ref[...])
    for g in range(2):
        block = slice(g * pops, (g + 1) * pops)
        out_ref[block] = alpha_ref[block] * k_ref[g][None]
    if not first:
        for is_odd, (g, x) in enumerate(late_layer):

            @pl.when(t.odd == is_odd)
            def _(g=g, x=x):
                kept = k_ref[g, x : x + 1, :]
                for i in range(pops):
                    out_ref[g * pops + i, x : x + 1, :] += added_ref[i : i + 1, :] * kept

    def add(g, start, layers, lanes, values):
        out_ref[pl.ds(g * pops, pops), pl.ds(start, layers), lanes] += values

    @pl.when(t.valid[0])
    def _():
        item = mate_ref[...] if first else mate_ref[...] + fix_ref[...]
        add_item(t, 0, item, half_scr, add)

    @pl.when(t.valid[2])
    def _():
        add_item(t, 2, rest_ref[0:40, :], half_scr, add)


def step_kernel(*refs, last):
    (d_ref, before_ref, k_ref, u_ref, keep_ref, gain_ref, bits_ref, lvl_ref, far_ref) = refs[:9]
    refs = refs[9:]
    if not last:
        (w_ref, pick_ref, place_ref), refs = refs[:3], refs[3:]
        out_ref, *sent, beta_scr, item_scr, rim_scr, half_scr = refs
    else:
        out_ref, beta_scr, half_scr = refs
    t = Table(d_ref[...])
    level, odd = t.level, t.odd
    for g in range(2):
        beta_scr[g, :, 8:24, :] = before_ref[g * pops : (g + 1) * pops]

    def add(g, start, layers, lanes, values):
        beta_scr[g, :, pl.ds(8 + start, layers), lanes] += values

    @pl.when(t.valid[1])
    def _():
        add_item(t, 1, far_ref[0:40, :], half_scr, add)

    from_d = lvl_ref[rest_mate_f : rest_mate_f + 8, :]
    from_f = far_ref[40:48, :] + lvl_ref[rest_far_d : rest_far_d + 8, :]
    above = jnp.where(odd == 1, from_f, from_d)
    below = jnp.where(odd == 1, from_d, from_f)
    above = jnp.where(t.next, above, 0.0)
    below = jnp.where(t.prev, below, 0.0)
    inner = t.inner
    for i in range(5):
        e, w = east_pops[i], west_pops[i]
        beta_scr[1, e, 24:25, :] = above[i : i + 1]
        beta_scr[0, w, 7:8, :] = below[i : i + 1]
        beta_scr[0, e, 24:25, :] = jnp.where(inner, beta_scr[1, e, 8:9, :], 0.0)
        beta_scr[1, w, 7:8, :] = jnp.where(inner, beta_scr[0, w, 23:24, :], 0.0)
    z = iota((8, plane), 1) & 15
    for g in range(2):
        for h in range(2):
            rows = slice(8 * h, 8 * h + 8)
            first = 8 + 8 * h
            bits = bits_ref[g, rows, :]
            pulled = []
            for i in range(pops):
                c = velocities[i]
                v = beta_scr[g, i, first + c[0] : first + c[0] + 8, :]
                v = moved_cells(v, c, z)
                back = beta_scr[g, opposite[i], first : first + 8, :]
                pulled.append(jnp.where((bits & (1 << i)) != 0, back, v))
            u = [u_ref[g, a, rows, :] for a in range(3)]
            done = collide(pulled, u, keep_ref[g, rows, :], gain_ref[g, rows, :])
            for i in range(pops):
                out_ref[g * pops + i, rows, :] = done[i]
    if not last:
        scratch = (item_scr, rim_scr, half_scr)
        matrices = lambda j: (pick_ref[j], place_ref[j])
        pack(t, out_ref, w_ref, k_ref, *sent, scratch, matrices)


late_layer = ((1, edge - 1), (0, 0))


def late_values(is_odd, late_ref, u_ref, keep_ref, gain_ref):
    g, x = late_layer[is_odd]
    z = iota((8, plane), 1) & 15
    late = late_ref[...]
    pulled = [0.0] * pops
    for n, i in enumerate((east_pops, west_pops)[is_odd]):
        pulled[i] = moved_cells(late, velocities[i], z)[n : n + 1]
    rows = slice(x, x + 1)
    u = [u_ref[g, a, rows, :] for a in range(3)]
    return collide(pulled, u, keep_ref[g, rows, :], gain_ref[g, rows, :])


def late_share(late, fields, step, odd):
    z = iota((8, plane), 1) & 15
    pulled = [0.0] * pops
    for n in range(5):
        e, w = east_pops[n], west_pops[n]
        pulled[e] = jnp.where(odd == 0, moved_cells(late, velocities[e], z)[n : n + 1], 0.0)
        pulled[w] = jnp.where(odd == 0, 0.0, moved_cells(late, velocities[w], z)[n : n + 1])
    u = [fields[3 * step + a : 3 * step + a + 1] for a in range(3)]
    return collide(pulled, u, fields[12:13], fields[13:14])


def leaving(values, odd, scr):
    for n in range(5):
        e, w = east_pops[n], west_pops[n]
        scr[n : n + 1, :] = jnp.where(odd == 0, values[w], values[e])
    return scr[...]


def item_share(weighted, pick, odd, ref, base):
    picked = select(weighted, pick)
    left = iota((1, 128), 1) < 64
    at_row = iota((8, plane), 0) == jnp.where(odd == 0, 7, 0)
    for n in range(5):
        a, b, c, d = (picked[m : m + 1] for m in (n, 5 + n, 10 + n, 15 + n))
        row = jnp.concatenate([jnp.where(left, a, b), jnp.where(left, c, d)], axis=1)
        tile = slice(base + 8 * n, base + 8 * n + 8)
        ref[tile, :] += jnp.where(at_row, row, 0.0)


def clear(*refs):
    for ref in refs:
        ref[...] = jnp.zeros_like(ref)


def far_message_kernel(*refs, step):
    (got_ref, planes_ref, lvl_ref, ends_ref, pair_ref, mate_ref, pick_ref, place_ref) = refs[:8]
    out_ref, all_scr, rim_scr = refs[8:]
    odd = lax.axis_index("slab") & 1
    clear(all_scr, rim_scr)
    out_ref[0:40, :] = lvl_ref[0:40, :]
    fields = pair_ref[...]
    values = late_share(got_ref[8:16, :], fields, step, odd)
    for i in range(pops):
        all_scr[i : i + 1, :] = values[i]
    item_share(all_scr[...] * fields[14:15], pick_ref[0], odd, out_ref, 0)
    fields = mate_ref[...]
    values = late_share(planes_ref[0:8, :], fields, step, 1 - odd)
    share = select(leaving(values, 1 - odd, rim_scr) * fields[14:15], place_ref[2])
    end = lvl_ref[own_f : own_f + 8, :] + ends_ref[kept_loc_f : kept_loc_f + 8, :]
    out_ref[40:48, :] = end + got_ref[16:24, :] + share
    out_ref[48:56, :] = lvl_ref[far_f : far_f + 8, :]
    out_ref[56:64, :] = ends_ref[kept_far_f : kept_far_f + 8, :]


def shares_kernel(*refs, step):
    (got_ref, planes_ref, lvl_ref, ends_ref, own_ref, pair_ref, mate_ref) = refs[:7]
    (pick_ref, place_ref) = refs[7:9]
    rest_ref, kept_ref, added_ref, fix_ref, all_scr, rim_scr = refs[9:]
    odd = lax.axis_index("slab") & 1
    clear(all_scr, rim_scr, added_ref, fix_ref)
    rest_ref[...] = lvl_ref[rest_at:level_rows, :]
    kept_ref[...] = ends_ref[kept_own_d:kept_rows, :]
    fields = pair_ref[...]
    values = late_share(got_ref[8:16, :], fields, step, odd)
    for i in range(pops):
        all_scr[i : i + 1, :] = values[i]
    item_share(all_scr[...] * fields[14:15], pick_ref[1], odd, rest_ref, 0)
    rim = leaving(values, odd, rim_scr)
    rest_ref[rest_loc_d : rest_loc_d + 8, :] += rim * fields[15:16]
    rim = rim * fields[14:15]
    rest_ref[rest_far_d : rest_far_d + 8, :] += select(rim, place_ref[0])
    rest_ref[rest_own_d : rest_own_d + 8, :] += select(rim, place_ref[1])
    fields = own_ref[...]
    values = late_share(got_ref[0:8, :], fields, step, odd)
    for i in range(pops):
        added_ref[i : i + 1, :] = values[i]
    rim = leaving(values, odd, rim_scr)
    kept_ref[8:16, :] += rim * fields[15:16]
    kept_ref[0:8, :] += select(rim * fields[14:15], place_ref[3])
    fields = mate_ref[...]
    values = late_share(planes_ref[0:8, :], fields, step, 1 - odd)
    for i in range(pops):
        all_scr[i : i + 1, :] = values[i]
    item_share(all_scr[...] * fields[14:15], pick_ref[2], 1 - odd, fix_ref, 0)


def last_kernel(d_ref, alpha_ref, late_ref, u_ref, keep_ref, gain_ref, out_ref, tile_scr, sems):
    def tile(source, g, x, sem):
        block, rows = pl.ds(g * pops, pops), pl.ds(x, 8)
        source = source.at[block, rows] if source is alpha_ref else source
        return pltpu.make_async_copy(source, out_ref.at[block, rows], sems.at[sem])

    copies = [tile(alpha_ref, 0, 8, 0), tile(alpha_ref, 1, 0, 1)]
    for copy in copies:
        copy.start()
    t = Table(d_ref[...])
    odd = t.odd
    copies.append(tile(alpha_ref, odd, pl.multiple_of(8 * odd, 8), 2))
    copies[2].start()
    reached = pl.multiple_of(8 - 8 * odd, 8)
    tile_scr[...] = alpha_ref[pl.ds((1 - odd) * pops, pops), pl.ds(reached, 8), :]

    def side(is_odd):
        values = late_values(is_odd, late_ref, u_ref, keep_ref, gain_ref)
        x = late_layer[is_odd][1] % 8
        for i in range(pops):
            tile_scr[i, x : x + 1, :] += values[i]

    @pl.when((odd == 0) & t.next)
    def _():
        side(0)

    @pl.when((odd == 1) & t.prev)
    def _():
        side(1)

    copies.append(tile(tile_scr, 1 - odd, reached, 3))
    copies[3].start()
    for copy in copies:
        copy.wait()


def vmem():
    return pl.BlockSpec(memory_space=pltpu.VMEM)


def shape(*dims, dtype=f32):
    return jax.ShapeDtypeStruct(dims, dtype)


params = pltpu.CompilerParams(vmem_limit_bytes=24 * 1024 * 1024)
half_scratch = [pltpu.VMEM((2, 320, 128), f32)]
pack_scratch = [pltpu.VMEM((160, plane), f32), pltpu.VMEM((8, plane), f32)] + half_scratch
messages = [shape(rows, plane) for rows in (40, 8, level_rows, kept_rows)]
share_scratch = [pltpu.VMEM((24, plane), f32), pltpu.VMEM((8, plane), f32)]
field = shape(2, edge, plane)
state = shape(2 * pops, edge, plane)
blend_at = 2 * pops
tables_at = blend_at + 2


def hbm():
    return pl.BlockSpec(memory_space=pltpu.HBM)


def cost(flops, bytes_accessed):
    return pl.CostEstimate(flops=flops, bytes_accessed=bytes_accessed, transcendentals=0)


def call(kernel, outs, ins, scratch, name, out_specs=None, estimate=None):
    with jax.named_scope(name):
        return pl.pallas_call(
            kernel,
            out_shape=outs,
            in_specs=[vmem()] * len(ins),
            out_specs=out_specs or [vmem()] * len(outs),
            scratch_shapes=scratch,
            compiler_params=params,
            cost_estimate=estimate,
        )(*ins)


def local(
    adjoint_final, populations, relaxation, blend, solid, chain, parent, children, *, slabs
):
    steps = populations.shape[0]
    tables = jnp.concatenate([children, parent, chain[0]], axis=1).astype(f32)
    tables = jnp.pad(tables, ((0, edge - 2), (0, plane - 12)), constant_values=-1.0)
    alpha = jnp.concatenate(
        [adjoint_final.reshape(2 * pops, edge, plane), blend[0], tables[None]], axis=0
    )
    table, *sent, kept = call(
        first_pack_kernel,
        [shape(8, 128, dtype=jnp.int32)] + messages + [field],
        (alpha,),
        pack_scratch,
        "pack_first",
    )
    weights = alpha[blend_at:tables_at]
    with jax.named_scope("exchange"):
        item, side, lvl, ends = sent
        lvl = level_swap(lvl, slabs)
        side = mate_swap(side, slabs, 1)
        end = lvl[own_f : own_f + 8] + ends[kept_loc_f : kept_loc_f + 8] + side
        parts = [lvl[0:40], end, lvl[far_f : far_f + 8], ends[kept_far_f : kept_far_f + 8]]
        message = jnp.concatenate(parts, axis=0)
        rest, kept_d = lvl[rest_at:], ends[kept_own_d:]
    flows, keep, gain, bits, pick, place, own_late, fix_pick, fix_place = call(
        fields_kernel,
        [
            shape(steps, 2, 3, edge, plane),
            field,
            field,
            shape(2, edge, plane, dtype=jnp.int32),
            shape(3, plane, 128, dtype=bf16),
            shape(3, plane, plane, dtype=bf16),
            shape(16, plane),
            shape(3, plane, 128, dtype=bf16),
            shape(4, plane, plane, dtype=bf16),
        ],
        (table, populations[:, 0], relaxation[0], solid[0], weights, kept),
        [pltpu.VMEM((32, plane), f32)],
        "flow_fields",
        estimate=cost(4_000_000, 2_000_000),
    )
    shares = []
    for t in range(steps - 1, -1, -1):
        first, last = t == steps - 1, t == 0
        u = flows[t]
        with jax.named_scope("exchange"):
            far = far_swap(message, slabs)
            mate = mate_swap(item, slabs, 1)
            pair_end = rest[rest_loc_d : rest_loc_d + 8] + kept_d[0:8] + far[56:64]
            own_end = kept_d[8:16] + rest[rest_own_d : rest_own_d + 8] + far[48:56]
            if last:
                late = mate_swap(pair_end, slabs, 1)
        before = call(
            functools.partial(before_kernel, first=first),
            [state],
            (table, alpha, kept, mate, rest, *shares),
            half_scratch,
            "before",
            estimate=cost(4_000_000, 2_000_000),
        )[0]
        ins = [table, before, kept, u, keep, gain, bits, rest, far]
        if not last:
            ins += [weights, pick, place]
        got = call(
            functools.partial(step_kernel, last=last),
            [state] + ([] if last else messages),
            ins,
            [pltpu.VMEM((2, pops, 32, plane), f32)] + (half_scratch if last else pack_scratch),
            "step",
            estimate=cost(8_000_000, 2_000_000),
        )
        alpha = got[0]
        if last:
            alpha = call(
                last_kernel,
                [state],
                (table, alpha, late, u, keep, gain),
                [pltpu.VMEM((pops, 8, plane), f32), pltpu.SemaphoreType.DMA((4,))],
                "finish",
                out_specs=[hbm()],
            )[0]
            continue
        item, side, lvl, ends = got[1:]
        with jax.named_scope("exchange"):
            planes = jnp.concatenate([pair_end, own_end], axis=0)
            parts = [planes, side]
            if first:
                lvl = jnp.concatenate([lvl, own_late], axis=0)
                parts += [own_late]
            lvl = level_swap(lvl, slabs)
            late = mate_swap(jnp.concatenate(parts, axis=0), slabs, 1)
            if first:
                pair_late, mate_late = lvl[level_rows:], late[24:40]
        message = call(
            functools.partial(far_message_kernel, step=t),
            [shape(64, plane)],
            (late, planes, lvl, ends, pair_late, mate_late, fix_pick, fix_place),
            share_scratch,
            "far_message",
        )[0]
        rest, kept_d, *shares = call(
            functools.partial(shares_kernel, step=t),
            [shape(rest_rows, plane), shape(16, plane), shape(24, plane), shape(40, plane)],
            (late, planes, lvl, ends, own_late, pair_late, mate_late, fix_pick, fix_place),
            share_scratch,
            "shares",
            estimate=cost(2_000_000, 500_000),
        )
    return alpha.reshape(1, 2, pops, edge, plane)


def solution(mesh):
    return jax.shard_map(
        functools.partial(local, slabs=mesh.shape["slab"]),
        mesh=mesh,
        in_specs=(
            P("lvl", "slab", None, None, None),
            P(None, "lvl", "slab", None, None, None),
            P("lvl", "slab", None, None),
            P("lvl", "slab", None, None),
            P("lvl", "slab", None, None),
            P("lvl", "slab", None),
            P("slab", None),
            P("slab", None),
        ),
        out_specs=P("lvl", "slab", None, None, None),
        check_vma=False,
    )
```

```python
import functools

import jax
import jax.numpy as jnp
from jax import lax
from jax.experimental import pallas as pl
from jax.experimental.pallas import tpu as pltpu
from jax.sharding import PartitionSpec as P

velocities = [
    (0, 0, 0),
    (1, 0, 0),
    (-1, 0, 0),
    (0, 1, 0),
    (0, -1, 0),
    (0, 0, 1),
    (0, 0, -1),
    (1, 1, 0),
    (-1, -1, 0),
    (1, -1, 0),
    (-1, 1, 0),
    (1, 0, 1),
    (-1, 0, -1),
    (1, 0, -1),
    (-1, 0, 1),
    (0, 1, 1),
    (0, -1, -1),
    (0, 1, -1),
    (0, -1, 1),
]
east_pops = [1, 7, 9, 11, 13]
west_pops = [2, 8, 10, 12, 14]
opposite = [velocities.index((-c[0], -c[1], -c[2])) for c in velocities]
axes = ("slab", "lvl")
pops, edge, plane = 19, 16, 256
f32, bf16 = jnp.float32, jnp.bfloat16

item_row = (0, 0, 56)
own_f, far_f, mate_f, far_d, loc_d, own_d, level_rows = 40, 48, 96, 104, 112, 120, 128
kept_loc_f, kept_far_f, kept_own_d, kept_loc_d, kept_rows = 0, 8, 16, 24, 32
rest_at, rest_rows = 56, 72
rest_mate_f, rest_far_d, rest_loc_d, rest_own_d = 40, 48, 56, 64


at_parent, at_octant, at_prev, at_next = 8, 9, 10, 11


def level_swap(value, slabs):
    pairs = [(2 * s + v, 2 * s + 1 - v) for s in range(slabs) for v in (0, 1)]
    return lax.ppermute(value, axes, pairs)


def mate_swap(value, slabs, cross):
    pairs = [(2 * s + v, 2 * (s ^ 1) + (v ^ cross)) for s in range(slabs) for v in (0, 1)]
    return lax.ppermute(value, axes, pairs)


def far_swap(value, slabs):
    pairs = []
    for s in range(slabs):
        other = s - 1 if s % 2 == 0 else s + 1
        for v in (0, 1):
            if 0 <= other < slabs:
                pairs.append((2 * s + v, 2 * other + v))
            else:
                pairs.append((2 * s + v, 2 * s + 1 - v))
    return lax.ppermute(value, axes, pairs)


def cell_key(index, level, octant):
    y, z = index >> 4, index & 15
    fine = (y >> 1) * 8 + (z >> 1)
    inside = ((y >> 3) == ((octant >> 1) & 1)) & ((z >> 3) == (octant & 1))
    coarse = jnp.where(inside, (y & 7) * 8 + (z & 7), -1)
    return jnp.where(level == 1, fine, coarse)


def select(values, matrix):
    rows = values.shape[0]
    high = values.astype(bf16).astype(f32)
    halves = jnp.concatenate([high, values - high], axis=0).astype(bf16)
    both = jnp.dot(halves, matrix, preferred_element_type=f32)
    return both[:rows] + both[rows:]


def ones_where(mask):
    return jnp.where(mask, 1.0, 0.0).astype(bf16)


def iota(shape, dim):
    return lax.broadcasted_iota(jnp.int32, shape, dim)


class Table:
    def __init__(self, row):
        codes = [row[0, j] for j in range(3)]
        self.pair_codes = [row[0, j] for j in range(8, 11)]
        self.valid = [code >= 0 for code in codes]
        self.block = [(code >> 4) & 1 for code in codes]
        self.octant = [(code >> 1) & 7 for code in codes]
        self.other = [code & 1 for code in codes]
        self.level, self.odd, prev, inner, next_ = (row[0, j] for j in range(3, 8))
        self.prev, self.inner, self.next = prev >= 0, inner >= 0, next_ >= 0


def make_table(tables, slab, level):
    odd = slab & 1
    row, lane = iota(tables.shape, 0), iota(tables.shape, 1)
    towards = 1 - 2 * odd

    def codes(of_level):
        octant = jnp.where(of_level == 0, lane, pltpu.roll(tables, 127, 1))
        coarse, fine = jnp.where(lane < at_parent, 1, 0), jnp.where(lane == at_parent, 1, 0)
        here = jnp.where(of_level == 0, coarse, fine)
        code = row * 16 + octant * 2 + (tables & 1)
        code = jnp.where((here == 1) & (row < 2) & (tables >= 0), code, -1)
        offset = (tables >> 1) - slab
        return [jnp.max(jnp.where(offset == d, code, -1)) for d in (towards, -towards, 0)]

    values = codes(level)
    values += [level, odd, tables[0, at_prev], tables[0, at_next], tables[1, at_next]]
    values += codes(1 - level)
    out = jnp.zeros(tables.shape, jnp.int32)
    for n, value in enumerate(values):
        out = jnp.where(lane == n, value, out)
    return out


def pick_matrices(t, j):
    return coupling_matrices(t.level, t.octant[j])


def coupling_matrices(level, octant):
    y0, z0 = ((octant >> 1) & 1) * 8, (octant & 1) * 8

    def own_cell(y, z):
        return jnp.where(level == 0, ((y0 + y) << 4) | (z0 + z), (y << 5) | (z << 1))

    cell = iota((plane, 128), 0) & jnp.where(level == 0, 255, 238)
    item = iota((1, 128), 1) & 63
    pick = ones_where(cell == own_cell(item >> 3, item & 7))
    there = iota((1, plane), 1)
    y, z = there >> 4, there & 15
    inside = ((y & 8) == y0) & ((z & 8) == z0)
    to_fine = own_cell(y >> 1, z >> 1)
    to_coarse = jnp.where(inside, own_cell(y & 7, z & 7), -1)
    target = jnp.where(level == 0, to_fine, to_coarse)
    place = jnp.concatenate(
        [ones_where(cell == target[:, :128]), ones_where(cell == target[:, 128:])], axis=1
    )
    return pick, place


def plane_scale(t):
    return jnp.where(t.level == 0, 0.125, 1.0)


def pack(t, alpha_ref, w_ref, k_ref, item_ref, side_ref, lvl_ref, ends_ref, scratch, matrices):
    item_scr, rim_scr, half_scr = scratch
    level, odd = t.level, t.odd
    for ref in (item_ref, side_ref, lvl_ref, ends_ref):
        if ref is not None:
            ref[...] = jnp.zeros_like(ref)
    item_scr[152:160, :] = jnp.zeros((8, plane), f32)
    rim_scr[...] = jnp.zeros_like(rim_scr)
    for i in range(5):
        e, w = east_pops[i], west_pops[i]
        low = alpha_ref[e, 0:1, :] * k_ref[0, 0:1, :]
        high = alpha_ref[pops + w, edge - 1 : edge, :] * k_ref[1, edge - 1 : edge, :]
        lvl_ref[loc_d + i : loc_d + i + 1, :] = jnp.where(odd == 1, low, high)
        ends_ref[kept_loc_f + i : kept_loc_f + i + 1, :] = jnp.where(odd == 1, high, low)
    for j in range(3):
        base = item_row[j]
        out_ref = item_ref if j == 0 else lvl_ref

        @pl.when(t.valid[j])
        def _(j=j, base=base, out_ref=out_ref):
            g, octant, other = t.block[j], t.octant[j], t.other[j]
            ox = octant >> 2
            pick, place = matrices(j)

            @pl.when(level == 0)
            def _():
                rows = pl.ds(pl.multiple_of(ox * 8, 8), 8)
                part = alpha_ref[pl.ds(g * pops, pops), rows, :] * w_ref[g, rows, :][None]
                item_scr[0:152, :] = part.reshape(152, plane)

            @pl.when(level == 1)
            def _():
                part = (alpha_ref[pl.ds(g * pops, pops)] * w_ref[g][None]).reshape(304, plane)
                for n in range(2):
                    lanes = slice(128 * n, 128 * n + 128)
                    half_scr[n, 0:304, :] = part[:, lanes]
                    item_scr[0:152, lanes] = (
                        half_scr[n, pl.ds(0, 152, stride=2), :]
                        + half_scr[n, pl.ds(1, 152, stride=2), :]
                    )

            picked = select(item_scr[...], pick)
            left = iota((40, 128), 1) < 64
            out_ref[base : base + 40, 0:128] = jnp.where(left, picked[0:40], picked[40:80])
            out_ref[base : base + 40, 128:256] = jnp.where(left, picked[80:120], picked[120:160])

            @pl.when((level == 0) | (ox == other))
            def _():
                for i in range(5):
                    e, w = east_pops[i] * 8, west_pops[i] * 8 + 7
                    rim_scr[i : i + 1, :] = jnp.where(
                        other == 1, item_scr[w : w + 1, :], item_scr[e : e + 1, :]
                    )
                spread = select(rim_scr[...], place) * plane_scale(t)
                towards_d = other != odd
                to_d = ((side_ref, 0), (lvl_ref, far_d), (lvl_ref, own_d))[j]
                to_f = ((lvl_ref, mate_f), (lvl_ref, far_f), (lvl_ref, own_f))[j]
                for wanted, (ref, row) in ((towards_d, to_d), (other == odd, to_f)):
                    if ref is None:
                        continue

                    @pl.when(wanted)
                    def _(ref=ref, row=row):
                        ref[row : row + 8, :] = spread

    for row, kept in ((far_f, kept_far_f), (own_d, kept_own_d), (loc_d, kept_loc_d)):
        ends_ref[kept : kept + 8, :] = lvl_ref[row : row + 8, :]


def first_pack_kernel(*refs):
    alpha_ref, d_ref, item_ref, side_ref, lvl_ref, ends_ref, k_ref = refs[:7]
    scratch = refs[7:]
    w_ref = alpha_ref.at[blend_at : blend_at + 2]
    tables = alpha_ref[tables_at, 0:8, 0:128].astype(jnp.int32)
    row = make_table(tables, lax.axis_index("slab"), lax.axis_index("lvl"))
    d_ref[...] = row
    t = Table(row)
    level = t.level
    x = iota((edge, plane), 0)
    cell = iota((edge, plane), 1)
    covers = []
    for g in range(2):
        covered = jnp.zeros((edge, plane), jnp.bool_)
        for j in range(3):
            octant = t.octant[j]
            inside = (
                ((x >> 3) == (octant >> 2))
                & ((cell >> 7) == ((octant >> 1) & 1))
                & (((cell >> 3) & 1) == (octant & 1))
            ) | (level == 1)
            covered = covered | (inside & t.valid[j] & (t.block[j] == g))
        covers.append(covered)
    for g in range(2):
        k_ref[g] = jnp.where(covers[g], 1.0 - w_ref[g], 1.0)
    matrices = functools.partial(pick_matrices, t)
    pack(t, alpha_ref, w_ref, k_ref, item_ref, side_ref, lvl_ref, ends_ref, scratch, matrices)


def moved_cells(values, c, z):
    if c[1] == 0 and c[2] == 0:
        return values
    base = -16 * c[1]
    axis = values.ndim - 1
    if c[2] == 0:
        return pltpu.roll(values, base % plane, axis)
    inner = pltpu.roll(values, (base - c[2]) % plane, axis)
    around = pltpu.roll(values, (base + 15 * c[2]) % plane, axis)
    return jnp.where(z == (15 if c[2] == 1 else 0), around, inner)


def fields_kernel(*refs):
    d_ref, pop_ref, relax_ref, solid_ref, w_ref, k_ref = refs[:6]
    u_ref, keep_ref, gain_ref, bits_ref, pick_ref, place_ref = refs[6:12]
    late_ref, fix_pick_ref, fix_place_ref, pad_scr = refs[12:]
    t = Table(d_ref[...])
    for j in range(3):
        pick_ref[j], place_ref[j] = pick_matrices(t, j)

    def fixes(level, odd, valid, block, octant, other):
        pick, place = coupling_matrices(level, octant)
        ox, side = octant >> 2, 1 - odd
        item = valid & (block == side) & ((level == 1) | (ox == side))
        end = item & (other == side) & ((level == 0) | (ox == other))
        scale = jnp.where(level == 0, 0.125, 1.0)
        pick = (pick.astype(f32) * jnp.where(item, 1.0, 0.0)).astype(bf16)
        place = (place.astype(f32) * jnp.where(end, scale, 0.0)).astype(bf16)
        return pick, place

    def of_code(code, level):
        return fixes(level, t.odd, code >= 0, (code >> 4) & 1, (code >> 1) & 7, code & 1)

    pair = 1 - t.level
    fix_pick_ref[0], fix_place_ref[0] = of_code(t.pair_codes[1], pair)
    fix_pick_ref[1], fix_place_ref[1] = of_code(t.pair_codes[2], pair)
    fix_pick_ref[2], fix_place_ref[2] = fixes(
        pair, 1 - t.odd, t.valid[0], t.other[0], t.octant[0], t.block[0]
    )
    fix_place_ref[3] = fixes(t.level, t.odd, t.valid[2], t.block[2], t.octant[2], t.other[2])[1]
    z = iota((edge, plane), 1) & 15
    for g in range(2):
        solid = solid_ref[g] > 0
        omega = relax_ref[g]
        keep_ref[g] = jnp.where(solid, 0.0, 1.0 - omega)
        gain_ref[g] = jnp.where(solid, 0.0, omega)
        pad_scr[0:8, :] = jnp.zeros((8, plane), f32)
        pad_scr[24:32, :] = jnp.zeros((8, plane), f32)
        pad_scr[8:24, :] = jnp.where(solid, 1.0, 0.0)
        bits = jnp.zeros((edge, plane), jnp.int32)
        for i in range(pops):
            c = velocities[i]
            blocked = moved_cells(pad_scr[8 + c[0] : 24 + c[0], :], c, z) > 0.5
            bits = bits | jnp.where(blocked, 1 << i, 0)
        bits_ref[g] = bits
    steps = pop_ref.shape[0]
    for n in range(steps):
        for g in range(2):
            total = jnp.zeros((edge, plane), f32)
            flow = [jnp.zeros((edge, plane), f32) for _ in range(3)]
            for i in range(pops):
                f = pop_ref[n, g, i].astype(f32)
                total = total + f
                for a in range(3):
                    if velocities[i][a] == 1:
                        flow[a] = flow[a] + f
                    elif velocities[i][a] == -1:
                        flow[a] = flow[a] - f
            for a in range(3):
                u_ref[n, g, a] = flow[a] / total
    for is_odd, (g, x) in enumerate(late_layer):

        @pl.when(t.odd == is_odd)
        def _(is_odd=is_odd, g=g, x=x):
            link = jnp.where(t.prev if is_odd else t.next, 1.0, 0.0)
            rows = [u_ref[n, g, a, x : x + 1, :] for n in range(steps) for a in range(3)]
            rows += [keep_ref[g, x : x + 1, :] * link, gain_ref[g, x : x + 1, :] * link]
            rows += [w_ref[g, x : x + 1, :], k_ref[g, x : x + 1, :]]
            for n, row in enumerate(rows):
                late_ref[n : n + 1, :] = row


def collide(pulled, u, keep, gain):
    g = pulled
    plus = {i: g[i] + g[i + 1] for i in range(1, pops, 2)}
    minus = {i: g[i] - g[i + 1] for i in range(1, pops, 2)}
    xy, xz, yz = plus[7] + plus[9], plus[11] + plus[13], plus[15] + plus[17]
    px, py, pz = 2.0 * plus[1], 2.0 * plus[3], 2.0 * plus[5]
    weight = 12.0 * g[0] + (px + py + pz) + (xy + xz + yz)
    qxx, qyy, qzz = px + xy + xz, py + xy + yz, pz + xz + yz
    qxy, qxz, qyz = plus[7] - plus[9], plus[11] - plus[13], plus[15] - plus[17]
    jx = 2.0 * minus[1] + (minus[7] + minus[9]) + (minus[11] + minus[13])
    jy = 2.0 * minus[3] + (minus[7] - minus[9]) + (minus[15] + minus[17])
    jz = 2.0 * minus[5] + (minus[11] - minus[13]) + (minus[15] - minus[17])
    ux, uy, uz = u
    qux = qxx * ux + qxy * uy + qxz * uz
    quy = qxy * ux + qyy * uy + qyz * uz
    quz = qxz * ux + qyz * uy + qzz * uz
    speed = ux * ux + uy * uy + uz * uz
    along = ux * qux + uy * quy + uz * quz
    scale = gain * (1.0 / 36.0)
    rest = scale * (weight * (1.0 + 1.5 * speed) - 4.5 * along)
    scale = gain * (1.0 / 12.0)
    mx = scale * (jx + 3.0 * qux - ux * weight)
    my = scale * (jy + 3.0 * quy - uy * weight)
    mz = scale * (jz + 3.0 * quz - uz * weight)
    out = [None] * pops
    out[0] = keep * g[0] + rest
    pairs = [mx, my, mz, mx + my, mx - my, mx + mz, mx - mz, my + mz, my - mz]
    for n, i in enumerate(range(1, pops, 2)):
        out[i] = keep * g[i] + (rest + pairs[n])
        out[i + 1] = keep * g[i + 1] + (rest - pairs[n])
    return out


def add_item(t, j, item, half_scr, add):
    level, g, octant = t.level, t.block[j], t.octant[j]
    left = iota((40, 128), 1) < 64
    a, b = item[:, 0:128], item[:, 128:256]
    parts = [(a, left), (a, ~left), (b, left), (b, ~left)]
    stacked = jnp.concatenate([jnp.where(m, v, 0.0) for v, m in parts], axis=0)
    high = stacked.astype(bf16).astype(f32)
    halves = jnp.concatenate([high, stacked - high], axis=1).astype(bf16)
    target = cell_key(iota((1, plane), 1), level, octant)
    matrix = ones_where((iota((plane, plane), 0) & 63) == target)
    spread = jnp.dot(halves, matrix, preferred_element_type=f32)

    @pl.when(level == 0)
    def _():
        first = pl.multiple_of((octant >> 2) * 8, 8)
        add(g, first, 8, slice(0, plane), spread[0:152].reshape(pops, 8, plane))

    @pl.when(level == 1)
    def _():
        for n in range(2):
            lanes = slice(128 * n, 128 * n + 128)
            half = spread[:, lanes] * 0.125
            half_scr[n, pl.ds(0, 160, stride=2), :] = half
            half_scr[n, pl.ds(1, 160, stride=2), :] = half
            both = half_scr[n, 0:304, :].reshape(pops, edge, 128)
            add(g, 0, edge, lanes, both)


def before_kernel(*refs, first):
    (d_ref, alpha_ref, k_ref, mate_ref, rest_ref) = refs[:5]
    refs = refs[5:]
    if not first:
        (added_ref, fix_ref), refs = refs[:2], refs[2:]
    out_ref, half_scr = refs
    t = Table(d_ref[...])
    for g in range(2):
        block = slice(g * pops, (g + 1) * pops)
        out_ref[block] = alpha_ref[block] * k_ref[g][None]
    if not first:
        for is_odd, (g, x) in enumerate(late_layer):

            @pl.when(t.odd == is_odd)
            def _(g=g, x=x):
                kept = k_ref[g, x : x + 1, :]
                for i in range(pops):
                    out_ref[g * pops + i, x : x + 1, :] += added_ref[i : i + 1, :] * kept

    def add(g, start, layers, lanes, values):
        out_ref[pl.ds(g * pops, pops), pl.ds(start, layers), lanes] += values

    @pl.when(t.valid[0])
    def _():
        item = mate_ref[...] if first else mate_ref[...] + fix_ref[...]
        add_item(t, 0, item, half_scr, add)

    @pl.when(t.valid[2])
    def _():
        add_item(t, 2, rest_ref[0:40, :], half_scr, add)


def step_kernel(*refs, last):
    (d_ref, before_ref, k_ref, u_ref, keep_ref, gain_ref, bits_ref, lvl_ref, far_ref) = refs[:9]
    refs = refs[9:]
    if not last:
        (w_ref, place_ref), refs = refs[:2], refs[2:]
        out_ref, side_ref, beta_scr, rim_scr, half_scr = refs
    else:
        out_ref, beta_scr, half_scr = refs
    t = Table(d_ref[...])
    level, odd = t.level, t.odd
    for g in range(2):
        beta_scr[g, :, 8:24, :] = before_ref[g * pops : (g + 1) * pops]

    def add(g, start, layers, lanes, values):
        beta_scr[g, :, pl.ds(8 + start, layers), lanes] += values

    @pl.when(t.valid[1])
    def _():
        add_item(t, 1, far_ref[0:40, :], half_scr, add)

    from_d = lvl_ref[rest_mate_f : rest_mate_f + 8, :]
    from_f = far_ref[40:48, :] + lvl_ref[rest_far_d : rest_far_d + 8, :]
    above = jnp.where(odd == 1, from_f, from_d)
    below = jnp.where(odd == 1, from_d, from_f)
    above = jnp.where(t.next, above, 0.0)
    below = jnp.where(t.prev, below, 0.0)
    inner = t.inner
    for i in range(5):
        e, w = east_pops[i], west_pops[i]
        beta_scr[1, e, 24:25, :] = above[i : i + 1]
        beta_scr[0, w, 7:8, :] = below[i : i + 1]
        beta_scr[0, e, 24:25, :] = jnp.where(inner, beta_scr[1, e, 8:9, :], 0.0)
        beta_scr[1, w, 7:8, :] = jnp.where(inner, beta_scr[0, w, 23:24, :], 0.0)
    z = iota((8, plane), 1) & 15
    for g in range(2):
        for h in range(2):
            rows = slice(8 * h, 8 * h + 8)
            first = 8 + 8 * h
            bits = bits_ref[g, rows, :]
            pulled = []
            for i in range(pops):
                c = velocities[i]
                v = beta_scr[g, i, first + c[0] : first + c[0] + 8, :]
                v = moved_cells(v, c, z)
                back = beta_scr[g, opposite[i], first : first + 8, :]
                pulled.append(jnp.where((bits & (1 << i)) != 0, back, v))
            u = [u_ref[g, a, rows, :] for a in range(3)]
            done = collide(pulled, u, keep_ref[g, rows, :], gain_ref[g, rows, :])
            for i in range(pops):
                out_ref[g * pops + i, rows, :] = done[i]
    if not last:
        side_plane(t, out_ref, w_ref, place_ref[0], side_ref, rim_scr)


def side_plane(t, alpha_ref, w_ref, place, side_ref, rim_scr):
    clear(side_ref, rim_scr)
    level, odd = t.level, t.odd
    g, other, ox = t.block[0], t.other[0], t.octant[0] >> 2
    x = jnp.where(other == 1, 7, 0)

    def rows(layer):
        weight = w_ref[g, pl.ds(layer, 1), :]
        for i in range(5):
            pop = jnp.where(other == 1, west_pops[i], east_pops[i])
            rim_scr[i : i + 1, :] += alpha_ref[g * pops + pop, pl.ds(layer, 1), :] * weight

    @pl.when(t.valid[0] & (other != odd) & ((level == 0) | (ox == other)))
    def _():
        @pl.when(level == 0)
        def _():
            rows(ox * 8 + x)

        @pl.when(level == 1)
        def _():
            rows(2 * x)
            rows(2 * x + 1)

        side_ref[...] = select(rim_scr[...], place) * plane_scale(t)


def pack_kernel(*refs):
    d_ref, alpha_ref, w_ref, k_ref, pick_ref, place_ref, item_ref, lvl_ref, ends_ref = refs[:9]
    matrices = lambda j: (pick_ref[j], place_ref[j])
    t = Table(d_ref[...])
    pack(t, alpha_ref, w_ref, k_ref, item_ref, None, lvl_ref, ends_ref, refs[9:], matrices)


late_layer = ((1, edge - 1), (0, 0))


def late_values(is_odd, late_ref, u_ref, keep_ref, gain_ref):
    g, x = late_layer[is_odd]
    z = iota((8, plane), 1) & 15
    late = late_ref[...]
    pulled = [0.0] * pops
    for n, i in enumerate((east_pops, west_pops)[is_odd]):
        pulled[i] = moved_cells(late, velocities[i], z)[n : n + 1]
    rows = slice(x, x + 1)
    u = [u_ref[g, a, rows, :] for a in range(3)]
    return collide(pulled, u, keep_ref[g, rows, :], gain_ref[g, rows, :])


def late_share(late, fields, step, odd):
    z = iota((8, plane), 1) & 15
    pulled = [0.0] * pops
    for n in range(5):
        e, w = east_pops[n], west_pops[n]
        pulled[e] = jnp.where(odd == 0, moved_cells(late, velocities[e], z)[n : n + 1], 0.0)
        pulled[w] = jnp.where(odd == 0, 0.0, moved_cells(late, velocities[w], z)[n : n + 1])
    u = [fields[3 * step + a : 3 * step + a + 1] for a in range(3)]
    return collide(pulled, u, fields[12:13], fields[13:14])


def leaving(values, odd, scr):
    for n in range(5):
        e, w = east_pops[n], west_pops[n]
        scr[n : n + 1, :] = jnp.where(odd == 0, values[w], values[e])
    return scr[...]


def item_share(weighted, pick, odd, ref, base):
    picked = select(weighted, pick)
    left = iota((1, 128), 1) < 64
    at_row = iota((8, plane), 0) == jnp.where(odd == 0, 7, 0)
    for n in range(5):
        a, b, c, d = (picked[m : m + 1] for m in (n, 5 + n, 10 + n, 15 + n))
        row = jnp.concatenate([jnp.where(left, a, b), jnp.where(left, c, d)], axis=1)
        tile = slice(base + 8 * n, base + 8 * n + 8)
        ref[tile, :] += jnp.where(at_row, row, 0.0)


def clear(*refs):
    for ref in refs:
        ref[...] = jnp.zeros_like(ref)


def far_shares_kernel(*refs, step):
    (got_ref, planes_ref, pair_ref, mate_ref, pick_ref, place_ref) = refs[:6]
    out_ref, all_scr, rim_scr = refs[6:]
    odd = lax.axis_index("slab") & 1
    clear(out_ref, all_scr, rim_scr)
    fields = pair_ref[...]
    values = late_share(got_ref[5:13, :], fields, step, odd)
    for i in range(pops):
        all_scr[i : i + 1, :] = values[i]
    item_share(all_scr[...] * fields[14:15], pick_ref[0], odd, out_ref, 0)
    fields = mate_ref[...]
    values = late_share(planes_ref[0:8, :], fields, step, 1 - odd)
    share = select(leaving(values, 1 - odd, rim_scr) * fields[14:15], place_ref[2])
    out_ref[40:45, :] = got_ref[10:15, :] + share[0:5]


def shares_kernel(*refs, step):
    (got_ref, planes_ref, lvl_ref, ends_ref, own_ref, pair_ref, mate_ref) = refs[:7]
    (pick_ref, place_ref) = refs[7:9]
    rest_ref, kept_ref, added_ref, fix_ref, all_scr, rim_scr = refs[9:]
    odd = lax.axis_index("slab") & 1
    clear(all_scr, rim_scr, added_ref, fix_ref)
    rest_ref[...] = lvl_ref[rest_at:level_rows, :]
    kept_ref[...] = ends_ref[kept_own_d:kept_rows, :]
    fields = pair_ref[...]
    values = late_share(got_ref[5:13, :], fields, step, odd)
    for i in range(pops):
        all_scr[i : i + 1, :] = values[i]
    item_share(all_scr[...] * fields[14:15], pick_ref[1], odd, rest_ref, 0)
    rim = leaving(values, odd, rim_scr)
    rest_ref[rest_loc_d : rest_loc_d + 8, :] += rim * fields[15:16]
    rim = rim * fields[14:15]
    rest_ref[rest_far_d : rest_far_d + 8, :] += select(rim, place_ref[0])
    rest_ref[rest_own_d : rest_own_d + 8, :] += select(rim, place_ref[1])
    fields = own_ref[...]
    values = late_share(got_ref[0:8, :], fields, step, odd)
    for i in range(pops):
        added_ref[i : i + 1, :] = values[i]
    rim = leaving(values, odd, rim_scr)
    kept_ref[8:16, :] += rim * fields[15:16]
    kept_ref[0:8, :] += select(rim * fields[14:15], place_ref[3])
    fields = mate_ref[...]
    values = late_share(planes_ref[0:8, :], fields, step, 1 - odd)
    for i in range(pops):
        all_scr[i : i + 1, :] = values[i]
    item_share(all_scr[...] * fields[14:15], pick_ref[2], 1 - odd, fix_ref, 0)


def last_kernel(d_ref, alpha_ref, late_ref, u_ref, keep_ref, gain_ref, out_ref, tile_scr, sems):
    def tile(source, g, x, sem):
        block, rows = pl.ds(g * pops, pops), pl.ds(x, 8)
        source = source.at[block, rows] if source is alpha_ref else source
        return pltpu.make_async_copy(source, out_ref.at[block, rows], sems.at[sem])

    copies = [tile(alpha_ref, 0, 8, 0), tile(alpha_ref, 1, 0, 1)]
    for copy in copies:
        copy.start()
    t = Table(d_ref[...])
    odd = t.odd
    copies.append(tile(alpha_ref, odd, pl.multiple_of(8 * odd, 8), 2))
    copies[2].start()
    reached = pl.multiple_of(8 - 8 * odd, 8)
    tile_scr[...] = alpha_ref[pl.ds((1 - odd) * pops, pops), pl.ds(reached, 8), :]

    def side(is_odd):
        values = late_values(is_odd, late_ref, u_ref, keep_ref, gain_ref)
        x = late_layer[is_odd][1] % 8
        for i in range(pops):
            tile_scr[i, x : x + 1, :] += values[i]

    @pl.when((odd == 0) & t.next)
    def _():
        side(0)

    @pl.when((odd == 1) & t.prev)
    def _():
        side(1)

    copies.append(tile(tile_scr, 1 - odd, reached, 3))
    copies[3].start()
    for copy in copies:
        copy.wait()


def vmem():
    return pl.BlockSpec(memory_space=pltpu.VMEM)


def shape(*dims, dtype=f32):
    return jax.ShapeDtypeStruct(dims, dtype)


params = pltpu.CompilerParams(vmem_limit_bytes=24 * 1024 * 1024)
half_scratch = [pltpu.VMEM((2, 320, 128), f32)]
pack_scratch = [pltpu.VMEM((160, plane), f32), pltpu.VMEM((8, plane), f32)] + half_scratch
messages = [shape(rows, plane) for rows in (40, 8, level_rows, kept_rows)]
share_scratch = [pltpu.VMEM((24, plane), f32), pltpu.VMEM((8, plane), f32)]
field = shape(2, edge, plane)
state = shape(2 * pops, edge, plane)
blend_at = 2 * pops
tables_at = blend_at + 2


def hbm():
    return pl.BlockSpec(memory_space=pltpu.HBM)


def cost(flops, bytes_accessed):
    return pl.CostEstimate(flops=flops, bytes_accessed=bytes_accessed, transcendentals=0)


def call(kernel, outs, ins, scratch, name, out_specs=None, estimate=None):
    with jax.named_scope(name):
        return pl.pallas_call(
            kernel,
            out_shape=outs,
            in_specs=[vmem()] * len(ins),
            out_specs=out_specs or [vmem()] * len(outs),
            scratch_shapes=scratch,
            compiler_params=params,
            cost_estimate=estimate,
        )(*ins)


def far_message(lvl, ends, side, share=0.0):
    end = lvl[own_f : own_f + 5] + ends[kept_loc_f : kept_loc_f + 5] + side
    parts = [lvl[0:40] + share, end, lvl[far_f : far_f + 5], ends[kept_far_f : kept_far_f + 5]]
    return jnp.pad(jnp.concatenate(parts, axis=0), ((0, 1), (0, 0)))


def local(
    adjoint_final, populations, relaxation, blend, solid, chain, parent, children, *, slabs
):
    steps = populations.shape[0]
    tables = jnp.concatenate([children, parent, chain[0]], axis=1).astype(f32)
    tables = jnp.pad(tables, ((0, edge - 2), (0, plane - 12)), constant_values=-1.0)
    alpha = jnp.concatenate(
        [adjoint_final.reshape(2 * pops, edge, plane), blend[0], tables[None]], axis=0
    )
    table, *sent, kept = call(
        first_pack_kernel,
        [shape(8, 128, dtype=jnp.int32)] + messages + [field],
        (alpha,),
        pack_scratch,
        "pack_first",
    )
    weights = alpha[blend_at:tables_at]
    with jax.named_scope("exchange"):
        item, side, lvl, ends = sent
        lvl = level_swap(lvl, slabs)
        side = mate_swap(side, slabs, 1)
        message = far_message(lvl, ends, side[0:5])
        rest, kept_d = lvl[rest_at:], ends[kept_own_d:]
    flows, keep, gain, bits, pick, place, own_late, fix_pick, fix_place = call(
        fields_kernel,
        [
            shape(steps, 2, 3, edge, plane),
            field,
            field,
            shape(2, edge, plane, dtype=jnp.int32),
            shape(3, plane, 128, dtype=bf16),
            shape(3, plane, plane, dtype=bf16),
            shape(16, plane),
            shape(3, plane, 128, dtype=bf16),
            shape(4, plane, plane, dtype=bf16),
        ],
        (table, populations[:, 0], relaxation[0], solid[0], weights, kept),
        [pltpu.VMEM((32, plane), f32)],
        "flow_fields",
        estimate=cost(4_000_000, 2_000_000),
    )
    shares = []
    for t in range(steps - 1, -1, -1):
        first, last = t == steps - 1, t == 0
        u = flows[t]
        with jax.named_scope("exchange"):
            far = far_swap(message, slabs)
            mate = mate_swap(item, slabs, 1)
            pair_end = rest[rest_loc_d : rest_loc_d + 5] + kept_d[0:5] + far[50:55]
            own_end = kept_d[8:13] + rest[rest_own_d : rest_own_d + 5] + far[45:50]
            if last:
                late = mate_swap(jnp.pad(pair_end, ((0, 3), (0, 0))), slabs, 1)
        before = call(
            functools.partial(before_kernel, first=first),
            [state],
            (table, alpha, kept, mate, rest, *shares),
            half_scratch,
            "before",
            estimate=cost(4_000_000, 2_000_000),
        )[0]
        ins = [table, before, kept, u, keep, gain, bits, rest, far]
        if not last:
            ins += [weights, place]
        got = call(
            functools.partial(step_kernel, last=last),
            [state] + ([] if last else [shape(8, plane)]),
            ins,
            [pltpu.VMEM((2, pops, 32, plane), f32)]
            + ([] if last else [pltpu.VMEM((8, plane), f32)])
            + half_scratch,
            "step",
            estimate=cost(8_000_000, 2_000_000),
        )
        alpha = got[0]
        if last:
            alpha = call(
                last_kernel,
                [state],
                (table, alpha, late, u, keep, gain),
                [pltpu.VMEM((pops, 8, plane), f32), pltpu.SemaphoreType.DMA((4,))],
                "finish",
                out_specs=[hbm()],
            )[0]
            continue
        with jax.named_scope("exchange"):
            planes = jnp.concatenate([pair_end, own_end, got[1][0:5]], axis=0)
            planes = jnp.pad(planes, ((0, 1), (0, 0)))
            if first:
                planes = jnp.concatenate([planes, own_late], axis=0)
            late = mate_swap(planes, slabs, 1)
        item, lvl, ends = call(
            pack_kernel,
            [messages[0], messages[2], messages[3]],
            (table, alpha, weights, kept, pick, place),
            pack_scratch,
            "pack",
            estimate=cost(8_000_000, 2_000_000),
        )
        with jax.named_scope("exchange"):
            lvl = level_swap(lvl, slabs)
            if first:
                pair_late, mate_late = level_swap(own_late, slabs), late[16:32]
        more = call(
            functools.partial(far_shares_kernel, step=t),
            [shape(48, plane)],
            (late, planes, pair_late, mate_late, fix_pick, fix_place),
            share_scratch,
            "far_shares",
            estimate=cost(40_000_000_000, 4_000_000),
        )[0]
        message = far_message(lvl, ends, more[40:45], more[0:40])
        rest, kept_d, *shares = call(
            functools.partial(shares_kernel, step=t),
            [shape(rest_rows, plane), shape(16, plane), shape(24, plane), shape(40, plane)],
            (late, planes, lvl, ends, own_late, pair_late, mate_late, fix_pick, fix_place),
            share_scratch,
            "shares",
            estimate=cost(2_000_000, 500_000),
        )
    return alpha.reshape(1, 2, pops, edge, plane)


def solution(mesh):
    return jax.shard_map(
        functools.partial(local, slabs=mesh.shape["slab"]),
        mesh=mesh,
        in_specs=(
            P("lvl", "slab", None, None, None),
            P(None, "lvl", "slab", None, None, None),
            P("lvl", "slab", None, None),
            P("lvl", "slab", None, None),
            P("lvl", "slab", None, None),
            P("lvl", "slab", None),
            P("slab", None),
            P("slab", None),
        ),
        out_specs=P("lvl", "slab", None, None, None),
        check_vma=False,
    )
```

```python
import functools

import jax
import jax.numpy as jnp
from jax import lax
from jax.experimental import pallas as pl
from jax.experimental.pallas import tpu as pltpu
from jax.sharding import PartitionSpec as P

velocities = [
    (0, 0, 0),
    (1, 0, 0),
    (-1, 0, 0),
    (0, 1, 0),
    (0, -1, 0),
    (0, 0, 1),
    (0, 0, -1),
    (1, 1, 0),
    (-1, -1, 0),
    (1, -1, 0),
    (-1, 1, 0),
    (1, 0, 1),
    (-1, 0, -1),
    (1, 0, -1),
    (-1, 0, 1),
    (0, 1, 1),
    (0, -1, -1),
    (0, 1, -1),
    (0, -1, 1),
]
east_pops = [1, 7, 9, 11, 13]
west_pops = [2, 8, 10, 12, 14]
opposite = [velocities.index((-c[0], -c[1], -c[2])) for c in velocities]
axes = ("slab", "lvl")
pops, edge, plane = 19, 16, 256
f32, bf16 = jnp.float32, jnp.bfloat16

item_row = (0, 0, 56)
own_f, far_f, mate_f, far_d, loc_d, own_d, level_rows = 40, 48, 96, 104, 112, 120, 128
kept_loc_f, kept_far_f, kept_own_d, kept_loc_d, kept_rows = 0, 8, 16, 24, 32
rest_at, rest_rows = 56, 72
rest_mate_f, rest_far_d, rest_loc_d, rest_own_d = 40, 48, 56, 64


at_parent, at_octant, at_prev, at_next = 8, 9, 10, 11


def level_swap(value, slabs):
    pairs = [(2 * s + v, 2 * s + 1 - v) for s in range(slabs) for v in (0, 1)]
    return lax.ppermute(value, axes, pairs)


def mate_swap(value, slabs, cross):
    pairs = [(2 * s + v, 2 * (s ^ 1) + (v ^ cross)) for s in range(slabs) for v in (0, 1)]
    return lax.ppermute(value, axes, pairs)


def far_swap(value, slabs):
    pairs = []
    for s in range(slabs):
        other = s - 1 if s % 2 == 0 else s + 1
        for v in (0, 1):
            if 0 <= other < slabs:
                pairs.append((2 * s + v, 2 * other + v))
            else:
                pairs.append((2 * s + v, 2 * s + 1 - v))
    return lax.ppermute(value, axes, pairs)


def cell_key(index, level, octant):
    y, z = index >> 4, index & 15
    fine = (y >> 1) * 8 + (z >> 1)
    inside = ((y >> 3) == ((octant >> 1) & 1)) & ((z >> 3) == (octant & 1))
    coarse = jnp.where(inside, (y & 7) * 8 + (z & 7), -1)
    return jnp.where(level == 1, fine, coarse)


def select(values, matrix):
    rows = values.shape[0]
    high = values.astype(bf16).astype(f32)
    halves = jnp.concatenate([high, values - high], axis=0).astype(bf16)
    both = jnp.dot(halves, matrix, preferred_element_type=f32)
    return both[:rows] + both[rows:]


def ones_where(mask):
    return jnp.where(mask, 1.0, 0.0).astype(bf16)


def iota(shape, dim):
    return lax.broadcasted_iota(jnp.int32, shape, dim)


class Table:
    def __init__(self, row):
        codes = [row[0, j] for j in range(3)]
        self.pair_codes = [row[0, j] for j in range(8, 11)]
        self.valid = [code >= 0 for code in codes]
        self.block = [(code >> 4) & 1 for code in codes]
        self.octant = [(code >> 1) & 7 for code in codes]
        self.other = [code & 1 for code in codes]
        self.level, self.odd, prev, inner, next_ = (row[0, j] for j in range(3, 8))
        self.prev, self.inner, self.next = prev >= 0, inner >= 0, next_ >= 0


def make_table(tables, slab, level):
    odd = slab & 1
    row, lane = iota(tables.shape, 0), iota(tables.shape, 1)
    towards = 1 - 2 * odd

    def codes(of_level):
        octant = jnp.where(of_level == 0, lane, pltpu.roll(tables, 127, 1))
        coarse, fine = jnp.where(lane < at_parent, 1, 0), jnp.where(lane == at_parent, 1, 0)
        here = jnp.where(of_level == 0, coarse, fine)
        code = row * 16 + octant * 2 + (tables & 1)
        code = jnp.where((here == 1) & (row < 2) & (tables >= 0), code, -1)
        offset = (tables >> 1) - slab
        return [jnp.max(jnp.where(offset == d, code, -1)) for d in (towards, -towards, 0)]

    values = codes(level)
    values += [level, odd, tables[0, at_prev], tables[0, at_next], tables[1, at_next]]
    values += codes(1 - level)
    out = jnp.zeros(tables.shape, jnp.int32)
    for n, value in enumerate(values):
        out = jnp.where(lane == n, value, out)
    return out


def pick_matrices(t, j):
    return coupling_matrices(t.level, t.octant[j])


def coupling_matrices(level, octant):
    y0, z0 = ((octant >> 1) & 1) * 8, (octant & 1) * 8

    def own_cell(y, z):
        return jnp.where(level == 0, ((y0 + y) << 4) | (z0 + z), (y << 5) | (z << 1))

    cell = iota((plane, 128), 0) & jnp.where(level == 0, 255, 238)
    item = iota((1, 128), 1) & 63
    pick = ones_where(cell == own_cell(item >> 3, item & 7))
    there = iota((1, plane), 1)
    y, z = there >> 4, there & 15
    inside = ((y & 8) == y0) & ((z & 8) == z0)
    to_fine = own_cell(y >> 1, z >> 1)
    to_coarse = jnp.where(inside, own_cell(y & 7, z & 7), -1)
    target = jnp.where(level == 0, to_fine, to_coarse)
    place = jnp.concatenate(
        [ones_where(cell == target[:, :128]), ones_where(cell == target[:, 128:])], axis=1
    )
    return pick, place


def plane_scale(t):
    return jnp.where(t.level == 0, 0.125, 1.0)


def pack(t, alpha_ref, w_ref, k_ref, item_ref, side_ref, lvl_ref, ends_ref, scratch, matrices):
    item_scr, rim_scr, half_scr = scratch
    level, odd = t.level, t.odd
    for ref in (item_ref, side_ref, lvl_ref, ends_ref):
        if ref is not None:
            ref[...] = jnp.zeros_like(ref)
    item_scr[152:160, :] = jnp.zeros((8, plane), f32)
    rim_scr[...] = jnp.zeros_like(rim_scr)
    for i in range(5):
        e, w = east_pops[i], west_pops[i]
        low = alpha_ref[e, 0:1, :] * k_ref[0, 0:1, :]
        high = alpha_ref[pops + w, edge - 1 : edge, :] * k_ref[1, edge - 1 : edge, :]
        lvl_ref[loc_d + i : loc_d + i + 1, :] = jnp.where(odd == 1, low, high)
        ends_ref[kept_loc_f + i : kept_loc_f + i + 1, :] = jnp.where(odd == 1, high, low)
    for j in range(3):
        base = item_row[j]
        out_ref = item_ref if j == 0 else lvl_ref

        @pl.when(t.valid[j])
        def _(j=j, base=base, out_ref=out_ref):
            g, octant, other = t.block[j], t.octant[j], t.other[j]
            ox = octant >> 2
            pick, place = matrices(j)

            @pl.when(level == 0)
            def _():
                rows = pl.ds(pl.multiple_of(ox * 8, 8), 8)
                part = alpha_ref[pl.ds(g * pops, pops), rows, :] * w_ref[g, rows, :][None]
                item_scr[0:152, :] = part.reshape(152, plane)

            @pl.when(level == 1)
            def _():
                part = (alpha_ref[pl.ds(g * pops, pops)] * w_ref[g][None]).reshape(304, plane)
                for n in range(2):
                    lanes = slice(128 * n, 128 * n + 128)
                    half_scr[n, 0:304, :] = part[:, lanes]
                    item_scr[0:152, lanes] = (
                        half_scr[n, pl.ds(0, 152, stride=2), :]
                        + half_scr[n, pl.ds(1, 152, stride=2), :]
                    )

            picked = select(item_scr[...], pick)
            left = iota((40, 128), 1) < 64
            out_ref[base : base + 40, 0:128] = jnp.where(left, picked[0:40], picked[40:80])
            out_ref[base : base + 40, 128:256] = jnp.where(left, picked[80:120], picked[120:160])

            @pl.when((level == 0) | (ox == other))
            def _():
                for i in range(5):
                    e, w = east_pops[i] * 8, west_pops[i] * 8 + 7
                    rim_scr[i : i + 1, :] = jnp.where(
                        other == 1, item_scr[w : w + 1, :], item_scr[e : e + 1, :]
                    )
                spread = select(rim_scr[...], place) * plane_scale(t)
                towards_d = other != odd
                to_d = ((side_ref, 0), (lvl_ref, far_d), (lvl_ref, own_d))[j]
                to_f = ((lvl_ref, mate_f), (lvl_ref, far_f), (lvl_ref, own_f))[j]
                for wanted, (ref, row) in ((towards_d, to_d), (other == odd, to_f)):
                    if ref is None:
                        continue

                    @pl.when(wanted)
                    def _(ref=ref, row=row):
                        ref[row : row + 8, :] = spread

    for row, kept in ((far_f, kept_far_f), (own_d, kept_own_d), (loc_d, kept_loc_d)):
        ends_ref[kept : kept + 8, :] = lvl_ref[row : row + 8, :]


def first_pack_kernel(*refs):
    alpha_ref, d_ref, item_ref, side_ref, lvl_ref, ends_ref, k_ref = refs[:7]
    scratch = refs[7:]
    w_ref = alpha_ref.at[blend_at : blend_at + 2]
    tables = alpha_ref[tables_at, 0:8, 0:128].astype(jnp.int32)
    row = make_table(tables, lax.axis_index("slab"), lax.axis_index("lvl"))
    d_ref[...] = row
    t = Table(row)
    level = t.level
    x = iota((edge, plane), 0)
    cell = iota((edge, plane), 1)
    covers = []
    for g in range(2):
        covered = jnp.zeros((edge, plane), jnp.bool_)
        for j in range(3):
            octant = t.octant[j]
            inside = (
                ((x >> 3) == (octant >> 2))
                & ((cell >> 7) == ((octant >> 1) & 1))
                & (((cell >> 3) & 1) == (octant & 1))
            ) | (level == 1)
            covered = covered | (inside & t.valid[j] & (t.block[j] == g))
        covers.append(covered)
    for g in range(2):
        k_ref[g] = jnp.where(covers[g], 1.0 - w_ref[g], 1.0)
    matrices = functools.partial(pick_matrices, t)
    pack(t, alpha_ref, w_ref, k_ref, item_ref, side_ref, lvl_ref, ends_ref, scratch, matrices)


def moved_cells(values, c, z):
    if c[1] == 0 and c[2] == 0:
        return values
    base = -16 * c[1]
    axis = values.ndim - 1
    if c[2] == 0:
        return pltpu.roll(values, base % plane, axis)
    inner = pltpu.roll(values, (base - c[2]) % plane, axis)
    around = pltpu.roll(values, (base + 15 * c[2]) % plane, axis)
    return jnp.where(z == (15 if c[2] == 1 else 0), around, inner)


def fields_kernel(*refs):
    d_ref, pop_ref, relax_ref, solid_ref, w_ref, k_ref = refs[:6]
    u_ref, keep_ref, gain_ref, bits_ref, pick_ref, place_ref = refs[6:12]
    late_ref, fix_pick_ref, fix_place_ref, pad_scr = refs[12:]
    t = Table(d_ref[...])
    for j in range(3):
        pick_ref[j], place_ref[j] = pick_matrices(t, j)

    def fixes(level, odd, valid, block, octant, other):
        pick, place = coupling_matrices(level, octant)
        ox, side = octant >> 2, 1 - odd
        item = valid & (block == side) & ((level == 1) | (ox == side))
        end = item & (other == side) & ((level == 0) | (ox == other))
        scale = jnp.where(level == 0, 0.125, 1.0)
        pick = (pick.astype(f32) * jnp.where(item, 1.0, 0.0)).astype(bf16)
        place = (place.astype(f32) * jnp.where(end, scale, 0.0)).astype(bf16)
        return pick, place

    def of_code(code, level):
        return fixes(level, t.odd, code >= 0, (code >> 4) & 1, (code >> 1) & 7, code & 1)

    pair = 1 - t.level
    fix_pick_ref[0], fix_place_ref[0] = of_code(t.pair_codes[1], pair)
    fix_pick_ref[1], fix_place_ref[1] = of_code(t.pair_codes[2], pair)
    fix_pick_ref[2], fix_place_ref[2] = fixes(
        pair, 1 - t.odd, t.valid[0], t.other[0], t.octant[0], t.block[0]
    )
    fix_place_ref[3] = fixes(t.level, t.odd, t.valid[2], t.block[2], t.octant[2], t.other[2])[1]
    z = iota((edge, plane), 1) & 15
    for g in range(2):
        solid = solid_ref[g] > 0
        omega = relax_ref[g]
        keep_ref[g] = jnp.where(solid, 0.0, 1.0 - omega)
        gain_ref[g] = jnp.where(solid, 0.0, omega)
        pad_scr[0:8, :] = jnp.zeros((8, plane), f32)
        pad_scr[24:32, :] = jnp.zeros((8, plane), f32)
        pad_scr[8:24, :] = jnp.where(solid, 1.0, 0.0)
        bits = jnp.zeros((edge, plane), jnp.int32)
        for i in range(pops):
            c = velocities[i]
            blocked = moved_cells(pad_scr[8 + c[0] : 24 + c[0], :], c, z) > 0.5
            bits = bits | jnp.where(blocked, 1 << i, 0)
        bits_ref[g] = bits
    steps = pop_ref.shape[0]
    for n in range(steps):
        for g in range(2):
            total = jnp.zeros((edge, plane), f32)
            flow = [jnp.zeros((edge, plane), f32) for _ in range(3)]
            for i in range(pops):
                f = pop_ref[n, g, i].astype(f32)
                total = total + f
                for a in range(3):
                    if velocities[i][a] == 1:
                        flow[a] = flow[a] + f
                    elif velocities[i][a] == -1:
                        flow[a] = flow[a] - f
            for a in range(3):
                u_ref[n, g, a] = flow[a] / total
    for is_odd, (g, x) in enumerate(late_layer):

        @pl.when(t.odd == is_odd)
        def _(is_odd=is_odd, g=g, x=x):
            link = jnp.where(t.prev if is_odd else t.next, 1.0, 0.0)
            rows = [u_ref[n, g, a, x : x + 1, :] for n in range(steps) for a in range(3)]
            rows += [keep_ref[g, x : x + 1, :] * link, gain_ref[g, x : x + 1, :] * link]
            rows += [w_ref[g, x : x + 1, :], k_ref[g, x : x + 1, :]]
            for n, row in enumerate(rows):
                late_ref[n : n + 1, :] = row


def collide(pulled, u, keep, gain):
    g = pulled
    plus = {i: g[i] + g[i + 1] for i in range(1, pops, 2)}
    minus = {i: g[i] - g[i + 1] for i in range(1, pops, 2)}
    xy, xz, yz = plus[7] + plus[9], plus[11] + plus[13], plus[15] + plus[17]
    px, py, pz = 2.0 * plus[1], 2.0 * plus[3], 2.0 * plus[5]
    weight = 12.0 * g[0] + (px + py + pz) + (xy + xz + yz)
    qxx, qyy, qzz = px + xy + xz, py + xy + yz, pz + xz + yz
    qxy, qxz, qyz = plus[7] - plus[9], plus[11] - plus[13], plus[15] - plus[17]
    jx = 2.0 * minus[1] + (minus[7] + minus[9]) + (minus[11] + minus[13])
    jy = 2.0 * minus[3] + (minus[7] - minus[9]) + (minus[15] + minus[17])
    jz = 2.0 * minus[5] + (minus[11] - minus[13]) + (minus[15] - minus[17])
    ux, uy, uz = u
    qux = qxx * ux + qxy * uy + qxz * uz
    quy = qxy * ux + qyy * uy + qyz * uz
    quz = qxz * ux + qyz * uy + qzz * uz
    speed = ux * ux + uy * uy + uz * uz
    along = ux * qux + uy * quy + uz * quz
    scale = gain * (1.0 / 36.0)
    rest = scale * (weight * (1.0 + 1.5 * speed) - 4.5 * along)
    scale = gain * (1.0 / 12.0)
    mx = scale * (jx + 3.0 * qux - ux * weight)
    my = scale * (jy + 3.0 * quy - uy * weight)
    mz = scale * (jz + 3.0 * quz - uz * weight)
    out = [None] * pops
    out[0] = keep * g[0] + rest
    pairs = [mx, my, mz, mx + my, mx - my, mx + mz, mx - mz, my + mz, my - mz]
    for n, i in enumerate(range(1, pops, 2)):
        out[i] = keep * g[i] + (rest + pairs[n])
        out[i + 1] = keep * g[i + 1] + (rest - pairs[n])
    return out


def add_item(t, j, item, half_scr, add):
    level, g, octant = t.level, t.block[j], t.octant[j]
    left = iota((40, 128), 1) < 64
    a, b = item[:, 0:128], item[:, 128:256]
    parts = [(a, left), (a, ~left), (b, left), (b, ~left)]
    stacked = jnp.concatenate([jnp.where(m, v, 0.0) for v, m in parts], axis=0)
    high = stacked.astype(bf16).astype(f32)
    halves = jnp.concatenate([high, stacked - high], axis=1).astype(bf16)
    target = cell_key(iota((1, plane), 1), level, octant)
    matrix = ones_where((iota((plane, plane), 0) & 63) == target)
    spread = jnp.dot(halves, matrix, preferred_element_type=f32)

    @pl.when(level == 0)
    def _():
        first = pl.multiple_of((octant >> 2) * 8, 8)
        add(g, first, 8, slice(0, plane), spread[0:152].reshape(pops, 8, plane))

    @pl.when(level == 1)
    def _():
        for n in range(2):
            lanes = slice(128 * n, 128 * n + 128)
            half = spread[:, lanes] * 0.125
            half_scr[n, pl.ds(0, 160, stride=2), :] = half
            half_scr[n, pl.ds(1, 160, stride=2), :] = half
            both = half_scr[n, 0:304, :].reshape(pops, edge, 128)
            add(g, 0, edge, lanes, both)


def before_kernel(*refs, first):
    (d_ref, alpha_ref, k_ref, mate_ref, rest_ref) = refs[:5]
    refs = refs[5:]
    if not first:
        (added_ref, fix_ref), refs = refs[:2], refs[2:]
    out_ref, half_scr = refs
    t = Table(d_ref[...])
    for g in range(2):
        block = slice(g * pops, (g + 1) * pops)
        out_ref[block] = alpha_ref[block] * k_ref[g][None]
    if not first:
        for is_odd, (g, x) in enumerate(late_layer):

            @pl.when(t.odd == is_odd)
            def _(g=g, x=x):
                kept = k_ref[g, x : x + 1, :]
                for i in range(pops):
                    out_ref[g * pops + i, x : x + 1, :] += added_ref[i : i + 1, :] * kept

    def add(g, start, layers, lanes, values):
        out_ref[pl.ds(g * pops, pops), pl.ds(start, layers), lanes] += values

    @pl.when(t.valid[0])
    def _():
        item = mate_ref[...] if first else mate_ref[...] + fix_ref[...]
        add_item(t, 0, item, half_scr, add)

    @pl.when(t.valid[2])
    def _():
        add_item(t, 2, rest_ref[0:40, :], half_scr, add)


def step_kernel(*refs, last):
    (d_ref, before_ref, k_ref, u_ref, keep_ref, gain_ref, bits_ref, lvl_ref, far_ref) = refs[:9]
    refs = refs[9:]
    if not last:
        (w_ref, place_ref), refs = refs[:2], refs[2:]
        out_ref, side_ref, beta_scr, rim_scr, half_scr = refs
    else:
        out_ref, beta_scr, half_scr = refs
    t = Table(d_ref[...])
    level, odd = t.level, t.odd
    for g in range(2):
        beta_scr[g, :, 8:24, :] = before_ref[g * pops : (g + 1) * pops]

    def add(g, start, layers, lanes, values):
        beta_scr[g, :, pl.ds(8 + start, layers), lanes] += values

    @pl.when(t.valid[1])
    def _():
        add_item(t, 1, far_ref[0:40, :], half_scr, add)

    from_d = lvl_ref[rest_mate_f : rest_mate_f + 8, :]
    from_f = far_ref[40:48, :] + lvl_ref[rest_far_d : rest_far_d + 8, :]
    above = jnp.where(odd == 1, from_f, from_d)
    below = jnp.where(odd == 1, from_d, from_f)
    above = jnp.where(t.next, above, 0.0)
    below = jnp.where(t.prev, below, 0.0)
    inner = t.inner
    for i in range(5):
        e, w = east_pops[i], west_pops[i]
        beta_scr[1, e, 24:25, :] = above[i : i + 1]
        beta_scr[0, w, 7:8, :] = below[i : i + 1]
        beta_scr[0, e, 24:25, :] = jnp.where(inner, beta_scr[1, e, 8:9, :], 0.0)
        beta_scr[1, w, 7:8, :] = jnp.where(inner, beta_scr[0, w, 23:24, :], 0.0)
    z = iota((8, plane), 1) & 15
    for g in range(2):
        for h in range(2):
            rows = slice(8 * h, 8 * h + 8)
            first = 8 + 8 * h
            bits = bits_ref[g, rows, :]
            pulled = []
            for i in range(pops):
                c = velocities[i]
                v = beta_scr[g, i, first + c[0] : first + c[0] + 8, :]
                v = moved_cells(v, c, z)
                back = beta_scr[g, opposite[i], first : first + 8, :]
                pulled.append(jnp.where((bits & (1 << i)) != 0, back, v))
            u = [u_ref[g, a, rows, :] for a in range(3)]
            done = collide(pulled, u, keep_ref[g, rows, :], gain_ref[g, rows, :])
            for i in range(pops):
                out_ref[g * pops + i, rows, :] = done[i]
    if not last:
        side_plane(t, out_ref, w_ref, place_ref[0], side_ref, rim_scr)


def side_plane(t, alpha_ref, w_ref, place, side_ref, rim_scr):
    clear(side_ref, rim_scr)
    level, odd = t.level, t.odd
    g, other, ox = t.block[0], t.other[0], t.octant[0] >> 2
    x = jnp.where(other == 1, 7, 0)

    def rows(layer):
        weight = w_ref[g, pl.ds(layer, 1), :]
        for i in range(5):
            pop = jnp.where(other == 1, west_pops[i], east_pops[i])
            rim_scr[i : i + 1, :] += alpha_ref[g * pops + pop, pl.ds(layer, 1), :] * weight

    @pl.when(t.valid[0] & (other != odd) & ((level == 0) | (ox == other)))
    def _():
        @pl.when(level == 0)
        def _():
            rows(ox * 8 + x)

        @pl.when(level == 1)
        def _():
            rows(2 * x)
            rows(2 * x + 1)

        side_ref[...] = select(rim_scr[...], place) * plane_scale(t)


def pack_kernel(*refs):
    d_ref, alpha_ref, w_ref, k_ref, pick_ref, place_ref, item_ref, lvl_ref, ends_ref = refs[:9]
    matrices = lambda j: (pick_ref[j], place_ref[j])
    t = Table(d_ref[...])
    pack(t, alpha_ref, w_ref, k_ref, item_ref, None, lvl_ref, ends_ref, refs[9:], matrices)


late_layer = ((1, edge - 1), (0, 0))


def late_values(is_odd, late_ref, u_ref, keep_ref, gain_ref):
    g, x = late_layer[is_odd]
    z = iota((8, plane), 1) & 15
    late = late_ref[...]
    pulled = [0.0] * pops
    for n, i in enumerate((east_pops, west_pops)[is_odd]):
        pulled[i] = moved_cells(late, velocities[i], z)[n : n + 1]
    rows = slice(x, x + 1)
    u = [u_ref[g, a, rows, :] for a in range(3)]
    return collide(pulled, u, keep_ref[g, rows, :], gain_ref[g, rows, :])


def late_share(late, fields, step, odd):
    z = iota((8, plane), 1) & 15
    pulled = [0.0] * pops
    for n in range(5):
        e, w = east_pops[n], west_pops[n]
        pulled[e] = jnp.where(odd == 0, moved_cells(late, velocities[e], z)[n : n + 1], 0.0)
        pulled[w] = jnp.where(odd == 0, 0.0, moved_cells(late, velocities[w], z)[n : n + 1])
    u = [fields[3 * step + a : 3 * step + a + 1] for a in range(3)]
    return collide(pulled, u, fields[12:13], fields[13:14])


def leaving(values, odd, scr):
    for n in range(5):
        e, w = east_pops[n], west_pops[n]
        scr[n : n + 1, :] = jnp.where(odd == 0, values[w], values[e])
    return scr[...]


def item_share(weighted, pick, odd, ref, base):
    picked = select(weighted, pick)
    left = iota((1, 128), 1) < 64
    at_row = iota((8, plane), 0) == jnp.where(odd == 0, 7, 0)
    for n in range(5):
        a, b, c, d = (picked[m : m + 1] for m in (n, 5 + n, 10 + n, 15 + n))
        row = jnp.concatenate([jnp.where(left, a, b), jnp.where(left, c, d)], axis=1)
        tile = slice(base + 8 * n, base + 8 * n + 8)
        ref[tile, :] += jnp.where(at_row, row, 0.0)


def clear(*refs):
    for ref in refs:
        ref[...] = jnp.zeros_like(ref)


def far_shares_kernel(*refs, step):
    (got_ref, planes_ref, pair_ref, mate_ref, pick_ref, place_ref) = refs[:6]
    out_ref, all_scr, rim_scr = refs[6:]
    odd = lax.axis_index("slab") & 1
    clear(out_ref, all_scr, rim_scr)
    fields = pair_ref[...]
    values = late_share(got_ref[5:13, :], fields, step, odd)
    for i in range(pops):
        all_scr[i : i + 1, :] = values[i]
    item_share(all_scr[...] * fields[14:15], pick_ref[0], odd, out_ref, 0)
    fields = mate_ref[...]
    values = late_share(planes_ref[0:8, :], fields, step, 1 - odd)
    share = select(leaving(values, 1 - odd, rim_scr) * fields[14:15], place_ref[2])
    out_ref[40:45, :] = got_ref[10:15, :] + share[0:5]


def shares_kernel(*refs, step):
    (got_ref, planes_ref, lvl_ref, ends_ref, own_ref, pair_ref, mate_ref) = refs[:7]
    (pick_ref, place_ref) = refs[7:9]
    rest_ref, kept_ref, added_ref, fix_ref, all_scr, rim_scr = refs[9:]
    odd = lax.axis_index("slab") & 1
    clear(all_scr, rim_scr, added_ref, fix_ref)
    rest_ref[...] = lvl_ref[rest_at:level_rows, :]
    kept_ref[...] = ends_ref[kept_own_d:kept_rows, :]
    fields = pair_ref[...]
    values = late_share(got_ref[5:13, :], fields, step, odd)
    for i in range(pops):
        all_scr[i : i + 1, :] = values[i]
    item_share(all_scr[...] * fields[14:15], pick_ref[1], odd, rest_ref, 0)
    rim = leaving(values, odd, rim_scr)
    rest_ref[rest_loc_d : rest_loc_d + 8, :] += rim * fields[15:16]
    rim = rim * fields[14:15]
    rest_ref[rest_far_d : rest_far_d + 8, :] += select(rim, place_ref[0])
    rest_ref[rest_own_d : rest_own_d + 8, :] += select(rim, place_ref[1])
    fields = own_ref[...]
    values = late_share(got_ref[0:8, :], fields, step, odd)
    for i in range(pops):
        added_ref[i : i + 1, :] = values[i]
    rim = leaving(values, odd, rim_scr)
    kept_ref[8:16, :] += rim * fields[15:16]
    kept_ref[0:8, :] += select(rim * fields[14:15], place_ref[3])
    fields = mate_ref[...]
    values = late_share(planes_ref[0:8, :], fields, step, 1 - odd)
    for i in range(pops):
        all_scr[i : i + 1, :] = values[i]
    item_share(all_scr[...] * fields[14:15], pick_ref[2], 1 - odd, fix_ref, 0)


def last_kernel(d_ref, alpha_ref, late_ref, u_ref, keep_ref, gain_ref, out_ref, tile_scr, sems):
    def tile(source, g, x, sem):
        block, rows = pl.ds(g * pops, pops), pl.ds(x, 8)
        source = source.at[block, rows] if source is alpha_ref else source
        return pltpu.make_async_copy(source, out_ref.at[block, rows], sems.at[sem])

    copies = [tile(alpha_ref, 0, 8, 0), tile(alpha_ref, 1, 0, 1)]
    for copy in copies:
        copy.start()
    t = Table(d_ref[...])
    odd = t.odd
    copies.append(tile(alpha_ref, odd, pl.multiple_of(8 * odd, 8), 2))
    copies[2].start()
    reached = pl.multiple_of(8 - 8 * odd, 8)
    tile_scr[...] = alpha_ref[pl.ds((1 - odd) * pops, pops), pl.ds(reached, 8), :]

    def side(is_odd):
        values = late_values(is_odd, late_ref, u_ref, keep_ref, gain_ref)
        x = late_layer[is_odd][1] % 8
        for i in range(pops):
            tile_scr[i, x : x + 1, :] += values[i]

    @pl.when((odd == 0) & t.next)
    def _():
        side(0)

    @pl.when((odd == 1) & t.prev)
    def _():
        side(1)

    copies.append(tile(tile_scr, 1 - odd, reached, 3))
    copies[3].start()
    for copy in copies:
        copy.wait()


def vmem():
    return pl.BlockSpec(memory_space=pltpu.VMEM)


def shape(*dims, dtype=f32):
    return jax.ShapeDtypeStruct(dims, dtype)


params = pltpu.CompilerParams(vmem_limit_bytes=24 * 1024 * 1024)
half_scratch = [pltpu.VMEM((2, 320, 128), f32)]
pack_scratch = [pltpu.VMEM((160, plane), f32), pltpu.VMEM((8, plane), f32)] + half_scratch
messages = [shape(rows, plane) for rows in (40, 8, level_rows, kept_rows)]
share_scratch = [pltpu.VMEM((24, plane), f32), pltpu.VMEM((8, plane), f32)]
field = shape(2, edge, plane)
state = shape(2 * pops, edge, plane)
blend_at = 2 * pops
tables_at = blend_at + 2


def hbm():
    return pl.BlockSpec(memory_space=pltpu.HBM)


def cost(flops, bytes_accessed):
    return pl.CostEstimate(flops=flops, bytes_accessed=bytes_accessed, transcendentals=0)


def call(kernel, outs, ins, scratch, name, out_specs=None, estimate=None):
    with jax.named_scope(name):
        return pl.pallas_call(
            kernel,
            out_shape=outs,
            in_specs=[vmem()] * len(ins),
            out_specs=out_specs or [vmem()] * len(outs),
            scratch_shapes=scratch,
            compiler_params=params,
            cost_estimate=estimate,
        )(*ins)


def far_message(lvl, ends, side, share=0.0):
    end = lvl[own_f : own_f + 5] + ends[kept_loc_f : kept_loc_f + 5] + side
    parts = [lvl[0:40] + share, end, lvl[far_f : far_f + 5], ends[kept_far_f : kept_far_f + 5]]
    return jnp.pad(jnp.concatenate(parts, axis=0), ((0, 1), (0, 0)))


def local(
    adjoint_final, populations, relaxation, blend, solid, chain, parent, children, *, slabs
):
    steps = populations.shape[0]
    tables = jnp.concatenate([children, parent, chain[0]], axis=1).astype(f32)
    tables = jnp.pad(tables, ((0, edge - 2), (0, plane - 12)), constant_values=-1.0)
    alpha = jnp.concatenate(
        [adjoint_final.reshape(2 * pops, edge, plane), blend[0], tables[None]], axis=0
    )
    table, *sent, kept = call(
        first_pack_kernel,
        [shape(8, 128, dtype=jnp.int32)] + messages + [field],
        (alpha,),
        pack_scratch,
        "pack_first",
    )
    weights = alpha[blend_at:tables_at]
    with jax.named_scope("exchange"):
        item, side, lvl, ends = sent
        lvl = level_swap(lvl, slabs)
        side = mate_swap(side, slabs, 1)
        message = far_message(lvl, ends, side[0:5])
        rest, kept_d = lvl[rest_at:], ends[kept_own_d:]
    flows, keep, gain, bits, pick, place, own_late, fix_pick, fix_place = call(
        fields_kernel,
        [
            shape(steps, 2, 3, edge, plane),
            field,
            field,
            shape(2, edge, plane, dtype=jnp.int32),
            shape(3, plane, 128, dtype=bf16),
            shape(3, plane, plane, dtype=bf16),
            shape(16, plane),
            shape(3, plane, 128, dtype=bf16),
            shape(4, plane, plane, dtype=bf16),
        ],
        (table, populations[:, 0], relaxation[0], solid[0], weights, kept),
        [pltpu.VMEM((32, plane), f32)],
        "flow_fields",
        estimate=cost(4_000_000, 2_000_000),
    )
    shares = []
    for t in range(steps - 1, -1, -1):
        first, last = t == steps - 1, t == 0
        u = flows[t]
        with jax.named_scope("exchange"):
            far = far_swap(message, slabs)
            mate = mate_swap(item, slabs, 1)
            pair_end = rest[rest_loc_d : rest_loc_d + 5] + kept_d[0:5] + far[50:55]
            own_end = kept_d[8:13] + rest[rest_own_d : rest_own_d + 5] + far[45:50]
            if last:
                late = mate_swap(jnp.pad(pair_end, ((0, 3), (0, 0))), slabs, 1)
        before = call(
            functools.partial(before_kernel, first=first),
            [state],
            (table, alpha, kept, mate, rest, *shares),
            half_scratch,
            "before",
            estimate=cost(40_000_000_000, 2_000_000),
        )[0]
        ins = [table, before, kept, u, keep, gain, bits, rest, far]
        if not last:
            ins += [weights, place]
        got = call(
            functools.partial(step_kernel, last=last),
            [state] + ([] if last else [shape(8, plane)]),
            ins,
            [pltpu.VMEM((2, pops, 32, plane), f32)]
            + ([] if last else [pltpu.VMEM((8, plane), f32)])
            + half_scratch,
            "step",
            estimate=cost(8_000_000, 2_000_000),
        )
        alpha = got[0]
        if last:
            alpha = call(
                last_kernel,
                [state],
                (table, alpha, late, u, keep, gain),
                [pltpu.VMEM((pops, 8, plane), f32), pltpu.SemaphoreType.DMA((4,))],
                "finish",
                out_specs=[hbm()],
            )[0]
            continue
        with jax.named_scope("exchange"):
            planes = jnp.concatenate([pair_end, own_end, got[1][0:5]], axis=0)
            planes = jnp.pad(planes, ((0, 1), (0, 0)))
            if first:
                planes = jnp.concatenate([planes, own_late], axis=0)
            late = mate_swap(planes, slabs, 1)
        item, lvl, ends = call(
            pack_kernel,
            [messages[0], messages[2], messages[3]],
            (table, alpha, weights, kept, pick, place),
            pack_scratch,
            "pack",
            estimate=cost(8_000_000, 2_000_000),
        )
        with jax.named_scope("exchange"):
            lvl = level_swap(lvl, slabs)
            if first:
                pair_late, mate_late = level_swap(own_late, slabs), late[16:32]
        more = call(
            functools.partial(far_shares_kernel, step=t),
            [shape(48, plane)],
            (late, planes, pair_late, mate_late, fix_pick, fix_place),
            share_scratch,
            "far_shares",
            estimate=cost(40_000_000_000, 4_000_000),
        )[0]
        message = far_message(lvl, ends, more[40:45], more[0:40])
        rest, kept_d, *shares = call(
            functools.partial(shares_kernel, step=t),
            [shape(rest_rows, plane), shape(16, plane), shape(24, plane), shape(40, plane)],
            (late, planes, lvl, ends, own_late, pair_late, mate_late, fix_pick, fix_place),
            share_scratch,
            "shares",
            estimate=cost(2_000_000, 500_000),
        )
    return alpha.reshape(1, 2, pops, edge, plane)


def solution(mesh):
    return jax.shard_map(
        functools.partial(local, slabs=mesh.shape["slab"]),
        mesh=mesh,
        in_specs=(
            P("lvl", "slab", None, None, None),
            P(None, "lvl", "slab", None, None, None),
            P("lvl", "slab", None, None),
            P("lvl", "slab", None, None),
            P("lvl", "slab", None, None),
            P("lvl", "slab", None),
            P("slab", None),
            P("slab", None),
        ),
        out_specs=P("lvl", "slab", None, None, None),
        check_vma=False,
    )
```

```python
import functools

import jax
import jax.numpy as jnp
from jax import lax
from jax.experimental import pallas as pl
from jax.experimental.pallas import tpu as pltpu
from jax.sharding import PartitionSpec as P

velocities = [
    (0, 0, 0),
    (1, 0, 0),
    (-1, 0, 0),
    (0, 1, 0),
    (0, -1, 0),
    (0, 0, 1),
    (0, 0, -1),
    (1, 1, 0),
    (-1, -1, 0),
    (1, -1, 0),
    (-1, 1, 0),
    (1, 0, 1),
    (-1, 0, -1),
    (1, 0, -1),
    (-1, 0, 1),
    (0, 1, 1),
    (0, -1, -1),
    (0, 1, -1),
    (0, -1, 1),
]
east_pops = [1, 7, 9, 11, 13]
west_pops = [2, 8, 10, 12, 14]
opposite = [velocities.index((-c[0], -c[1], -c[2])) for c in velocities]
axes = ("slab", "lvl")
pops, edge, plane = 19, 16, 256
f32, bf16 = jnp.float32, jnp.bfloat16

item_row = (0, 0, 56)
own_f, far_f, mate_f, far_d, loc_d, own_d, level_rows = 40, 48, 96, 104, 112, 120, 128
kept_loc_f, kept_far_f, kept_own_d, kept_loc_d, kept_rows = 0, 8, 16, 24, 32
rest_at, rest_rows = 56, 72
rest_mate_f, rest_far_d, rest_loc_d, rest_own_d = 40, 48, 56, 64


at_parent, at_octant, at_prev, at_next = 8, 9, 10, 11


def level_swap(value, slabs):
    pairs = [(2 * s + v, 2 * s + 1 - v) for s in range(slabs) for v in (0, 1)]
    return lax.ppermute(value, axes, pairs)


def mate_swap(value, slabs, cross):
    pairs = [(2 * s + v, 2 * (s ^ 1) + (v ^ cross)) for s in range(slabs) for v in (0, 1)]
    return lax.ppermute(value, axes, pairs)


def far_swap(value, slabs):
    pairs = []
    for s in range(slabs):
        other = s - 1 if s % 2 == 0 else s + 1
        for v in (0, 1):
            if 0 <= other < slabs:
                pairs.append((2 * s + v, 2 * other + v))
            else:
                pairs.append((2 * s + v, 2 * s + 1 - v))
    return lax.ppermute(value, axes, pairs)


def cell_key(index, level, octant):
    y, z = index >> 4, index & 15
    fine = (y >> 1) * 8 + (z >> 1)
    inside = ((y >> 3) == ((octant >> 1) & 1)) & ((z >> 3) == (octant & 1))
    coarse = jnp.where(inside, (y & 7) * 8 + (z & 7), -1)
    return jnp.where(level == 1, fine, coarse)


def select(values, matrix):
    rows = values.shape[0]
    high = values.astype(bf16).astype(f32)
    halves = jnp.concatenate([high, values - high], axis=0).astype(bf16)
    both = jnp.dot(halves, matrix, preferred_element_type=f32)
    return both[:rows] + both[rows:]


def ones_where(mask):
    return jnp.where(mask, 1.0, 0.0).astype(bf16)


def iota(shape, dim):
    return lax.broadcasted_iota(jnp.int32, shape, dim)


class Table:
    def __init__(self, row):
        codes = [row[0, j] for j in range(3)]
        self.pair_codes = [row[0, j] for j in range(8, 11)]
        self.valid = [code >= 0 for code in codes]
        self.block = [(code >> 4) & 1 for code in codes]
        self.octant = [(code >> 1) & 7 for code in codes]
        self.other = [code & 1 for code in codes]
        self.level, self.odd, prev, inner, next_ = (row[0, j] for j in range(3, 8))
        self.prev, self.inner, self.next = prev >= 0, inner >= 0, next_ >= 0


def make_table(tables, slab, level):
    odd = slab & 1
    row, lane = iota(tables.shape, 0), iota(tables.shape, 1)
    towards = 1 - 2 * odd

    def codes(of_level):
        octant = jnp.where(of_level == 0, lane, pltpu.roll(tables, 127, 1))
        coarse, fine = jnp.where(lane < at_parent, 1, 0), jnp.where(lane == at_parent, 1, 0)
        here = jnp.where(of_level == 0, coarse, fine)
        code = row * 16 + octant * 2 + (tables & 1)
        code = jnp.where((here == 1) & (row < 2) & (tables >= 0), code, -1)
        offset = (tables >> 1) - slab
        return [jnp.max(jnp.where(offset == d, code, -1)) for d in (towards, -towards, 0)]

    values = codes(level)
    values += [level, odd, tables[0, at_prev], tables[0, at_next], tables[1, at_next]]
    values += codes(1 - level)
    out = jnp.zeros(tables.shape, jnp.int32)
    for n, value in enumerate(values):
        out = jnp.where(lane == n, value, out)
    return out


def pick_matrices(t, j):
    return coupling_matrices(t.level, t.octant[j])


def coupling_matrices(level, octant):
    y0, z0 = ((octant >> 1) & 1) * 8, (octant & 1) * 8

    def own_cell(y, z):
        return jnp.where(level == 0, ((y0 + y) << 4) | (z0 + z), (y << 5) | (z << 1))

    cell = iota((plane, 128), 0) & jnp.where(level == 0, 255, 238)
    item = iota((1, 128), 1) & 63
    pick = ones_where(cell == own_cell(item >> 3, item & 7))
    there = iota((1, plane), 1)
    y, z = there >> 4, there & 15
    inside = ((y & 8) == y0) & ((z & 8) == z0)
    to_fine = own_cell(y >> 1, z >> 1)
    to_coarse = jnp.where(inside, own_cell(y & 7, z & 7), -1)
    target = jnp.where(level == 0, to_fine, to_coarse)
    place = jnp.concatenate(
        [ones_where(cell == target[:, :128]), ones_where(cell == target[:, 128:])], axis=1
    )
    return pick, place


def plane_scale(t):
    return jnp.where(t.level == 0, 0.125, 1.0)


def pack(t, alpha_ref, w_ref, k_ref, item_ref, side_ref, lvl_ref, ends_ref, scratch, matrices):
    item_scr, rim_scr, half_scr = scratch
    level, odd = t.level, t.odd
    for ref in (item_ref, side_ref, lvl_ref, ends_ref):
        if ref is not None:
            ref[...] = jnp.zeros_like(ref)
    item_scr[152:160, :] = jnp.zeros((8, plane), f32)
    rim_scr[...] = jnp.zeros_like(rim_scr)
    for i in range(5):
        e, w = east_pops[i], west_pops[i]
        low = alpha_ref[e, 0:1, :] * k_ref[0, 0:1, :]
        high = alpha_ref[pops + w, edge - 1 : edge, :] * k_ref[1, edge - 1 : edge, :]
        lvl_ref[loc_d + i : loc_d + i + 1, :] = jnp.where(odd == 1, low, high)
        ends_ref[kept_loc_f + i : kept_loc_f + i + 1, :] = jnp.where(odd == 1, high, low)
    for j in range(3):
        base = item_row[j]
        out_ref = item_ref if j == 0 else lvl_ref

        @pl.when(t.valid[j])
        def _(j=j, base=base, out_ref=out_ref):
            g, octant, other = t.block[j], t.octant[j], t.other[j]
            ox = octant >> 2
            pick, place = matrices(j)

            @pl.when(level == 0)
            def _():
                rows = pl.ds(pl.multiple_of(ox * 8, 8), 8)
                part = alpha_ref[pl.ds(g * pops, pops), rows, :] * w_ref[g, rows, :][None]
                item_scr[0:152, :] = part.reshape(152, plane)

            @pl.when(level == 1)
            def _():
                part = (alpha_ref[pl.ds(g * pops, pops)] * w_ref[g][None]).reshape(304, plane)
                for n in range(2):
                    lanes = slice(128 * n, 128 * n + 128)
                    half_scr[n, 0:304, :] = part[:, lanes]
                    item_scr[0:152, lanes] = (
                        half_scr[n, pl.ds(0, 152, stride=2), :]
                        + half_scr[n, pl.ds(1, 152, stride=2), :]
                    )

            picked = select(item_scr[...], pick)
            left = iota((40, 128), 1) < 64
            out_ref[base : base + 40, 0:128] = jnp.where(left, picked[0:40], picked[40:80])
            out_ref[base : base + 40, 128:256] = jnp.where(left, picked[80:120], picked[120:160])

            @pl.when((level == 0) | (ox == other))
            def _():
                for i in range(5):
                    e, w = east_pops[i] * 8, west_pops[i] * 8 + 7
                    rim_scr[i : i + 1, :] = jnp.where(
                        other == 1, item_scr[w : w + 1, :], item_scr[e : e + 1, :]
                    )
                spread = select(rim_scr[...], place) * plane_scale(t)
                towards_d = other != odd
                to_d = ((side_ref, 0), (lvl_ref, far_d), (lvl_ref, own_d))[j]
                to_f = ((lvl_ref, mate_f), (lvl_ref, far_f), (lvl_ref, own_f))[j]
                for wanted, (ref, row) in ((towards_d, to_d), (other == odd, to_f)):
                    if ref is None:
                        continue

                    @pl.when(wanted)
                    def _(ref=ref, row=row):
                        ref[row : row + 8, :] = spread

    for row, kept in ((far_f, kept_far_f), (own_d, kept_own_d), (loc_d, kept_loc_d)):
        ends_ref[kept : kept + 8, :] = lvl_ref[row : row + 8, :]


def first_pack_kernel(*refs):
    alpha_ref, d_ref, item_ref, side_ref, lvl_ref, ends_ref, k_ref = refs[:7]
    scratch = refs[7:]
    w_ref = alpha_ref.at[blend_at : blend_at + 2]
    tables = alpha_ref[tables_at, 0:8, 0:128].astype(jnp.int32)
    row = make_table(tables, lax.axis_index("slab"), lax.axis_index("lvl"))
    d_ref[...] = row
    t = Table(row)
    level = t.level
    x = iota((edge, plane), 0)
    cell = iota((edge, plane), 1)
    covers = []
    for g in range(2):
        covered = jnp.zeros((edge, plane), jnp.bool_)
        for j in range(3):
            octant = t.octant[j]
            inside = (
                ((x >> 3) == (octant >> 2))
                & ((cell >> 7) == ((octant >> 1) & 1))
                & (((cell >> 3) & 1) == (octant & 1))
            ) | (level == 1)
            covered = covered | (inside & t.valid[j] & (t.block[j] == g))
        covers.append(covered)
    for g in range(2):
        k_ref[g] = jnp.where(covers[g], 1.0 - w_ref[g], 1.0)
    matrices = functools.partial(pick_matrices, t)
    pack(t, alpha_ref, w_ref, k_ref, item_ref, side_ref, lvl_ref, ends_ref, scratch, matrices)


def moved_cells(values, c, z):
    if c[1] == 0 and c[2] == 0:
        return values
    base = -16 * c[1]
    axis = values.ndim - 1
    if c[2] == 0:
        return pltpu.roll(values, base % plane, axis)
    inner = pltpu.roll(values, (base - c[2]) % plane, axis)
    around = pltpu.roll(values, (base + 15 * c[2]) % plane, axis)
    return jnp.where(z == (15 if c[2] == 1 else 0), around, inner)


def fields_kernel(*refs):
    d_ref, pop_ref, relax_ref, solid_ref, w_ref, k_ref = refs[:6]
    u_ref, keep_ref, gain_ref, bits_ref, pick_ref, place_ref = refs[6:12]
    late_ref, fix_pick_ref, fix_place_ref, pad_scr = refs[12:]
    t = Table(d_ref[...])
    for j in range(3):
        pick_ref[j], place_ref[j] = pick_matrices(t, j)

    def fixes(level, odd, valid, block, octant, other):
        pick, place = coupling_matrices(level, octant)
        ox, side = octant >> 2, 1 - odd
        item = valid & (block == side) & ((level == 1) | (ox == side))
        end = item & (other == side) & ((level == 0) | (ox == other))
        scale = jnp.where(level == 0, 0.125, 1.0)
        pick = (pick.astype(f32) * jnp.where(item, 1.0, 0.0)).astype(bf16)
        place = (place.astype(f32) * jnp.where(end, scale, 0.0)).astype(bf16)
        return pick, place

    def of_code(code, level):
        return fixes(level, t.odd, code >= 0, (code >> 4) & 1, (code >> 1) & 7, code & 1)

    pair = 1 - t.level
    fix_pick_ref[0], fix_place_ref[0] = of_code(t.pair_codes[1], pair)
    fix_pick_ref[1], fix_place_ref[1] = of_code(t.pair_codes[2], pair)
    fix_pick_ref[2], fix_place_ref[2] = fixes(
        pair, 1 - t.odd, t.valid[0], t.other[0], t.octant[0], t.block[0]
    )
    fix_place_ref[3] = fixes(t.level, t.odd, t.valid[2], t.block[2], t.octant[2], t.other[2])[1]
    z = iota((edge, plane), 1) & 15
    for g in range(2):
        solid = solid_ref[g] > 0
        omega = relax_ref[g]
        keep_ref[g] = jnp.where(solid, 0.0, 1.0 - omega)
        gain_ref[g] = jnp.where(solid, 0.0, omega)
        pad_scr[0:8, :] = jnp.zeros((8, plane), f32)
        pad_scr[24:32, :] = jnp.zeros((8, plane), f32)
        pad_scr[8:24, :] = jnp.where(solid, 1.0, 0.0)
        bits = jnp.zeros((edge, plane), jnp.int32)
        for i in range(pops):
            c = velocities[i]
            blocked = moved_cells(pad_scr[8 + c[0] : 24 + c[0], :], c, z) > 0.5
            bits = bits | jnp.where(blocked, 1 << i, 0)
        bits_ref[g] = bits
    steps = pop_ref.shape[0]
    for n in range(steps):
        for g in range(2):
            total = jnp.zeros((edge, plane), f32)
            flow = [jnp.zeros((edge, plane), f32) for _ in range(3)]
            for i in range(pops):
                f = pop_ref[n, g, i].astype(f32)
                total = total + f
                for a in range(3):
                    if velocities[i][a] == 1:
                        flow[a] = flow[a] + f
                    elif velocities[i][a] == -1:
                        flow[a] = flow[a] - f
            for a in range(3):
                u_ref[n, g, a] = flow[a] / total
    for is_odd, (g, x) in enumerate(late_layer):

        @pl.when(t.odd == is_odd)
        def _(is_odd=is_odd, g=g, x=x):
            link = jnp.where(t.prev if is_odd else t.next, 1.0, 0.0)
            rows = [u_ref[n, g, a, x : x + 1, :] for n in range(steps) for a in range(3)]
            rows += [keep_ref[g, x : x + 1, :] * link, gain_ref[g, x : x + 1, :] * link]
            rows += [w_ref[g, x : x + 1, :], k_ref[g, x : x + 1, :]]
            for n, row in enumerate(rows):
                late_ref[n : n + 1, :] = row


def collide(pulled, u, keep, gain):
    g = pulled
    plus = {i: g[i] + g[i + 1] for i in range(1, pops, 2)}
    minus = {i: g[i] - g[i + 1] for i in range(1, pops, 2)}
    xy, xz, yz = plus[7] + plus[9], plus[11] + plus[13], plus[15] + plus[17]
    px, py, pz = 2.0 * plus[1], 2.0 * plus[3], 2.0 * plus[5]
    weight = 12.0 * g[0] + (px + py + pz) + (xy + xz + yz)
    qxx, qyy, qzz = px + xy + xz, py + xy + yz, pz + xz + yz
    qxy, qxz, qyz = plus[7] - plus[9], plus[11] - plus[13], plus[15] - plus[17]
    jx = 2.0 * minus[1] + (minus[7] + minus[9]) + (minus[11] + minus[13])
    jy = 2.0 * minus[3] + (minus[7] - minus[9]) + (minus[15] + minus[17])
    jz = 2.0 * minus[5] + (minus[11] - minus[13]) + (minus[15] - minus[17])
    ux, uy, uz = u
    qux = qxx * ux + qxy * uy + qxz * uz
    quy = qxy * ux + qyy * uy + qyz * uz
    quz = qxz * ux + qyz * uy + qzz * uz
    speed = ux * ux + uy * uy + uz * uz
    along = ux * qux + uy * quy + uz * quz
    scale = gain * (1.0 / 36.0)
    rest = scale * (weight * (1.0 + 1.5 * speed) - 4.5 * along)
    scale = gain * (1.0 / 12.0)
    mx = scale * (jx + 3.0 * qux - ux * weight)
    my = scale * (jy + 3.0 * quy - uy * weight)
    mz = scale * (jz + 3.0 * quz - uz * weight)
    out = [None] * pops
    out[0] = keep * g[0] + rest
    pairs = [mx, my, mz, mx + my, mx - my, mx + mz, mx - mz, my + mz, my - mz]
    for n, i in enumerate(range(1, pops, 2)):
        out[i] = keep * g[i] + (rest + pairs[n])
        out[i + 1] = keep * g[i + 1] + (rest - pairs[n])
    return out


def add_item(t, j, item, half_scr, add):
    level, g, octant = t.level, t.block[j], t.octant[j]
    left = iota((40, 128), 1) < 64
    a, b = item[:, 0:128], item[:, 128:256]
    parts = [(a, left), (a, ~left), (b, left), (b, ~left)]
    stacked = jnp.concatenate([jnp.where(m, v, 0.0) for v, m in parts], axis=0)
    high = stacked.astype(bf16).astype(f32)
    halves = jnp.concatenate([high, stacked - high], axis=1).astype(bf16)
    target = cell_key(iota((1, plane), 1), level, octant)
    matrix = ones_where((iota((plane, plane), 0) & 63) == target)
    spread = jnp.dot(halves, matrix, preferred_element_type=f32)

    @pl.when(level == 0)
    def _():
        first = pl.multiple_of((octant >> 2) * 8, 8)
        add(g, first, 8, slice(0, plane), spread[0:152].reshape(pops, 8, plane))

    @pl.when(level == 1)
    def _():
        for n in range(2):
            lanes = slice(128 * n, 128 * n + 128)
            half = spread[:, lanes] * 0.125
            half_scr[n, pl.ds(0, 160, stride=2), :] = half
            half_scr[n, pl.ds(1, 160, stride=2), :] = half
            both = half_scr[n, 0:304, :].reshape(pops, edge, 128)
            add(g, 0, edge, lanes, both)


def before_kernel(*refs, first):
    (d_ref, alpha_ref, k_ref, mate_ref, rest_ref) = refs[:5]
    refs = refs[5:]
    if not first:
        (added_ref, fix_ref), refs = refs[:2], refs[2:]
    out_ref, half_scr = refs
    t = Table(d_ref[...])
    for g in range(2):
        block = slice(g * pops, (g + 1) * pops)
        out_ref[block] = alpha_ref[block] * k_ref[g][None]
    if not first:
        for is_odd, (g, x) in enumerate(late_layer):

            @pl.when(t.odd == is_odd)
            def _(g=g, x=x):
                kept = k_ref[g, x : x + 1, :]
                for i in range(pops):
                    out_ref[g * pops + i, x : x + 1, :] += added_ref[i : i + 1, :] * kept

    def add(g, start, layers, lanes, values):
        out_ref[pl.ds(g * pops, pops), pl.ds(start, layers), lanes] += values

    @pl.when(t.valid[0])
    def _():
        item = mate_ref[...] if first else mate_ref[...] + fix_ref[...]
        add_item(t, 0, item, half_scr, add)

    @pl.when(t.valid[2])
    def _():
        add_item(t, 2, rest_ref[0:40, :], half_scr, add)


def step_kernel(*refs, last):
    (d_ref, before_ref, k_ref, u_ref, keep_ref, gain_ref, bits_ref, lvl_ref, far_ref) = refs[:9]
    refs = refs[9:]
    if not last:
        (w_ref, place_ref), refs = refs[:2], refs[2:]
        out_ref, side_ref, beta_scr, rim_scr, half_scr = refs
    else:
        out_ref, beta_scr, half_scr = refs
    t = Table(d_ref[...])
    level, odd = t.level, t.odd
    for g in range(2):
        beta_scr[g, :, 8:24, :] = before_ref[g * pops : (g + 1) * pops]

    def add(g, start, layers, lanes, values):
        beta_scr[g, :, pl.ds(8 + start, layers), lanes] += values

    @pl.when(t.valid[1])
    def _():
        add_item(t, 1, far_ref[0:40, :], half_scr, add)

    from_d = lvl_ref[rest_mate_f : rest_mate_f + 8, :]
    from_f = far_ref[40:48, :] + lvl_ref[rest_far_d : rest_far_d + 8, :]
    above = jnp.where(odd == 1, from_f, from_d)
    below = jnp.where(odd == 1, from_d, from_f)
    above = jnp.where(t.next, above, 0.0)
    below = jnp.where(t.prev, below, 0.0)
    inner = t.inner
    for i in range(5):
        e, w = east_pops[i], west_pops[i]
        beta_scr[1, e, 24:25, :] = above[i : i + 1]
        beta_scr[0, w, 7:8, :] = below[i : i + 1]
        beta_scr[0, e, 24:25, :] = jnp.where(inner, beta_scr[1, e, 8:9, :], 0.0)
        beta_scr[1, w, 7:8, :] = jnp.where(inner, beta_scr[0, w, 23:24, :], 0.0)
    z = iota((8, plane), 1) & 15
    for g in range(2):
        for h in range(2):
            rows = slice(8 * h, 8 * h + 8)
            first = 8 + 8 * h
            bits = bits_ref[g, rows, :]
            pulled = []
            for i in range(pops):
                c = velocities[i]
                v = beta_scr[g, i, first + c[0] : first + c[0] + 8, :]
                v = moved_cells(v, c, z)
                back = beta_scr[g, opposite[i], first : first + 8, :]
                pulled.append(jnp.where((bits & (1 << i)) != 0, back, v))
            u = [u_ref[g, a, rows, :] for a in range(3)]
            done = collide(pulled, u, keep_ref[g, rows, :], gain_ref[g, rows, :])
            for i in range(pops):
                out_ref[g * pops + i, rows, :] = done[i]
    if not last:
        side_plane(t, out_ref, w_ref, place_ref[0], side_ref, rim_scr)


def side_plane(t, alpha_ref, w_ref, place, side_ref, rim_scr):
    clear(side_ref, rim_scr)
    level, odd = t.level, t.odd
    g, other, ox = t.block[0], t.other[0], t.octant[0] >> 2
    x = jnp.where(other == 1, 7, 0)

    def rows(layer):
        weight = w_ref[g, pl.ds(layer, 1), :]
        for i in range(5):
            pop = jnp.where(other == 1, west_pops[i], east_pops[i])
            rim_scr[i : i + 1, :] += alpha_ref[g * pops + pop, pl.ds(layer, 1), :] * weight

    @pl.when(t.valid[0] & (other != odd) & ((level == 0) | (ox == other)))
    def _():
        @pl.when(level == 0)
        def _():
            rows(ox * 8 + x)

        @pl.when(level == 1)
        def _():
            rows(2 * x)
            rows(2 * x + 1)

        side_ref[...] = select(rim_scr[...], place) * plane_scale(t)


def pack_kernel(*refs):
    d_ref, alpha_ref, w_ref, k_ref, pick_ref, place_ref, item_ref, lvl_ref, ends_ref = refs[:9]
    matrices = lambda j: (pick_ref[j], place_ref[j])
    t = Table(d_ref[...])
    pack(t, alpha_ref, w_ref, k_ref, item_ref, None, lvl_ref, ends_ref, refs[9:], matrices)


late_layer = ((1, edge - 1), (0, 0))


def late_values(is_odd, late_ref, u_ref, keep_ref, gain_ref):
    g, x = late_layer[is_odd]
    z = iota((8, plane), 1) & 15
    late = late_ref[...]
    pulled = [0.0] * pops
    for n, i in enumerate((east_pops, west_pops)[is_odd]):
        pulled[i] = moved_cells(late, velocities[i], z)[n : n + 1]
    rows = slice(x, x + 1)
    u = [u_ref[g, a, rows, :] for a in range(3)]
    return collide(pulled, u, keep_ref[g, rows, :], gain_ref[g, rows, :])


def late_share(late, fields, step, odd):
    z = iota((8, plane), 1) & 15
    pulled = [0.0] * pops
    for n in range(5):
        e, w = east_pops[n], west_pops[n]
        pulled[e] = jnp.where(odd == 0, moved_cells(late, velocities[e], z)[n : n + 1], 0.0)
        pulled[w] = jnp.where(odd == 0, 0.0, moved_cells(late, velocities[w], z)[n : n + 1])
    u = [fields[3 * step + a : 3 * step + a + 1] for a in range(3)]
    return collide(pulled, u, fields[12:13], fields[13:14])


def leaving(values, odd, scr):
    for n in range(5):
        e, w = east_pops[n], west_pops[n]
        scr[n : n + 1, :] = jnp.where(odd == 0, values[w], values[e])
    return scr[...]


def item_share(weighted, pick, odd, ref, base):
    picked = select(weighted, pick)
    left = iota((1, 128), 1) < 64
    at_row = iota((8, plane), 0) == jnp.where(odd == 0, 7, 0)
    for n in range(5):
        a, b, c, d = (picked[m : m + 1] for m in (n, 5 + n, 10 + n, 15 + n))
        row = jnp.concatenate([jnp.where(left, a, b), jnp.where(left, c, d)], axis=1)
        tile = slice(base + 8 * n, base + 8 * n + 8)
        ref[tile, :] += jnp.where(at_row, row, 0.0)


def clear(*refs):
    for ref in refs:
        ref[...] = jnp.zeros_like(ref)


def far_shares_kernel(*refs, step):
    (got_ref, planes_ref, pair_ref, mate_ref, pick_ref, place_ref) = refs[:6]
    out_ref, all_scr, rim_scr = refs[6:]
    odd = lax.axis_index("slab") & 1
    clear(out_ref, all_scr, rim_scr)
    fields = pair_ref[...]
    values = late_share(got_ref[5:13, :], fields, step, odd)
    for i in range(pops):
        all_scr[i : i + 1, :] = values[i]
    item_share(all_scr[...] * fields[14:15], pick_ref[0], odd, out_ref, 0)
    fields = mate_ref[...]
    values = late_share(planes_ref[0:8, :], fields, step, 1 - odd)
    share = select(leaving(values, 1 - odd, rim_scr) * fields[14:15], place_ref[2])
    out_ref[40:45, :] = got_ref[10:15, :] + share[0:5]


def shares_kernel(*refs, step):
    (got_ref, planes_ref, lvl_ref, ends_ref, own_ref, pair_ref, mate_ref) = refs[:7]
    (pick_ref, place_ref) = refs[7:9]
    rest_ref, kept_ref, added_ref, fix_ref, all_scr, rim_scr = refs[9:]
    odd = lax.axis_index("slab") & 1
    clear(all_scr, rim_scr, added_ref, fix_ref)
    rest_ref[...] = lvl_ref[rest_at:level_rows, :]
    kept_ref[...] = ends_ref[kept_own_d:kept_rows, :]
    fields = pair_ref[...]
    values = late_share(got_ref[5:13, :], fields, step, odd)
    for i in range(pops):
        all_scr[i : i + 1, :] = values[i]
    item_share(all_scr[...] * fields[14:15], pick_ref[1], odd, rest_ref, 0)
    rim = leaving(values, odd, rim_scr)
    rest_ref[rest_loc_d : rest_loc_d + 8, :] += rim * fields[15:16]
    rim = rim * fields[14:15]
    rest_ref[rest_far_d : rest_far_d + 8, :] += select(rim, place_ref[0])
    rest_ref[rest_own_d : rest_own_d + 8, :] += select(rim, place_ref[1])
    fields = own_ref[...]
    values = late_share(got_ref[0:8, :], fields, step, odd)
    for i in range(pops):
        added_ref[i : i + 1, :] = values[i]
    rim = leaving(values, odd, rim_scr)
    kept_ref[8:16, :] += rim * fields[15:16]
    kept_ref[0:8, :] += select(rim * fields[14:15], place_ref[3])
    fields = mate_ref[...]
    values = late_share(planes_ref[0:8, :], fields, step, 1 - odd)
    for i in range(pops):
        all_scr[i : i + 1, :] = values[i]
    item_share(all_scr[...] * fields[14:15], pick_ref[2], 1 - odd, fix_ref, 0)


def last_kernel(d_ref, alpha_ref, late_ref, u_ref, keep_ref, gain_ref, out_ref, tile_scr, sems):
    def tile(source, g, x, sem):
        block, rows = pl.ds(g * pops, pops), pl.ds(x, 8)
        source = source.at[block, rows] if source is alpha_ref else source
        return pltpu.make_async_copy(source, out_ref.at[block, rows], sems.at[sem])

    copies = [tile(alpha_ref, 0, 8, 0), tile(alpha_ref, 1, 0, 1)]
    for copy in copies:
        copy.start()
    t = Table(d_ref[...])
    odd = t.odd
    copies.append(tile(alpha_ref, odd, pl.multiple_of(8 * odd, 8), 2))
    copies[2].start()
    reached = pl.multiple_of(8 - 8 * odd, 8)
    tile_scr[...] = alpha_ref[pl.ds((1 - odd) * pops, pops), pl.ds(reached, 8), :]

    def side(is_odd):
        values = late_values(is_odd, late_ref, u_ref, keep_ref, gain_ref)
        x = late_layer[is_odd][1] % 8
        for i in range(pops):
            tile_scr[i, x : x + 1, :] += values[i]

    @pl.when((odd == 0) & t.next)
    def _():
        side(0)

    @pl.when((odd == 1) & t.prev)
    def _():
        side(1)

    copies.append(tile(tile_scr, 1 - odd, reached, 3))
    copies[3].start()
    for copy in copies:
        copy.wait()


def vmem():
    return pl.BlockSpec(memory_space=pltpu.VMEM)


def shape(*dims, dtype=f32):
    return jax.ShapeDtypeStruct(dims, dtype)


params = pltpu.CompilerParams(vmem_limit_bytes=24 * 1024 * 1024)
half_scratch = [pltpu.VMEM((2, 320, 128), f32)]
pack_scratch = [pltpu.VMEM((160, plane), f32), pltpu.VMEM((8, plane), f32)] + half_scratch
messages = [shape(rows, plane) for rows in (40, 8, level_rows, kept_rows)]
share_scratch = [pltpu.VMEM((24, plane), f32), pltpu.VMEM((8, plane), f32)]
field = shape(2, edge, plane)
state = shape(2 * pops, edge, plane)
blend_at = 2 * pops
tables_at = blend_at + 2


def hbm():
    return pl.BlockSpec(memory_space=pltpu.HBM)


def cost(flops, bytes_accessed):
    return pl.CostEstimate(flops=flops, bytes_accessed=bytes_accessed, transcendentals=0)


def call(kernel, outs, ins, scratch, name, out_specs=None, estimate=None):
    with jax.named_scope(name):
        return pl.pallas_call(
            kernel,
            out_shape=outs,
            in_specs=[vmem()] * len(ins),
            out_specs=out_specs or [vmem()] * len(outs),
            scratch_shapes=scratch,
            compiler_params=params,
            cost_estimate=estimate,
        )(*ins)


def far_message(lvl, ends, side, share=0.0):
    end = lvl[own_f : own_f + 5] + ends[kept_loc_f : kept_loc_f + 5] + side
    parts = [lvl[0:40] + share, end, lvl[far_f : far_f + 5], ends[kept_far_f : kept_far_f + 5]]
    return jnp.pad(jnp.concatenate(parts, axis=0), ((0, 1), (0, 0)))


def local(
    adjoint_final, populations, relaxation, blend, solid, chain, parent, children, *, slabs
):
    steps = populations.shape[0]
    tables = jnp.concatenate([children, parent, chain[0]], axis=1).astype(f32)
    tables = jnp.pad(tables, ((0, edge - 2), (0, plane - 12)), constant_values=-1.0)
    alpha = jnp.concatenate(
        [adjoint_final.reshape(2 * pops, edge, plane), blend[0], tables[None]], axis=0
    )
    table, *sent, kept = call(
        first_pack_kernel,
        [shape(8, 128, dtype=jnp.int32)] + messages + [field],
        (alpha,),
        pack_scratch,
        "pack_first",
    )
    weights = alpha[blend_at:tables_at]
    with jax.named_scope("exchange"):
        item, side, lvl, ends = sent
        lvl = level_swap(lvl, slabs)
        side = mate_swap(side, slabs, 1)
        message = far_message(lvl, ends, side[0:5])
        rest, kept_d = lvl[rest_at:], ends[kept_own_d:]
    flows, keep, gain, bits, pick, place, own_late, fix_pick, fix_place = call(
        fields_kernel,
        [
            shape(steps, 2, 3, edge, plane),
            field,
            field,
            shape(2, edge, plane, dtype=jnp.int32),
            shape(3, plane, 128, dtype=bf16),
            shape(3, plane, plane, dtype=bf16),
            shape(16, plane),
            shape(3, plane, 128, dtype=bf16),
            shape(4, plane, plane, dtype=bf16),
        ],
        (table, populations[:, 0], relaxation[0], solid[0], weights, kept),
        [pltpu.VMEM((32, plane), f32)],
        "flow_fields",
        estimate=cost(4_000_000, 2_000_000),
    )
    shares = []
    for t in range(steps - 1, -1, -1):
        first, last = t == steps - 1, t == 0
        u = flows[t]
        with jax.named_scope("exchange"):
            far = far_swap(message, slabs)
            mate = mate_swap(item, slabs, 1)
            pair_end = rest[rest_loc_d : rest_loc_d + 5] + kept_d[0:5] + far[50:55]
            own_end = kept_d[8:13] + rest[rest_own_d : rest_own_d + 5] + far[45:50]
            if last:
                late = mate_swap(jnp.pad(pair_end, ((0, 3), (0, 0))), slabs, 1)
        before = call(
            functools.partial(before_kernel, first=first),
            [state],
            (table, alpha, kept, mate, rest, *shares),
            half_scratch,
            "before",
            estimate=cost(40_000_000_000, 2_000_000),
        )[0]
        ins = [table, before, kept, u, keep, gain, bits, rest, far]
        if not last:
            ins += [weights, place]
        got = call(
            functools.partial(step_kernel, last=last),
            [state] + ([] if last else [shape(8, plane)]),
            ins,
            [pltpu.VMEM((2, pops, 32, plane), f32)]
            + ([] if last else [pltpu.VMEM((8, plane), f32)])
            + half_scratch,
            "step",
            estimate=cost(8_000_000, 2_000_000),
        )
        alpha = got[0]
        if last:
            alpha = call(
                last_kernel,
                [state],
                (table, alpha, late, u, keep, gain),
                [pltpu.VMEM((pops, 8, plane), f32), pltpu.SemaphoreType.DMA((4,))],
                "finish",
                out_specs=[hbm()],
            )[0]
            continue
        with jax.named_scope("exchange"):
            planes = jnp.concatenate([pair_end, own_end, got[1][0:5]], axis=0)
            planes = jnp.pad(planes, ((0, 1), (0, 0)))
            if first:
                planes = jnp.concatenate([planes, own_late], axis=0)
            late = mate_swap(planes, slabs, 1)
        item, lvl, ends = call(
            pack_kernel,
            [messages[0], messages[2], messages[3]],
            (table, alpha, weights, kept, pick, place),
            pack_scratch,
            "pack",
            estimate=cost(8_000_000, 2_000_000),
        )
        with jax.named_scope("exchange"):
            lvl = level_swap(lvl, slabs)
            if first:
                pair_late, mate_late = level_swap(own_late, slabs), late[16:32]
        more = call(
            functools.partial(far_shares_kernel, step=t),
            [shape(48, plane)],
            (late, planes, pair_late, mate_late, fix_pick, fix_place),
            share_scratch,
            "far_shares",
            estimate=cost(40_000_000_000, 4_000_000),
        )[0]
        message = far_message(lvl, ends, more[40:45], more[0:40])
        rest, kept_d, *shares = call(
            functools.partial(shares_kernel, step=t),
            [shape(rest_rows, plane), shape(16, plane), shape(24, plane), shape(40, plane)],
            (late, planes, lvl, ends, own_late, pair_late, mate_late, fix_pick, fix_place),
            share_scratch,
            "shares",
            estimate=cost(40_000_000_000, 2_000_000),
        )
    return alpha.reshape(1, 2, pops, edge, plane)


def solution(mesh):
    return jax.shard_map(
        functools.partial(local, slabs=mesh.shape["slab"]),
        mesh=mesh,
        in_specs=(
            P("lvl", "slab", None, None, None),
            P(None, "lvl", "slab", None, None, None),
            P("lvl", "slab", None, None),
            P("lvl", "slab", None, None),
            P("lvl", "slab", None, None),
            P("lvl", "slab", None),
            P("slab", None),
            P("slab", None),
        ),
        out_specs=P("lvl", "slab", None, None, None),
        check_vma=False,
    )
```
